512 devices in a mesh: leaf: 128 (over y, z, core), vec: 4 (over x).
Axes of the slice: x: 4, y: 8, z: 8, core: 2. Of those that a mesh axis runs over, the one named last changes fastest.
Arguments:
- vectors: bfloat16 [64, 131072], P('vec', 'leaf'), may hold values from -6 to 6
- leaf_basis: bfloat16 [64, 131072], P(None, 'leaf'), may hold values from -0.75 to 0.75
- local_transfer: bfloat16 [64, 245760], P(None, 'leaf'), may hold values from -0.625 to 0.625
- upper_transfer: bfloat16 [64, 15872], replicated, may hold values from -0.625 to 0.625
- upper_coupling: bfloat16 [64, 256], replicated, may hold values from -0.75 to 0.75
- leaf_coupling: bfloat16 [64, 786432], P(None, 'leaf'), may hold values from -0.3125 to 0.3125
- far_list: int32 [6, 2048], P(None, 'leaf'), may hold values from 0 to 2047, as said below
- near_list: int32 [6, 2048], P(None, 'leaf'), may hold values from 0 to 2047, as said below
- near_tiles: bfloat16 [2048, 64, 384], P(('leaf', 'vec')), may hold values from -0.3125 to 0.3125
Outputs:
- product: bfloat16 [64, 131072], P('vec', 'leaf')
The draws below stay inside these ranges and needn't reach their ends.
Inputs may be any that keep to these rules, and one draw needn't show every extreme that they name: `far_list`: every entry names a leaf 2 to 16 leaves away from its own leaf l (column l); on every device some leaf has an entry exactly 16 leaves away. `near_list`: row 0 names the leaf itself; every other entry names a leaf 1 to 16 leaves away from its own leaf; on every device some leaf has an entry exactly 16 leaves away.
All inputs are finite; a program needn't handle non-finite values.
Results may differ from the reference program's by a relative error of at most 0.0055.
Values may be sent and summed in bfloat16 or wider, within the bound.
A program may use at most 64 MiB of HBM per device.

```python
import jax
import jax.numpy as jnp
from jax import lax

VECS = 64
LEAF = 64
RANK = 64
LEAF_DEV = 16
K_FAR = 6
K_NEAR = 6
LEAVES = 2048
POINTS = 131072
N_LEAF = 128


def reach_table(key, number, least):
    magnitudes = jnp.arange(least, LEAF_DEV + 1, dtype=jnp.int32)
    candidates = jnp.concatenate([-magnitudes, magnitudes])
    keys = jax.random.split(key, LEAVES)
    orders = jax.vmap(lambda one_key: jax.random.permutation(one_key, candidates.shape[0]))(keys)
    offsets = candidates[orders[:, :number]]
    leaf_ids = jnp.arange(LEAVES, dtype=jnp.int32)[:, None]
    slot_ids = jnp.arange(number, dtype=jnp.int32)[None, :]
    edge_rows = leaf_ids % LEAF_DEV == LEAF_DEV - 1
    offsets = jnp.where(edge_rows & (slot_ids == 0), LEAF_DEV, offsets)
    source_points = leaf_ids + offsets
    source_points = jnp.where((source_points < 0) | (source_points >= LEAVES), leaf_ids - offsets, source_points)
    return source_points.T.astype(jnp.int32)


def draw_far_list(key, part):
    key = jax.random.fold_in(key, 11)
    return reach_table(key, K_FAR, 2)


def draw_near_list(key, part):
    key = jax.random.fold_in(key, 23)
    others = reach_table(key, K_NEAR - 1, 1)
    selves = jnp.arange(LEAVES, dtype=jnp.int32)[None, :]
    return jnp.concatenate([selves, others], axis=0).astype(jnp.int32)


def shard_levels(own_key, extent, pieces, low, top_value):
    def one(position, shards_of):
        draws = jax.random.uniform(jax.random.fold_in(jax.random.fold_in(own_key, 6), position), (shards_of,), jnp.float32, low / len(pieces), top_value / len(pieces))
        return jnp.repeat(jnp.exp(draws), extent[position] // shards_of).reshape((-1,) + (1,) * (len(extent) - position - 1))

    level = one(*pieces[0])
    for cut in pieces[1:]:
        level = level * one(*cut)
    return level


def bell_draw(key, extent, deviation, bound, pieces=(), kind=jnp.bfloat16):
    entries = jax.random.normal(key, extent, jnp.float32) * deviation
    if len(pieces) > 0:
        entries = shard_levels(key, extent, pieces, -0.22, 0.18) * entries
    return jnp.clip(entries, min=-bound, max=bound).astype(kind)


def setup_inputs(seed: int = 0) -> dict:
    seeds = jax.random.split(jax.random.key(seed), 10)
    return {
        "vectors": bell_draw(seeds[0], (VECS, POINTS), 1.0, 6.0, ((0, 4), (1, 128))),
        "leaf_basis": bell_draw(seeds[1], (RANK, POINTS), LEAF ** -0.5, 0.75, ((1, 128),)),
        "local_transfer": bell_draw(seeds[2], (RANK, N_LEAF * (2 * LEAF_DEV - 2) * RANK), (3 * RANK // 2) ** -0.5, 0.625, ((1, 128),)),
        "upper_transfer": bell_draw(seeds[3], (RANK, (2 * N_LEAF - 8) * RANK), (3 * RANK // 2) ** -0.5, 0.625),
        "upper_coupling": bell_draw(seeds[4], (RANK, 4 * RANK), RANK ** -0.5, 0.75),
        "leaf_coupling": bell_draw(seeds[5], (RANK, LEAVES * K_FAR * RANK), (K_FAR * RANK) ** -0.5, 0.3125, ((1, 128),)),
        "far_list": draw_far_list(jax.random.fold_in(seeds[9], 71), 0),
        "near_list": draw_near_list(jax.random.fold_in(seeds[9], 71), 0),
        "near_tiles": bell_draw(seeds[8], (LEAVES, LEAF, K_NEAR * LEAF), (K_NEAR * LEAF) ** -0.5, 0.3125, ((0, 512),)),
    }


exact_arithmetic = lax.Precision.HIGHEST


def couple_nodes(values, coupling):
    columns, number, rank_size = values.shape
    padded = jnp.pad(values, ((0, 0), (3, 3), (0, 0)))
    parity = (jnp.arange(number) % 2).astype(jnp.float32)[None, :, None]
    before_three = padded[:, 0:number] * parity
    before_two = padded[:, 1:1 + number]
    after_two = padded[:, 5:5 + number]
    after_three = padded[:, 6:6 + number] * (1.0 - parity)
    summed = jnp.zeros_like(values)
    for slot_index, shifted in enumerate((before_three, before_two, after_two, after_three)):
        summed = summed + jnp.einsum("vns,ts->vnt", shifted, coupling[:, slot_index, :], precision=exact_arithmetic)
    return summed


def upper_tree(root_values, upper_transfer, upper_coupling, heights):
    columns, number, rank_size = root_values.shape
    coupling = upper_coupling.astype(jnp.float32).reshape(rank_size, 4, rank_size)
    values = [root_values]
    current = root_values
    transfers = []
    for tree_height in range(heights):
        node_count = number >> tree_height
        offset = 2 * number - 2 * node_count
        transfer = upper_transfer[:, offset * rank_size:(offset + node_count) * rank_size]
        transfer = transfer.reshape(rank_size, node_count, rank_size).astype(jnp.float32)
        transfers.append(transfer)
        lifted = jnp.einsum("vnk,knj->vnj", current, transfer, precision=exact_arithmetic)
        current = lifted.reshape(columns, node_count // 2, 2, rank_size).sum(axis=2)
        values.append(current)
    downward_sweep = couple_nodes(values[heights], coupling)
    for tree_height in reversed(range(heights)):
        spread = jnp.repeat(downward_sweep, 2, axis=1)
        downward_sweep = couple_nodes(values[tree_height], coupling) + jnp.einsum(
            "vnj,knj->vnk", spread, transfers[tree_height], precision=exact_arithmetic)
    return downward_sweep


def reference(vectors, leaf_basis, local_transfer, upper_transfer, upper_coupling, leaf_coupling, far_list, near_list, near_tiles):
    point_rows = vectors.reshape(VECS, LEAVES, LEAF).astype(jnp.float32)
    leaf_bases = leaf_basis.reshape(RANK, LEAVES, LEAF).astype(jnp.float32)
    leaf_coeff = jnp.einsum("vlp,rlp->vlr", point_rows, leaf_bases, precision=exact_arithmetic)
    local_all = local_transfer.reshape(RANK, N_LEAF, 2 * LEAF_DEV - 2, RANK).astype(jnp.float32)
    depth_local = LEAF_DEV.bit_length() - 1
    current = leaf_coeff
    transfers = []
    for tree_height in range(depth_local):
        node_count = LEAF_DEV >> tree_height
        offset = 2 * LEAF_DEV - 2 * node_count
        transfer = local_all[:, :, offset:offset + node_count, :].reshape(RANK, N_LEAF * node_count, RANK)
        transfers.append(transfer)
        lifted = jnp.einsum("vnk,knj->vnj", current, transfer, precision=exact_arithmetic)
        current = lifted.reshape(VECS, N_LEAF * node_count // 2, 2, RANK).sum(axis=2)
    heights = N_LEAF.bit_length() - 3
    downward_sweep = upper_tree(current, upper_transfer, upper_coupling, heights)
    for tree_height in reversed(range(depth_local)):
        spread = jnp.repeat(downward_sweep, 2, axis=1)
        downward_sweep = jnp.einsum("vnj,knj->vnk", spread, transfers[tree_height], precision=exact_arithmetic)
    leaf_rounded = leaf_coeff.astype(jnp.bfloat16)
    coupling = leaf_coupling.reshape(RANK, LEAVES, K_FAR, RANK)
    for slot_index in range(K_FAR):
        source_point = leaf_rounded[:, far_list[slot_index]].astype(jnp.float32)
        block_collection = coupling[:, :, slot_index, :].astype(jnp.float32)
        downward_sweep = downward_sweep + jnp.einsum("rqw,yqw->rqy", source_point, block_collection, precision=exact_arithmetic)
    leaf_down = lax.optimization_barrier(downward_sweep.astype(jnp.bfloat16)).astype(jnp.float32)
    far_part = jnp.einsum("vlr,rlp->vlp", leaf_down, leaf_bases, precision=exact_arithmetic)
    tile_blocks = near_tiles.reshape(LEAVES, LEAF, K_NEAR, LEAF)
    near_part = jnp.zeros((VECS, LEAVES, LEAF), jnp.float32)
    for slot_index in range(K_NEAR):
        source_point = point_rows[:, near_list[slot_index]]
        block_collection = tile_blocks[:, :, slot_index, :].astype(jnp.float32)
        near_part = near_part + jnp.einsum("vlq,lpq->vlp", source_point, block_collection, precision=exact_arithmetic)
    return (far_part + near_part).reshape(VECS, POINTS).astype(jnp.bfloat16)
```

```python
import jax
import jax.numpy as jnp
from jax import lax
from jax.experimental import pallas as pl
from jax.experimental.pallas import tpu as pltpu
from jax.sharding import PartitionSpec as P

MESH = pl.DeviceIdType.MESH
BF = jnp.bfloat16
F32 = jnp.float32
ROW = 16
ROWS = 8
LEAF_COUNT = ROW * ROWS
BASES = (0, 16, 24, 28, 30)
FAR_ORDER = (8, 9, 7, 10, 6, 11, 5, 12, 4, 13, 3, 14, 2, 15, 1)


def low(shape):
    return lax.broadcasted_iota(jnp.int32, shape, 1) < 64


def halves(a, b):
    return jnp.where(low(a.shape), a, b)


def turned(tile):
    return pltpu.roll(tile.astype(F32), 64, 1).astype(tile.dtype)


def rounded(x):
    return x.astype(BF).astype(F32)


def hilo(x):
    hi = rounded(x)
    return halves(hi, x - hi).astype(BF)


def two_terms(x):
    hi = rounded(x)
    return hi.astype(BF), (x - hi).astype(BF)


def nn(a, b):
    return jnp.dot(a, b, preferred_element_type=F32)


def nt(a, b):
    return lax.dot_general(a, b, (((1,), (1,)), ((), ())), preferred_element_type=F32)


def rows(*parts):
    return jnp.concatenate(parts, axis=0)


def lanes(*parts):
    return jnp.concatenate(parts, axis=1)


def kernel(
    vec_h, basis_h, lt_h, ut_h, uc_h, lc_h, far_h, near_h, tiles_h, out_ref,
    vec_v, basis_v, lt_v, ut_v, uc_v, lc_v, far_s, near_s, tiles_v,
    points, coeffs, ext0, ext1, ext2, ext3, ext4, ext5,
    dup, path_hi, path_lo, r0_hi, r0_lo, far_out, near_out, near_in,
    in_sem, send_sem, recv_sem,
):
    d = lax.axis_index("leaf")
    x = lax.axis_index("vec")
    y = d // ROW
    i = d % ROW
    exts = (ext0, ext1, ext2, ext3)

    def load(src, dst, n):
        copy = pltpu.make_async_copy(src, dst, in_sem.at[n])
        copy.start()
        return copy

    vec_in = load(vec_h, vec_v, 0)
    basis_in = load(basis_h, basis_v, 1)
    lt_in = load(lt_h, lt_v, 2)
    ut_in = [
        load(ut_h.at[:, pl.ds(pl.multiple_of(1024 * y, 128), 1024)], ut_v.at[:, 0:1024], 3),
        load(ut_h.at[:, pl.ds(pl.multiple_of(8192 + 512 * y, 128), 512)], ut_v.at[:, 1024:1536], 4),
        load(ut_h.at[:, pl.ds(pl.multiple_of(12288 + 256 * y, 128), 256)], ut_v.at[:, 1536:1792], 5),
        load(ut_h.at[:, pl.ds(pl.multiple_of(14336 + 128 * y, 128), 128)], ut_v.at[:, 1792:1920], 6),
        load(ut_h.at[:, 15360:15872], ut_v.at[:, 1920:2432], 7),
    ]
    uc_in = load(uc_h, uc_v, 8)
    lc_in = load(lc_h, lc_v, 9)
    far_in_s = load(far_h, far_s, 10)
    near_in_s = load(near_h, near_s, 11)
    tiles_in = load(tiles_h, tiles_v, 12)

    right = (d + 1) % LEAF_COUNT
    left = (d + LEAF_COUNT - 1) % LEAF_COUNT
    row_peers = [ROW * y + (i + k) % ROW for k in FAR_ORDER]
    column_peers = [(d + ROW * k) % LEAF_COUNT for k in (4, 3, 5, 2, 6, 1, 7)]
    vec_peers = [(x + k) % 4 for k in (2, 1, 3)]

    barrier = pltpu.get_barrier_semaphore()
    for peer in row_peers + column_peers + [right, left]:
        pl.semaphore_signal(barrier, inc=1, device_id={"leaf": peer, "vec": x}, device_id_type=MESH)
    for peer in vec_peers:
        pl.semaphore_signal(barrier, inc=1, device_id={"leaf": d, "vec": peer}, device_id_type=MESH)

    sent = []

    def send(src, dst, n_send, n_recv, leaf, vec):
        copy = pltpu.make_async_remote_copy(
            src_ref=src, dst_ref=dst, send_sem=send_sem.at[n_send], recv_sem=recv_sem.at[n_recv],
            device_id={"leaf": leaf, "vec": vec}, device_id_type=MESH,
        )
        copy.start()
        return copy

    def wait_for(ref, sem):
        pltpu.make_async_copy(ref, ref, sem).wait()

    own = pl.ds(pl.multiple_of(16 * x, 16), 16)
    vec_in.wait()
    for j in range(8):
        points[8 + j, 0, own, :] = vec_v[:, 128 * j : 128 * j + 128]
    pl.semaphore_wait(barrier, 27)
    for peer in vec_peers:
        send(points.at[8:16, 0, own], points.at[8:16, 0, own], 0, 0, d, peer)

    basis_in.wait()
    lt_in.wait()
    zero = jnp.zeros((16, 128), BF)
    current = []
    for j in range(8):
        tile = vec_v[:, 128 * j : 128 * j + 128]
        block = basis_v[:, 128 * j : 128 * j + 128]
        coeff = nt(rows(halves(tile, zero), halves(zero, tile)), rows(block, block))
        first, second = coeff[0:16], coeff[16:32]
        coeffs[8 + j, 0] = halves(first, second).astype(BF)
        coeffs[8 + j, 1] = halves(second, first).astype(BF)
        transfer = lt_v[:, 128 * j : 128 * j + 128]
        lifted = nn(hilo(coeff), rows(transfer, transfer))
        current.append(halves(lifted[0:16], lifted[16:32]))
    for start in (1024, 1536):
        following = []
        for m in range(len(current) // 2):
            hi, lo = two_terms(rows(current[2 * m], current[2 * m + 1]))
            transfer = lt_v[:, start + 128 * m : start + 128 * m + 128]
            lifted = nn(lanes(hi, lo), rows(transfer, transfer, transfer, transfer))
            following.append(halves(lifted[0:16], lifted[16:32]))
        current = following
    transfer = lt_v[:, 1792:1920]
    crossed = turned(transfer)
    top = (halves(transfer, crossed), halves(crossed, transfer))
    first_hi, first_lo = two_terms(current[0])
    second_hi, second_lo = two_terms(current[1])
    root = nn(lanes(first_hi, first_lo, second_hi, second_lo), rows(*([top[0]] * 4 + [top[1]] * 4)))
    ext0[2 + i] = hilo(root)
    for peer in row_peers:
        send(ext0.at[2 + i], ext0.at[2 + i], 1, 1, peer, x)

    send(coeffs.at[8:16, 0], coeffs.at[0:8, 0], 2, 2, right, x)
    send(coeffs.at[8:16, 0], coeffs.at[16:24, 0], 3, 3, left, x)
    wait_for(points.at[8:16, 0, 0:48], recv_sem.at[0])
    send(points.at[8:16, 0], points.at[0:8, 0], 4, 4, right, x)
    send(points.at[8:16, 0], points.at[16:24, 0], 5, 5, left, x)

    for copy in ut_in:
        copy.wait()
    for p in range(19):
        pair = ut_v[:, 128 * p : 128 * p + 128]
        swapped = turned(pair)
        dup[2 * p] = halves(pair, swapped)
        dup[2 * p + 1] = halves(swapped, pair)
    step = dup[i]
    path_hi[0] = step
    step = step.astype(F32)
    for u in range(1, 5):
        node = BASES[u] + (i // (1 << u) if u < 4 else y)
        matrix = dup[node]
        step = nn(hilo(step), rows(matrix, matrix))
        path_hi[u], path_lo[u] = two_terms(step)

    below_hi = [top[0], top[1]]
    below_lo = [None, None]
    for start, count in ((1536, 2), (1024, 4), (0, 8)):
        next_hi, next_lo = [], []
        for m in range(count):
            pair = lt_v[:, start + 128 * m : start + 128 * m + 128]
            none = jnp.zeros_like(pair)
            left_side = rows(halves(pair, none), halves(none, pair))
            hi, lo = below_hi[m], below_lo[m]
            if lo is None:
                product = nn(left_side, rows(hi, hi))
            else:
                product = nn(lanes(left_side, left_side), rows(hi, hi, lo, lo))
            hi, lo = two_terms(product)
            if start == 0:
                r0_hi[m] = hi
                r0_lo[m] = lo
            else:
                next_hi += [hi[0:64], hi[64:128]]
                next_lo += [lo[0:64], lo[64:128]]
        below_hi, below_lo = next_hi, next_lo

    wait_for(ext0.at[0:15], recv_sem.at[1])
    after = (d + ROW) % LEAF_COUNT
    before = (d + LEAF_COUNT - ROW) % LEAF_COUNT
    for u in range(4):
        ext, count = exts[u], ROW >> u
        send(ext.at[count : count + 2], ext.at[0:2], 6 + 2 * u, 6 + 2 * u, after, x)
        send(ext.at[2:4], ext.at[2 + count : 4 + count], 7 + 2 * u, 7 + 2 * u, before, x)
        for m in range(count // 2):
            left_m, right_m = dup[BASES[u] + 2 * m], dup[BASES[u] + 2 * m + 1]
            value = nn(lanes(ext[2 + 2 * m], ext[3 + 2 * m]), rows(left_m, left_m, right_m, right_m))
            if u < 3:
                exts[u + 1][2 + m] = hilo(value)
            else:
                ext4[y] = hilo(value)
    for peer in column_peers:
        send(ext4.at[y], ext4.at[y], 14, 14, peer, x)

    near_in_s.wait()
    tiles_in.wait()
    wait_for(points.at[0:8, 0], recv_sem.at[4])
    wait_for(points.at[16:24, 0], recv_sem.at[5])
    for p in range(24):
        points[p, 1] = turned(points[p, 0])
    first_leaf = ROW * d - ROW

    def chosen(table, lists, slots, column):
        parts = []
        for s in range(0, slots, 2):
            a = jnp.clip(lists[s, column] - first_leaf, 0, 3 * ROW - 1)
            b = jnp.clip(lists[s + 1, column] - first_leaf, 0, 3 * ROW - 1)
            parts.append(halves(table[a // 2, a % 2], table[b // 2, 1 - b % 2]))
        return lanes(*parts)

    for q in range(2):
        source = rows(*[chosen(points, near_s, 6, 4 * x + 2 * q + e) for e in range(2)])
        value = nt(source, rows(tiles_v[2 * q], tiles_v[2 * q + 1]))
        value = halves(value[0:64], value[64:128]).astype(BF)
        for v in range(4):
            near_out[v, q] = value[16 * v : 16 * v + 16]
    for n, peer in enumerate(vec_peers):
        send(near_out.at[peer], near_in.at[x], 15, 15, d, peer)
    near_in[x] = near_out[x]

    far_in_s.wait()
    lc_in.wait()
    wait_for(coeffs.at[0:8, 0], recv_sem.at[2])
    wait_for(coeffs.at[16:24, 0], recv_sem.at[3])
    for p in list(range(8)) + list(range(16, 24)):
        coeffs[p, 1] = turned(coeffs[p, 0])
    for j in range(8):
        source = rows(*[chosen(coeffs, far_s, 6, 2 * j + e) for e in range(2)])
        value = nt(source, rows(lc_v[:, 768 * j : 768 * j + 384], lc_v[:, 768 * j + 384 : 768 * j + 768]))
        far_out[j] = halves(value[0:16], value[16:32])

    uc_in.wait()
    weights = []
    for o in range(2):
        pair = uc_v[:, 128 * o : 128 * o + 128]
        swapped = turned(pair)
        weights += [halves(pair, swapped), halves(swapped, pair)]
    weights = lanes(*weights)
    for n in range(6, 14):
        ext, count = exts[(n - 6) // 2], ROW >> ((n - 6) // 2)
        wait_for(ext.at[0:2] if n % 2 == 0 else ext.at[2 + count : 4 + count], recv_sem.at[n])
    wait_for(ext4.at[0:7], recv_sem.at[14])
    for m in range(4):
        left_m, right_m = dup[30 + 2 * m], dup[31 + 2 * m]
        value = nn(lanes(ext4[2 * m], ext4[2 * m + 1]), rows(left_m, left_m, right_m, right_m))
        ext5[m] = hilo(value)
    sources = []
    for u in range(6):
        g = d // (1 << u)
        odd = g % 2
        number = LEAF_COUNT >> u
        parts = []
        for o, wanted in ((-3, odd == 1), (-2, None), (2, None), (3, odd == 0)):
            if u < 4:
                shift = o if wanted is None else (-3 * odd if o < 0 else 3 * (1 - odd))
                tile = exts[u][2 + i // (1 << u) + shift]
            else:
                tile = (ext4, ext5)[u - 4][(g + o + number) % number]
            valid = (g + o >= 0) if o < 0 else (g + o < number)
            if wanted is not None:
                valid = jnp.logical_and(valid, wanted)
            keep = jnp.where(valid, 1.0, 0.0).astype(F32)
            parts.append((tile.astype(F32) * keep).astype(BF))
        sources.append(lanes(*parts))
    coupled = nt(rows(*sources), rows(weights, weights))
    left_side, right_side = [], []
    for u in range(1, 6):
        tile = hilo(coupled[16 * u : 16 * u + 16])
        left_side.append(tile)
        right_side.append(path_hi[u - 1])
        if u > 1:
            left_side.append(tile)
            right_side.append(path_lo[u - 1])
    matrix = lanes(*right_side)
    down = coupled[0:16] + nt(lanes(*left_side), rows(matrix, matrix))
    down = hilo(down)
    down = lanes(down, down)

    wait_for(near_in.at[0:3], recv_sem.at[15])
    for j in range(8):
        local = nt(down, lanes(r0_hi[j], r0_lo[j]))
        leaf_down = (local + far_out[j]).astype(BF)
        block = basis_v[:, 128 * j : 128 * j + 128]
        none = jnp.zeros_like(block)
        value = nn(leaf_down, rows(halves(block, none), halves(none, block)))
        out_ref[:, 128 * j : 128 * j + 128] = (value + near_in[j // 2, j % 2].astype(F32)).astype(BF)

    wait_for(points.at[8:16, 0, 0:48], send_sem.at[0])
    wait_for(ext0.at[0:15], send_sem.at[1])
    wait_for(coeffs.at[0:8, 0], send_sem.at[2])
    wait_for(coeffs.at[0:8, 0], send_sem.at[3])
    wait_for(points.at[0:8, 0], send_sem.at[4])
    wait_for(points.at[0:8, 0], send_sem.at[5])
    for n in range(6, 14):
        wait_for(ext0.at[0:2], send_sem.at[n])
    wait_for(ext4.at[0:7], send_sem.at[14])
    wait_for(near_out.at[0:3], send_sem.at[15])


def shards(vectors, leaf_basis, local_transfer, upper_transfer, upper_coupling, leaf_coupling, far_list, near_list, near_tiles):
    tile = (16, 128)
    scratch = [
        pltpu.VMEM(vectors.shape, BF),
        pltpu.VMEM(leaf_basis.shape, BF),
        pltpu.VMEM(local_transfer.shape, BF),
        pltpu.VMEM((64, 2432), BF),
        pltpu.VMEM(upper_coupling.shape, BF),
        pltpu.VMEM(leaf_coupling.shape, BF),
        pltpu.SMEM(far_list.shape, jnp.int32),
        pltpu.SMEM(near_list.shape, jnp.int32),
        pltpu.VMEM(near_tiles.shape, BF),
        pltpu.VMEM((24, 2, 64, 128), BF),
        pltpu.VMEM((24, 2) + tile, BF),
        pltpu.VMEM((20,) + tile, BF),
        pltpu.VMEM((12,) + tile, BF),
        pltpu.VMEM((8,) + tile, BF),
        pltpu.VMEM((6,) + tile, BF),
        pltpu.VMEM((8,) + tile, BF),
        pltpu.VMEM((4,) + tile, BF),
        pltpu.VMEM((38, 64, 128), BF),
        pltpu.VMEM((5, 64, 128), BF),
        pltpu.VMEM((5, 64, 128), BF),
        pltpu.VMEM((8, 128, 128), BF),
        pltpu.VMEM((8, 128, 128), BF),
        pltpu.VMEM((8,) + tile, F32),
        pltpu.VMEM((4, 2) + tile, BF),
        pltpu.VMEM((4, 2) + tile, BF),
        pltpu.SemaphoreType.DMA((13,)),
        pltpu.SemaphoreType.DMA((16,)),
        pltpu.SemaphoreType.DMA((16,)),
    ]
    return pl.pallas_call(
        kernel,
        out_shape=jax.ShapeDtypeStruct(vectors.shape, BF),
        in_specs=[pl.BlockSpec(memory_space=pl.ANY)] * 9,
        out_specs=pl.BlockSpec(memory_space=pltpu.VMEM),
        scratch_shapes=scratch,
        compiler_params=pltpu.CompilerParams(
            collective_id=0, has_side_effects=True, vmem_limit_bytes=63 * 1024 * 1024
        ),
    )(vectors, leaf_basis, local_transfer, upper_transfer, upper_coupling, leaf_coupling, far_list, near_list, near_tiles)


def solution(mesh):
    placed = (
        P("vec", "leaf"),
        P(None, "leaf"),
        P(None, "leaf"),
        P(),
        P(),
        P(None, "leaf"),
        P(None, "leaf"),
        P(None, "leaf"),
        P(("leaf", "vec"), None, None),
    )
    return jax.shard_map(
        shards, mesh=mesh, in_specs=placed, out_specs=P("vec", "leaf"), check_vma=False
    )
```

```python
import jax
import jax.numpy as jnp
from jax import lax
from jax.experimental import pallas as pl
from jax.experimental.pallas import tpu as pltpu
from jax.sharding import PartitionSpec as P

MESH = pl.DeviceIdType.MESH
BF = jnp.bfloat16
F32 = jnp.float32
ROW = 16
ROWS = 8
LEAF_COUNT = ROW * ROWS
BASES = (0, 16, 24, 28, 30)
FAR_ORDER = (8, 9, 7, 10, 6, 11, 5, 12, 4, 13, 3, 14, 2, 15, 1)


def low(shape):
    return lax.broadcasted_iota(jnp.int32, shape, 1) < 64


def halves(a, b):
    return jnp.where(low(a.shape), a, b)


def turned(tile):
    return pltpu.roll(tile.astype(F32), 64, 1).astype(tile.dtype)


def rounded(x):
    return x.astype(BF).astype(F32)


def hilo(x):
    hi = rounded(x)
    return halves(hi, x - hi).astype(BF)


def two_terms(x):
    hi = rounded(x)
    return hi.astype(BF), (x - hi).astype(BF)


def nn(a, b):
    return jnp.dot(a, b, preferred_element_type=F32)


def nt(a, b):
    return lax.dot_general(a, b, (((1,), (1,)), ((), ())), preferred_element_type=F32)


def rows(*parts):
    return jnp.concatenate(parts, axis=0)


def lanes(*parts):
    return jnp.concatenate(parts, axis=1)


def kernel(
    vec_h, basis_h, lt_h, ut_h, uc_h, lc_h, far_h, near_h, tiles_h, out_ref,
    vec_v, basis_v, lt_v, ut_v, uc_v, lc_v, far_s, near_s, tiles_v,
    points, coeffs, ext0, ext1, ext2, ext3, ext4, ext5,
    dup, path_hi, path_lo, r0_hi, r0_lo, far_out, near_out, near_in,
    in_sem, send_sem, recv_sem,
):
    d = lax.axis_index("leaf")
    x = lax.axis_index("vec")
    y = d >> 4
    i = d & 15
    exts = (ext0, ext1, ext2, ext3)

    def load(src, dst, n):
        copy = pltpu.make_async_copy(src, dst, in_sem.at[n])
        copy.start()
        return copy

    vec_in = load(vec_h, vec_v, 0)
    basis_in = load(basis_h, basis_v, 1)
    lt_in = load(lt_h, lt_v, 2)
    ut_in = [
        load(ut_h.at[:, pl.ds(pl.multiple_of(1024 * y, 128), 1024)], ut_v.at[:, 0:1024], 3),
        load(ut_h.at[:, pl.ds(pl.multiple_of(8192 + 512 * y, 128), 512)], ut_v.at[:, 1024:1536], 4),
        load(ut_h.at[:, pl.ds(pl.multiple_of(12288 + 256 * y, 128), 256)], ut_v.at[:, 1536:1792], 5),
        load(ut_h.at[:, pl.ds(pl.multiple_of(14336 + 128 * y, 128), 128)], ut_v.at[:, 1792:1920], 6),
        load(ut_h.at[:, 15360:15872], ut_v.at[:, 1920:2432], 7),
    ]
    uc_in = load(uc_h, uc_v, 8)
    lc_in = load(lc_h, lc_v, 9)
    far_in_s = load(far_h, far_s, 10)
    near_in_s = load(near_h, near_s, 11)
    tiles_in = load(tiles_h, tiles_v, 12)

    right = (d + 1) & (LEAF_COUNT - 1)
    left = (d + LEAF_COUNT - 1) & (LEAF_COUNT - 1)
    row_peers = [ROW * y + ((i + k) & (ROW - 1)) for k in FAR_ORDER]
    column_peers = [(d + ROW * k) & (LEAF_COUNT - 1) for k in (4, 3, 5, 2, 6, 1, 7)]
    vec_peers = [(x + k) & 3 for k in (2, 1, 3)]

    barrier = pltpu.get_barrier_semaphore()
    for peer in row_peers + column_peers + [right, left]:
        pl.semaphore_signal(barrier, inc=1, device_id={"leaf": peer, "vec": x}, device_id_type=MESH)
    for peer in vec_peers:
        pl.semaphore_signal(barrier, inc=1, device_id={"leaf": d, "vec": peer}, device_id_type=MESH)

    def send(src, dst, n_send, n_recv, leaf, vec):
        copy = pltpu.make_async_remote_copy(
            src_ref=src, dst_ref=dst, send_sem=send_sem.at[n_send], recv_sem=recv_sem.at[n_recv],
            device_id={"leaf": leaf, "vec": vec}, device_id_type=MESH,
        )
        copy.start()
        return copy

    def wait_for(ref, sem):
        pltpu.make_async_copy(ref, ref, sem).wait()

    own = pl.ds(pl.multiple_of(16 * x, 16), 16)
    vec_in.wait()
    for j in range(8):
        points[8 + j, 0, own, :] = vec_v[:, 128 * j : 128 * j + 128]
    pl.semaphore_wait(barrier, 27)
    for peer in vec_peers:
        send(points.at[8:16, 0, own], points.at[8:16, 0, own], 0, 0, d, peer)

    basis_in.wait()
    lt_in.wait()
    transfer = lt_v[:, 1792:1920]
    crossed = turned(transfer)
    top = (halves(transfer, crossed), halves(crossed, transfer))
    for copy in ut_in:
        copy.wait()
    for p in range(19):
        pair = ut_v[:, 128 * p : 128 * p + 128]
        swapped = turned(pair)
        dup[2 * p] = halves(pair, swapped)
        dup[2 * p + 1] = halves(swapped, pair)
    path = dup[i]
    path_hi[0] = path
    path = path.astype(F32)
    below = [(top[0], None), (top[1], None)]

    def path_step(path, u):
        matrix = dup[BASES[u] + (i >> u if u < 4 else y)]
        path = nn(hilo(path), rows(matrix, matrix))
        path_hi[u], path_lo[u] = two_terms(path)
        return path

    def product_step(below, start):
        following = []
        for m, (hi, lo) in enumerate(below):
            pair = lt_v[:, start + 128 * m : start + 128 * m + 128]
            none = jnp.zeros_like(pair)
            left_side = rows(halves(pair, none), halves(none, pair))
            if lo is None:
                product = nn(left_side, rows(hi, hi))
            else:
                product = nn(lanes(left_side, left_side), rows(hi, hi, lo, lo))
            hi, lo = two_terms(product)
            if start == 0:
                r0_hi[m] = hi
                r0_lo[m] = lo
            following += [(hi[0:64], lo[0:64]), (hi[64:128], lo[64:128])]
        return following

    zero = jnp.zeros((16, 128), BF)
    leaves = []
    for j in range(8):
        tile = vec_v[:, 128 * j : 128 * j + 128]
        block = basis_v[:, 128 * j : 128 * j + 128]
        leaves.append(nt(rows(halves(tile, zero), halves(zero, tile)), rows(block, block)))
    path = path_step(path, 1)
    below = product_step(below, 1536)
    current = []
    for j in range(8):
        coeff = leaves[j]
        first, second = coeff[0:16], coeff[16:32]
        coeffs[8 + j, 0] = halves(first, second).astype(BF)
        coeffs[8 + j, 1] = halves(second, first).astype(BF)
        transfer = lt_v[:, 128 * j : 128 * j + 128]
        lifted = nn(hilo(coeff), rows(transfer, transfer))
        current.append(halves(lifted[0:16], lifted[16:32]))
    path = path_step(path, 2)
    below = product_step(below, 1024)
    for u, start in ((3, 1024), (4, 1536)):
        following = []
        for m in range(len(current) // 2):
            hi, lo = two_terms(rows(current[2 * m], current[2 * m + 1]))
            transfer = lt_v[:, start + 128 * m : start + 128 * m + 128]
            lifted = nn(lanes(hi, lo), rows(transfer, transfer, transfer, transfer))
            following.append(halves(lifted[0:16], lifted[16:32]))
        current = following
        path = path_step(path, u)
        if u == 3:
            product_step(below, 0)
    first_hi, first_lo = two_terms(current[0])
    second_hi, second_lo = two_terms(current[1])
    root = nn(lanes(first_hi, first_lo, second_hi, second_lo), rows(*([top[0]] * 4 + [top[1]] * 4)))
    ext0[2 + i] = hilo(root)
    for peer in row_peers:
        send(ext0.at[2 + i], ext0.at[2 + i], 1, 1, peer, x)

    send(coeffs.at[8:16, 0], coeffs.at[0:8, 0], 2, 2, right, x)
    send(coeffs.at[8:16, 0], coeffs.at[16:24, 0], 3, 3, left, x)
    wait_for(points.at[8:16, 0, 0:48], recv_sem.at[0])
    send(points.at[8:16, 0], points.at[0:8, 0], 4, 4, right, x)
    send(points.at[8:16, 0], points.at[16:24, 0], 5, 5, left, x)

    wait_for(ext0.at[0:15], recv_sem.at[1])
    after = (d + ROW) & (LEAF_COUNT - 1)
    before = (d + LEAF_COUNT - ROW) & (LEAF_COUNT - 1)
    for u in range(4):
        ext, count = exts[u], ROW >> u
        send(ext.at[count : count + 2], ext.at[0:2], 6 + 2 * u, 6 + 2 * u, after, x)
        send(ext.at[2:4], ext.at[2 + count : 4 + count], 7 + 2 * u, 7 + 2 * u, before, x)
        for m in range(count // 2):
            left_m, right_m = dup[BASES[u] + 2 * m], dup[BASES[u] + 2 * m + 1]
            value = nn(lanes(ext[2 + 2 * m], ext[3 + 2 * m]), rows(left_m, left_m, right_m, right_m))
            if u < 3:
                exts[u + 1][2 + m] = hilo(value)
            else:
                ext4[y] = hilo(value)
    for peer in column_peers:
        send(ext4.at[y], ext4.at[y], 14, 14, peer, x)

    near_in_s.wait()
    tiles_in.wait()
    wait_for(points.at[0:8, 0], recv_sem.at[4])
    wait_for(points.at[16:24, 0], recv_sem.at[5])
    for p in range(24):
        points[p, 1] = turned(points[p, 0])
    first_leaf = ROW * d - ROW

    def chosen(table, lists, slots, column):
        parts = []
        for s in range(0, slots, 2):
            a = jnp.clip(lists[s, column] - first_leaf, 0, 3 * ROW - 1)
            b = jnp.clip(lists[s + 1, column] - first_leaf, 0, 3 * ROW - 1)
            parts.append(halves(table[a >> 1, a & 1], table[b >> 1, 1 - (b & 1)]))
        return lanes(*parts)

    for q in range(2):
        source = rows(*[chosen(points, near_s, 6, 4 * x + 2 * q + e) for e in range(2)])
        value = nt(source, rows(tiles_v[2 * q], tiles_v[2 * q + 1]))
        value = halves(value[0:64], value[64:128]).astype(BF)
        for v in range(4):
            near_out[v, q] = value[16 * v : 16 * v + 16]
    for n, peer in enumerate(vec_peers):
        send(near_out.at[peer], near_in.at[x], 15, 15, d, peer)
    near_in[x] = near_out[x]

    far_in_s.wait()
    lc_in.wait()
    wait_for(coeffs.at[0:8, 0], recv_sem.at[2])
    wait_for(coeffs.at[16:24, 0], recv_sem.at[3])
    for p in list(range(8)) + list(range(16, 24)):
        coeffs[p, 1] = turned(coeffs[p, 0])
    for j in range(8):
        source = rows(*[chosen(coeffs, far_s, 6, 2 * j + e) for e in range(2)])
        value = nt(source, rows(lc_v[:, 768 * j : 768 * j + 384], lc_v[:, 768 * j + 384 : 768 * j + 768]))
        far_out[j] = halves(value[0:16], value[16:32])

    uc_in.wait()
    weights = []
    for o in range(2):
        pair = uc_v[:, 128 * o : 128 * o + 128]
        swapped = turned(pair)
        weights += [halves(pair, swapped), halves(swapped, pair)]
    weights = lanes(*weights)
    for n in range(6, 14):
        ext, count = exts[(n - 6) // 2], ROW >> ((n - 6) // 2)
        wait_for(ext.at[0:2] if n % 2 == 0 else ext.at[2 + count : 4 + count], recv_sem.at[n])
    wait_for(ext4.at[0:7], recv_sem.at[14])
    for m in range(4):
        left_m, right_m = dup[30 + 2 * m], dup[31 + 2 * m]
        value = nn(lanes(ext4[2 * m], ext4[2 * m + 1]), rows(left_m, left_m, right_m, right_m))
        ext5[m] = hilo(value)
    sources = []
    for u in range(6):
        g = d >> u
        odd = g & 1
        number = LEAF_COUNT >> u
        parts = []
        for o, wanted in ((-3, odd == 1), (-2, None), (2, None), (3, odd == 0)):
            if u < 4:
                shift = o if wanted is None else (-3 * odd if o < 0 else 3 * (1 - odd))
                tile = exts[u][2 + (i >> u) + shift]
            else:
                tile = (ext4, ext5)[u - 4][(g + o + number) & (number - 1)]
            valid = (g + o >= 0) if o < 0 else (g + o < number)
            if wanted is not None:
                valid = jnp.logical_and(valid, wanted)
            keep = jnp.where(valid, 1.0, 0.0).astype(F32)
            parts.append((tile.astype(F32) * keep).astype(BF))
        sources.append(lanes(*parts))
    coupled = nt(rows(*sources), rows(weights, weights))
    left_side, right_side = [], []
    for u in range(1, 6):
        tile = hilo(coupled[16 * u : 16 * u + 16])
        left_side.append(tile)
        right_side.append(path_hi[u - 1])
        if u > 1:
            left_side.append(tile)
            right_side.append(path_lo[u - 1])
    matrix = lanes(*right_side)
    down = coupled[0:16] + nt(lanes(*left_side), rows(matrix, matrix))
    down = hilo(down)
    down = lanes(down, down)

    wait_for(near_in.at[0:3], recv_sem.at[15])
    for j in range(8):
        local = nt(down, lanes(r0_hi[j], r0_lo[j]))
        leaf_down = (local + far_out[j]).astype(BF)
        block = basis_v[:, 128 * j : 128 * j + 128]
        none = jnp.zeros_like(block)
        value = nn(leaf_down, rows(halves(block, none), halves(none, block)))
        out_ref[:, 128 * j : 128 * j + 128] = (value + near_in[j // 2, j % 2].astype(F32)).astype(BF)

    wait_for(points.at[8:16, 0, 0:48], send_sem.at[0])
    wait_for(ext0.at[0:15], send_sem.at[1])
    wait_for(coeffs.at[0:8, 0], send_sem.at[2])
    wait_for(coeffs.at[0:8, 0], send_sem.at[3])
    wait_for(points.at[0:8, 0], send_sem.at[4])
    wait_for(points.at[0:8, 0], send_sem.at[5])
    for n in range(6, 14):
        wait_for(ext0.at[0:2], send_sem.at[n])
    wait_for(ext4.at[0:7], send_sem.at[14])
    wait_for(near_out.at[0:3], send_sem.at[15])


def shards(vectors, leaf_basis, local_transfer, upper_transfer, upper_coupling, leaf_coupling, far_list, near_list, near_tiles):
    tile = (16, 128)
    scratch = [
        pltpu.VMEM(vectors.shape, BF),
        pltpu.VMEM(leaf_basis.shape, BF),
        pltpu.VMEM(local_transfer.shape, BF),
        pltpu.VMEM((64, 2432), BF),
        pltpu.VMEM(upper_coupling.shape, BF),
        pltpu.VMEM(leaf_coupling.shape, BF),
        pltpu.SMEM(far_list.shape, jnp.int32),
        pltpu.SMEM(near_list.shape, jnp.int32),
        pltpu.VMEM(near_tiles.shape, BF),
        pltpu.VMEM((24, 2, 64, 128), BF),
        pltpu.VMEM((24, 2) + tile, BF),
        pltpu.VMEM((20,) + tile, BF),
        pltpu.VMEM((12,) + tile, BF),
        pltpu.VMEM((8,) + tile, BF),
        pltpu.VMEM((6,) + tile, BF),
        pltpu.VMEM((8,) + tile, BF),
        pltpu.VMEM((4,) + tile, BF),
        pltpu.VMEM((38, 64, 128), BF),
        pltpu.VMEM((5, 64, 128), BF),
        pltpu.VMEM((5, 64, 128), BF),
        pltpu.VMEM((8, 128, 128), BF),
        pltpu.VMEM((8, 128, 128), BF),
        pltpu.VMEM((8,) + tile, F32),
        pltpu.VMEM((4, 2) + tile, BF),
        pltpu.VMEM((4, 2) + tile, BF),
        pltpu.SemaphoreType.DMA((13,)),
        pltpu.SemaphoreType.DMA((16,)),
        pltpu.SemaphoreType.DMA((16,)),
    ]
    return pl.pallas_call(
        kernel,
        out_shape=pltpu.VMEM(vectors.shape, BF),
        in_specs=[pl.BlockSpec(memory_space=pl.ANY)] * 9,
        out_specs=pl.BlockSpec(memory_space=pltpu.VMEM),
        scratch_shapes=scratch,
        compiler_params=pltpu.CompilerParams(
            collective_id=0, has_side_effects=True, vmem_limit_bytes=62 * 1024 * 1024
        ),
    )(vectors, leaf_basis, local_transfer, upper_transfer, upper_coupling, leaf_coupling, far_list, near_list, near_tiles)


def solution(mesh):
    placed = (
        P("vec", "leaf"),
        P(None, "leaf"),
        P(None, "leaf"),
        P(),
        P(),
        P(None, "leaf"),
        P(None, "leaf"),
        P(None, "leaf"),
        P(("leaf", "vec"), None, None),
    )
    return jax.shard_map(
        shards, mesh=mesh, in_specs=placed, out_specs=P("vec", "leaf"), check_vma=False
    )
```

```python
import jax
import jax.numpy as jnp
from jax import lax
from jax.experimental import pallas as pl
from jax.experimental.pallas import tpu as pltpu
from jax.sharding import PartitionSpec as P

MESH = pl.DeviceIdType.MESH
BF = jnp.bfloat16
F32 = jnp.float32
ROW = 16
ROWS = 8
LEAF_COUNT = ROW * ROWS
BASES = (0, 16, 24, 28, 30)
FAR_ORDER = (8, 9, 7, 10, 6, 11, 5, 12, 4, 13, 3, 14, 2, 15, 1)


def low(shape):
    return lax.broadcasted_iota(jnp.int32, shape, 1) < 64


def halves(a, b):
    return jnp.where(low(a.shape), a, b)


def turned(tile):
    return pltpu.roll(tile.astype(F32), 64, 1).astype(tile.dtype)


def rounded(x):
    return x.astype(BF).astype(F32)


def hilo(x):
    hi = rounded(x)
    return halves(hi, x - hi).astype(BF)


def two_terms(x):
    hi = rounded(x)
    return hi.astype(BF), (x - hi).astype(BF)


def nn(a, b):
    return jnp.dot(a, b, preferred_element_type=F32)


def nt(a, b):
    return lax.dot_general(a, b, (((1,), (1,)), ((), ())), preferred_element_type=F32)


def rows(*parts):
    return jnp.concatenate(parts, axis=0)


def lanes(*parts):
    return jnp.concatenate(parts, axis=1)


def kernel(
    vec_h, basis_h, lt_h, ut_h, uc_h, lc_h, far_h, near_h, tiles_h, out_ref,
    basis_v, lt_v, ut_v, uc_v, lc_v, far_s, near_s, tiles_v,
    arrived, points, coeffs, ext0, ext1, ext2, ext3, ext4, ext5,
    dup, path_hi, path_lo, r0_hi, r0_lo, far_out, near_out, near_in,
    in_sem, send_sem, recv_sem,
):
    d = lax.axis_index("leaf")
    x = lax.axis_index("vec")
    y = d >> 4
    i = d & 15
    exts = (ext0, ext1, ext2, ext3)

    def load(src, dst, n):
        copy = pltpu.make_async_copy(src, dst, in_sem.at[n])
        copy.start()
        return copy

    own = pl.ds(pl.multiple_of(16 * x, 16), 16)
    vec_in = load(vec_h, arrived.at[1, own], 0)
    basis_in = load(basis_h, basis_v, 1)
    lt_in = load(lt_h, lt_v, 2)
    ut_in = [
        load(ut_h.at[:, pl.ds(pl.multiple_of(1024 * y, 128), 1024)], ut_v.at[:, 0:1024], 3),
        load(ut_h.at[:, pl.ds(pl.multiple_of(8192 + 512 * y, 128), 512)], ut_v.at[:, 1024:1536], 4),
        load(ut_h.at[:, pl.ds(pl.multiple_of(12288 + 256 * y, 128), 256)], ut_v.at[:, 1536:1792], 5),
        load(ut_h.at[:, pl.ds(pl.multiple_of(14336 + 128 * y, 128), 128)], ut_v.at[:, 1792:1920], 6),
        load(ut_h.at[:, 15360:15872], ut_v.at[:, 1920:2432], 7),
    ]
    right = (d + 1) & (LEAF_COUNT - 1)
    left = (d + LEAF_COUNT - 1) & (LEAF_COUNT - 1)
    row_peers = [ROW * y + ((i + k) & (ROW - 1)) for k in FAR_ORDER]
    column_peers = [(d + ROW * k) & (LEAF_COUNT - 1) for k in (4, 3, 5, 2, 6, 1, 7)]
    vec_peers = [(x + k) & 3 for k in (2, 1, 3)]

    barrier = pltpu.get_barrier_semaphore()
    for peer in row_peers + column_peers + [right, left]:
        pl.semaphore_signal(barrier, inc=1, device_id={"leaf": peer, "vec": x}, device_id_type=MESH)
    for leaf in (d, right, left):
        for peer in vec_peers:
            pl.semaphore_signal(barrier, inc=1, device_id={"leaf": leaf, "vec": peer}, device_id_type=MESH)
    uc_in = load(uc_h, uc_v, 8)
    lc_in = load(lc_h, lc_v, 9)
    far_in_s = load(far_h, far_s, 10)
    near_in_s = load(near_h, near_s, 11)
    tiles_in = load(tiles_h, tiles_v, 12)


    def send(src, dst, n_send, n_recv, leaf, vec):
        copy = pltpu.make_async_remote_copy(
            src_ref=src, dst_ref=dst, send_sem=send_sem.at[n_send], recv_sem=recv_sem.at[n_recv],
            device_id={"leaf": leaf, "vec": vec}, device_id_type=MESH,
        )
        copy.start()
        return copy

    def wait_for(ref, sem):
        pltpu.make_async_copy(ref, ref, sem).wait()

    pl.semaphore_wait(barrier, 33)
    for peer in vec_peers:
        send(vec_h, arrived.at[1, own], 0, 0, d, peer)
    for peer in vec_peers + [x]:
        send(vec_h, arrived.at[0, own], 4, 4, right, peer)
        send(vec_h, arrived.at[2, own], 5, 5, left, peer)

    vec_in.wait()
    basis_in.wait()
    lt_in.wait()
    transfer = lt_v[:, 1792:1920]
    crossed = turned(transfer)
    top = (halves(transfer, crossed), halves(crossed, transfer))
    for copy in ut_in:
        copy.wait()
    for p in range(19):
        pair = ut_v[:, 128 * p : 128 * p + 128]
        swapped = turned(pair)
        dup[2 * p] = halves(pair, swapped)
        dup[2 * p + 1] = halves(swapped, pair)
    path = dup[i]
    path_hi[0] = path
    path = path.astype(F32)
    below = [(top[0], None), (top[1], None)]

    def path_step(path, u):
        matrix = dup[BASES[u] + (i >> u if u < 4 else y)]
        path = nn(hilo(path), rows(matrix, matrix))
        path_hi[u], path_lo[u] = two_terms(path)
        return path

    def product_step(below, start):
        following = []
        for m, (hi, lo) in enumerate(below):
            pair = lt_v[:, start + 128 * m : start + 128 * m + 128]
            none = jnp.zeros_like(pair)
            left_side = rows(halves(pair, none), halves(none, pair))
            if lo is None:
                product = nn(left_side, rows(hi, hi))
            else:
                product = nn(lanes(left_side, left_side), rows(hi, hi, lo, lo))
            hi, lo = two_terms(product)
            if start == 0:
                r0_hi[m] = hi
                r0_lo[m] = lo
            following += [(hi[0:64], lo[0:64]), (hi[64:128], lo[64:128])]
        return following

    zero = jnp.zeros((16, 128), BF)
    leaves = []
    for j in range(8):
        tile = arrived[1, own, 128 * j : 128 * j + 128]
        block = basis_v[:, 128 * j : 128 * j + 128]
        leaves.append(nt(rows(halves(tile, zero), halves(zero, tile)), rows(block, block)))
    path = path_step(path, 1)
    below = product_step(below, 1536)
    current = []
    for j in range(8):
        coeff = leaves[j]
        first, second = coeff[0:16], coeff[16:32]
        coeffs[8 + j, 0] = halves(first, second).astype(BF)
        coeffs[8 + j, 1] = halves(second, first).astype(BF)
        transfer = lt_v[:, 128 * j : 128 * j + 128]
        lifted = nn(hilo(coeff), rows(transfer, transfer))
        current.append(halves(lifted[0:16], lifted[16:32]))
    path = path_step(path, 2)
    below = product_step(below, 1024)
    for u, start in ((3, 1024), (4, 1536)):
        following = []
        for m in range(len(current) // 2):
            hi, lo = two_terms(rows(current[2 * m], current[2 * m + 1]))
            transfer = lt_v[:, start + 128 * m : start + 128 * m + 128]
            lifted = nn(lanes(hi, lo), rows(transfer, transfer, transfer, transfer))
            following.append(halves(lifted[0:16], lifted[16:32]))
        current = following
        path = path_step(path, u)
        if u == 3:
            product_step(below, 0)
    first_hi, first_lo = two_terms(current[0])
    second_hi, second_lo = two_terms(current[1])
    root = nn(lanes(first_hi, first_lo, second_hi, second_lo), rows(*([top[0]] * 4 + [top[1]] * 4)))
    ext0[2 + i] = hilo(root)
    for peer in row_peers:
        send(ext0.at[2 + i], ext0.at[2 + i], 1, 1, peer, x)

    send(coeffs.at[8:16, 0], coeffs.at[0:8, 0], 2, 2, right, x)
    send(coeffs.at[8:16, 0], coeffs.at[16:24, 0], 3, 3, left, x)

    wait_for(ext0.at[0:15], recv_sem.at[1])
    after = (d + ROW) & (LEAF_COUNT - 1)
    before = (d + LEAF_COUNT - ROW) & (LEAF_COUNT - 1)
    for u in range(4):
        ext, count = exts[u], ROW >> u
        send(ext.at[count : count + 2], ext.at[0:2], 6 + 2 * u, 6 + 2 * u, after, x)
        send(ext.at[2:4], ext.at[2 + count : 4 + count], 7 + 2 * u, 7 + 2 * u, before, x)
        for m in range(count // 2):
            left_m, right_m = dup[BASES[u] + 2 * m], dup[BASES[u] + 2 * m + 1]
            value = nn(lanes(ext[2 + 2 * m], ext[3 + 2 * m]), rows(left_m, left_m, right_m, right_m))
            if u < 3:
                exts[u + 1][2 + m] = hilo(value)
            else:
                ext4[y] = hilo(value)
    for peer in column_peers:
        send(ext4.at[y], ext4.at[y], 14, 14, peer, x)

    near_in_s.wait()
    tiles_in.wait()
    wait_for(arrived.at[1, 0:48], recv_sem.at[0])
    wait_for(arrived.at[0], recv_sem.at[4])
    wait_for(arrived.at[2], recv_sem.at[5])
    for w in range(3):
        for j in range(8):
            block = arrived[w, :, 128 * j : 128 * j + 128]
            points[8 * w + j, 0] = block
            points[8 * w + j, 1] = turned(block)
    first_leaf = ROW * d - ROW

    def chosen(table, lists, slots, column):
        parts = []
        for s in range(0, slots, 2):
            a = jnp.clip(lists[s, column] - first_leaf, 0, 3 * ROW - 1)
            b = jnp.clip(lists[s + 1, column] - first_leaf, 0, 3 * ROW - 1)
            parts.append(halves(table[a >> 1, a & 1], table[b >> 1, 1 - (b & 1)]))
        return lanes(*parts)

    for q in range(2):
        source = rows(*[chosen(points, near_s, 6, 4 * x + 2 * q + e) for e in range(2)])
        value = nt(source, rows(tiles_v[2 * q], tiles_v[2 * q + 1]))
        value = halves(value[0:64], value[64:128]).astype(BF)
        for v in range(4):
            near_out[v, q] = value[16 * v : 16 * v + 16]
    for n, peer in enumerate(vec_peers):
        send(near_out.at[peer], near_in.at[x], 15, 15, d, peer)
    near_in[x] = near_out[x]

    far_in_s.wait()
    lc_in.wait()
    wait_for(coeffs.at[0:8, 0], recv_sem.at[2])
    wait_for(coeffs.at[16:24, 0], recv_sem.at[3])
    for p in list(range(8)) + list(range(16, 24)):
        coeffs[p, 1] = turned(coeffs[p, 0])
    for j in range(8):
        source = rows(*[chosen(coeffs, far_s, 6, 2 * j + e) for e in range(2)])
        value = nt(source, rows(lc_v[:, 768 * j : 768 * j + 384], lc_v[:, 768 * j + 384 : 768 * j + 768]))
        far_out[j] = halves(value[0:16], value[16:32])

    uc_in.wait()
    weights = []
    for o in range(2):
        pair = uc_v[:, 128 * o : 128 * o + 128]
        swapped = turned(pair)
        weights += [halves(pair, swapped), halves(swapped, pair)]
    weights = lanes(*weights)
    for n in range(6, 14):
        ext, count = exts[(n - 6) // 2], ROW >> ((n - 6) // 2)
        wait_for(ext.at[0:2] if n % 2 == 0 else ext.at[2 + count : 4 + count], recv_sem.at[n])
    wait_for(ext4.at[0:7], recv_sem.at[14])
    for m in range(4):
        left_m, right_m = dup[30 + 2 * m], dup[31 + 2 * m]
        value = nn(lanes(ext4[2 * m], ext4[2 * m + 1]), rows(left_m, left_m, right_m, right_m))
        ext5[m] = hilo(value)
    sources = []
    for u in range(6):
        g = d >> u
        odd = g & 1
        number = LEAF_COUNT >> u
        parts = []
        for o, wanted in ((-3, odd == 1), (-2, None), (2, None), (3, odd == 0)):
            if u < 4:
                shift = o if wanted is None else (-3 * odd if o < 0 else 3 * (1 - odd))
                tile = exts[u][2 + (i >> u) + shift]
            else:
                tile = (ext4, ext5)[u - 4][(g + o + number) & (number - 1)]
            valid = (g + o >= 0) if o < 0 else (g + o < number)
            if wanted is not None:
                valid = jnp.logical_and(valid, wanted)
            keep = jnp.where(valid, 1.0, 0.0).astype(F32)
            parts.append((tile.astype(F32) * keep).astype(BF))
        sources.append(lanes(*parts))
    coupled = nt(rows(*sources), rows(weights, weights))
    left_side, right_side = [], []
    for u in range(1, 6):
        tile = hilo(coupled[16 * u : 16 * u + 16])
        left_side.append(tile)
        right_side.append(path_hi[u - 1])
        if u > 1:
            left_side.append(tile)
            right_side.append(path_lo[u - 1])
    matrix = lanes(*right_side)
    down = coupled[0:16] + nt(lanes(*left_side), rows(matrix, matrix))
    down = hilo(down)
    down = lanes(down, down)

    wait_for(near_in.at[0:3], recv_sem.at[15])
    for j in range(8):
        local = nt(down, lanes(r0_hi[j], r0_lo[j]))
        leaf_down = (local + far_out[j]).astype(BF)
        block = basis_v[:, 128 * j : 128 * j + 128]
        none = jnp.zeros_like(block)
        value = nn(leaf_down, rows(halves(block, none), halves(none, block)))
        out_ref[:, 128 * j : 128 * j + 128] = (value + near_in[j // 2, j % 2].astype(F32)).astype(BF)

    wait_for(arrived.at[1, 0:48], send_sem.at[0])
    wait_for(ext0.at[0:15], send_sem.at[1])
    wait_for(coeffs.at[0:8, 0], send_sem.at[2])
    wait_for(coeffs.at[0:8, 0], send_sem.at[3])
    wait_for(arrived.at[0], send_sem.at[4])
    wait_for(arrived.at[2], send_sem.at[5])
    for n in range(6, 14):
        wait_for(ext0.at[0:2], send_sem.at[n])
    wait_for(ext4.at[0:7], send_sem.at[14])
    wait_for(near_out.at[0:3], send_sem.at[15])


def shards(vectors, leaf_basis, local_transfer, upper_transfer, upper_coupling, leaf_coupling, far_list, near_list, near_tiles):
    tile = (16, 128)
    scratch = [
        pltpu.VMEM(leaf_basis.shape, BF),
        pltpu.VMEM(local_transfer.shape, BF),
        pltpu.VMEM((64, 2432), BF),
        pltpu.VMEM(upper_coupling.shape, BF),
        pltpu.VMEM(leaf_coupling.shape, BF),
        pltpu.SMEM(far_list.shape, jnp.int32),
        pltpu.SMEM(near_list.shape, jnp.int32),
        pltpu.VMEM(near_tiles.shape, BF),
        pltpu.VMEM((3, 64, 1024), BF),
        pltpu.VMEM((24, 2, 64, 128), BF),
        pltpu.VMEM((24, 2) + tile, BF),
        pltpu.VMEM((20,) + tile, BF),
        pltpu.VMEM((12,) + tile, BF),
        pltpu.VMEM((8,) + tile, BF),
        pltpu.VMEM((6,) + tile, BF),
        pltpu.VMEM((8,) + tile, BF),
        pltpu.VMEM((4,) + tile, BF),
        pltpu.VMEM((38, 64, 128), BF),
        pltpu.VMEM((5, 64, 128), BF),
        pltpu.VMEM((5, 64, 128), BF),
        pltpu.VMEM((8, 128, 128), BF),
        pltpu.VMEM((8, 128, 128), BF),
        pltpu.VMEM((8,) + tile, F32),
        pltpu.VMEM((4, 2) + tile, BF),
        pltpu.VMEM((4, 2) + tile, BF),
        pltpu.SemaphoreType.DMA((13,)),
        pltpu.SemaphoreType.DMA((16,)),
        pltpu.SemaphoreType.DMA((16,)),
    ]
    return pl.pallas_call(
        kernel,
        out_shape=pltpu.VMEM(vectors.shape, BF),
        in_specs=[pl.BlockSpec(memory_space=pl.ANY)] * 9,
        out_specs=pl.BlockSpec(memory_space=pltpu.VMEM),
        scratch_shapes=scratch,
        compiler_params=pltpu.CompilerParams(
            collective_id=0, has_side_effects=True, vmem_limit_bytes=62 * 1024 * 1024
        ),
    )(vectors, leaf_basis, local_transfer, upper_transfer, upper_coupling, leaf_coupling, far_list, near_list, near_tiles)


def solution(mesh):
    placed = (
        P("vec", "leaf"),
        P(None, "leaf"),
        P(None, "leaf"),
        P(),
        P(),
        P(None, "leaf"),
        P(None, "leaf"),
        P(None, "leaf"),
        P(("leaf", "vec"), None, None),
    )
    return jax.shard_map(
        shards, mesh=mesh, in_specs=placed, out_specs=P("vec", "leaf"), check_vma=False
    )
```

```python
import jax
import jax.numpy as jnp
from jax import lax
from jax.experimental import pallas as pl
from jax.experimental.pallas import tpu as pltpu
from jax.sharding import PartitionSpec as P

MESH = pl.DeviceIdType.MESH
BF = jnp.bfloat16
F32 = jnp.float32
ROW = 16
ROWS = 8
LEAF_COUNT = ROW * ROWS
BASES = (0, 16, 24, 28, 30)
PREV = 42
NEXT = 51
FAR_ORDER = (8, 9, 7, 10, 6, 11, 5, 12, 4, 13, 3, 14, 2, 15, 1)


def low(shape):
    return lax.broadcasted_iota(jnp.int32, shape, 1) < 64


def halves(a, b):
    return jnp.where(low(a.shape), a, b)


def turned(tile):
    return pltpu.roll(tile.astype(F32), 64, 1).astype(tile.dtype)


def rounded(x):
    return x.astype(BF).astype(F32)


def hilo(x):
    hi = rounded(x)
    return halves(hi, x - hi).astype(BF)


def two_terms(x):
    hi = rounded(x)
    return hi.astype(BF), (x - hi).astype(BF)


def nn(a, b):
    return jnp.dot(a, b, preferred_element_type=F32)


def nt(a, b):
    return lax.dot_general(a, b, (((1,), (1,)), ((), ())), preferred_element_type=F32)


def rows(*parts):
    return jnp.concatenate(parts, axis=0)


def lanes(*parts):
    return jnp.concatenate(parts, axis=1)


def kernel(
    vec_h, basis_h, lt_h, ut_h, uc_h, lc_h, far_h, near_h, tiles_h, out_ref,
    vec_v, basis_v, lt_v, ut_v, uc_v, lc_v, far_s, near_s, tiles_v,
    points, coeffs, nodes, heads, tails,
    dup, path_hi, path_lo, r0_hi, r0_lo, far_out, near_out, near_in,
    in_sem, send_sem, recv_sem,
):
    d = lax.axis_index("leaf")
    x = lax.axis_index("vec")
    y = d >> 4
    i = d & 15

    def load(src, dst, n):
        copy = pltpu.make_async_copy(src, dst, in_sem.at[n])
        copy.start()
        return copy

    vec_in = load(vec_h, vec_v, 0)
    basis_in = load(basis_h, basis_v, 1)
    lt_in = load(lt_h, lt_v, 2)
    ut_in = [
        load(ut_h.at[:, pl.ds(pl.multiple_of(1024 * y, 128), 1024)], ut_v.at[:, 0:1024], 3),
        load(ut_h.at[:, pl.ds(pl.multiple_of(8192 + 512 * y, 128), 512)], ut_v.at[:, 1024:1536], 4),
        load(ut_h.at[:, pl.ds(pl.multiple_of(12288 + 256 * y, 128), 256)], ut_v.at[:, 1536:1792], 5),
        load(ut_h.at[:, pl.ds(pl.multiple_of(14336 + 128 * y, 128), 128)], ut_v.at[:, 1792:1920], 6),
        load(ut_h.at[:, 15360:15872], ut_v.at[:, 1920:2432], 7),
    ]
    right = (d + 1) & (LEAF_COUNT - 1)
    left = (d + LEAF_COUNT - 1) & (LEAF_COUNT - 1)
    row_peers = [ROW * y + ((i + k) & (ROW - 1)) for k in FAR_ORDER]
    column_peers = [(d + ROW * k) & (LEAF_COUNT - 1) for k in (4, 3, 5, 2, 1, 6, 7)]
    vec_peers = [(x + k) & 3 for k in (2, 1, 3)]

    barrier = pltpu.get_barrier_semaphore()
    for peer in row_peers + column_peers + [right, left]:
        pl.semaphore_signal(barrier, inc=1, device_id={"leaf": peer, "vec": x}, device_id_type=MESH)
    for peer in vec_peers:
        pl.semaphore_signal(barrier, inc=1, device_id={"leaf": d, "vec": peer}, device_id_type=MESH)

    def send(src, dst, n_send, n_recv, leaf, vec):
        copy = pltpu.make_async_remote_copy(
            src_ref=src, dst_ref=dst, send_sem=send_sem.at[n_send], recv_sem=recv_sem.at[n_recv],
            device_id={"leaf": leaf, "vec": vec}, device_id_type=MESH,
        )
        copy.start()
        return copy

    def wait_for(ref, sem):
        pltpu.make_async_copy(ref, ref, sem).wait()

    own = pl.ds(pl.multiple_of(16 * x, 16), 16)
    vec_in.wait()
    for j in range(8):
        points[8 + j, 0, own, :] = vec_v[:, 128 * j : 128 * j + 128]
    pl.semaphore_wait(barrier, 27)
    for peer in vec_peers:
        send(points.at[8:16, 0, own], points.at[8:16, 0, own], 0, 0, d, peer)

    basis_in.wait()
    lt_in.wait()
    transfer = lt_v[:, 1792:1920]
    crossed = turned(transfer)
    top = (halves(transfer, crossed), halves(crossed, transfer))

    zero = jnp.zeros((16, 128), BF)
    leaves = []
    for j in range(8):
        tile = vec_v[:, 128 * j : 128 * j + 128]
        block = basis_v[:, 128 * j : 128 * j + 128]
        leaves.append(nt(rows(halves(tile, zero), halves(zero, tile)), rows(block, block)))
    current = []
    for j in range(8):
        coeff = leaves[j]
        first, second = coeff[0:16], coeff[16:32]
        coeffs[8 + j, 0] = halves(first, second).astype(BF)
        coeffs[8 + j, 1] = halves(second, first).astype(BF)
        transfer = lt_v[:, 128 * j : 128 * j + 128]
        lifted = nn(hilo(coeff), rows(transfer, transfer))
        current.append(halves(lifted[0:16], lifted[16:32]))
    for start in (1024, 1536):
        following = []
        for m in range(len(current) // 2):
            hi, lo = two_terms(rows(current[2 * m], current[2 * m + 1]))
            transfer = lt_v[:, start + 128 * m : start + 128 * m + 128]
            lifted = nn(lanes(hi, lo), rows(transfer, transfer, transfer, transfer))
            following.append(halves(lifted[0:16], lifted[16:32]))
        current = following
    first_hi, first_lo = two_terms(current[0])
    second_hi, second_lo = two_terms(current[1])
    root = nn(lanes(first_hi, first_lo, second_hi, second_lo), rows(*([top[0]] * 4 + [top[1]] * 4)))
    nodes[i] = hilo(root)
    for peer in row_peers:
        send(nodes.at[i], nodes.at[i], 1, 1, peer, x)
    uc_in = load(uc_h, uc_v, 8)
    lc_in = load(lc_h, lc_v, 9)
    far_in_s = load(far_h, far_s, 10)
    near_in_s = load(near_h, near_s, 11)
    tiles_in = load(tiles_h, tiles_v, 12)

    send(coeffs.at[8:16, 0], coeffs.at[0:8, 0], 2, 2, right, x)
    send(coeffs.at[8:16, 0], coeffs.at[16:24, 0], 3, 3, left, x)
    wait_for(points.at[8:16, 0, 0:48], recv_sem.at[0])
    send(points.at[8:16, 0], points.at[0:8, 0], 4, 4, right, x)
    send(points.at[8:16, 0], points.at[16:24, 0], 5, 5, left, x)

    for copy in ut_in:
        copy.wait()
    for p in range(19):
        pair = ut_v[:, 128 * p : 128 * p + 128]
        swapped = turned(pair)
        dup[2 * p] = halves(pair, swapped)
        dup[2 * p + 1] = halves(swapped, pair)

    path = dup[i]
    path_hi[0] = path
    path = path.astype(F32)
    below = [(top[0], None), (top[1], None)]

    def path_step(path, u):
        matrix = dup[BASES[u] + (i >> u if u < 4 else y)]
        path = nn(hilo(path), rows(matrix, matrix))
        path_hi[u], path_lo[u] = two_terms(path)
        return path

    def product_step(below, start):
        following = []
        for m, (hi, lo) in enumerate(below):
            pair = lt_v[:, start + 128 * m : start + 128 * m + 128]
            none = jnp.zeros_like(pair)
            left_side = rows(halves(pair, none), halves(none, pair))
            if lo is None:
                product = nn(left_side, rows(hi, hi))
            else:
                product = nn(lanes(left_side, left_side), rows(hi, hi, lo, lo))
            hi, lo = two_terms(product)
            if start == 0:
                r0_hi[m] = hi
                r0_lo[m] = lo
            following += [(hi[0:64], lo[0:64]), (hi[64:128], lo[64:128])]
        return following

    for u, start in ((1, 1536), (2, 1024), (3, 0)):
        path = path_step(path, u)
        below = product_step(below, start)
    path_step(path, 4)

    wait_for(nodes.at[0:15], recv_sem.at[1])
    for u in range(4):
        base, count = BASES[u], ROW >> u
        for m in range(count // 2):
            left_m, right_m = dup[base + 2 * m], dup[base + 2 * m + 1]
            value = nn(lanes(nodes[base + 2 * m], nodes[base + 2 * m + 1]), rows(left_m, left_m, right_m, right_m))
            if u < 3:
                nodes[BASES[u + 1] + m] = hilo(value)
            else:
                top_tile = hilo(value)
                nodes[30 + y] = top_tile
                heads[8] = top_tile
                tails[8] = top_tile
    for u in range(4):
        for e in range(2):
            heads[2 * u + e] = nodes[BASES[u] + e]
            tails[2 * u + e] = nodes[BASES[u + 1] - 2 + e]
    send(tails, nodes.at[PREV : PREV + 9], 6, 6, column_peers[4], x)
    send(heads, nodes.at[NEXT : NEXT + 9], 7, 7, column_peers[6], x)
    for peer in column_peers[:4] + column_peers[5:6]:
        send(nodes.at[30 + y], nodes.at[30 + y], 8, 8, peer, x)

    near_in_s.wait()
    tiles_in.wait()
    wait_for(points.at[0:8, 0], recv_sem.at[4])
    wait_for(points.at[16:24, 0], recv_sem.at[5])
    for p in range(24):
        points[p, 1] = turned(points[p, 0])
    first_leaf = ROW * d - ROW

    def chosen(table, lists, slots, column):
        parts = []
        for s in range(0, slots, 2):
            a = jnp.clip(lists[s, column] - first_leaf, 0, 3 * ROW - 1)
            b = jnp.clip(lists[s + 1, column] - first_leaf, 0, 3 * ROW - 1)
            parts.append(halves(table[a >> 1, a & 1], table[b >> 1, 1 - (b & 1)]))
        return lanes(*parts)

    for q in range(2):
        source = rows(*[chosen(points, near_s, 6, 4 * x + 2 * q + e) for e in range(2)])
        value = nt(source, rows(tiles_v[2 * q], tiles_v[2 * q + 1]))
        value = halves(value[0:64], value[64:128]).astype(BF)
        for v in range(4):
            near_out[v, q] = value[16 * v : 16 * v + 16]
    for n, peer in enumerate(vec_peers):
        send(near_out.at[peer], near_in.at[x], 9, 9, d, peer)
    near_in[x] = near_out[x]

    far_in_s.wait()
    lc_in.wait()
    wait_for(coeffs.at[0:8, 0], recv_sem.at[2])
    wait_for(coeffs.at[16:24, 0], recv_sem.at[3])
    for p in list(range(8)) + list(range(16, 24)):
        coeffs[p, 1] = turned(coeffs[p, 0])
    for j in range(8):
        source = rows(*[chosen(coeffs, far_s, 6, 2 * j + e) for e in range(2)])
        value = nt(source, rows(lc_v[:, 768 * j : 768 * j + 384], lc_v[:, 768 * j + 384 : 768 * j + 768]))
        far_out[j] = halves(value[0:16], value[16:32])

    uc_in.wait()
    weights = []
    for o in range(2):
        pair = uc_v[:, 128 * o : 128 * o + 128]
        swapped = turned(pair)
        weights += [halves(pair, swapped), halves(swapped, pair)]
    weights = lanes(*weights)
    wait_for(nodes.at[0:9], recv_sem.at[6])
    wait_for(nodes.at[0:9], recv_sem.at[7])
    wait_for(nodes.at[0:5], recv_sem.at[8])
    nodes[30 + ((y + 7) & 7)] = nodes[PREV + 8]
    nodes[30 + ((y + 1) & 7)] = nodes[NEXT + 8]
    for m in range(4):
        left_m, right_m = dup[30 + 2 * m], dup[31 + 2 * m]
        value = nn(lanes(nodes[30 + 2 * m], nodes[31 + 2 * m]), rows(left_m, left_m, right_m, right_m))
        nodes[38 + m] = hilo(value)
    sources = []
    for u in range(6):
        g = d >> u
        odd = g & 1
        number = LEAF_COUNT >> u
        parts = []
        for o, wanted in ((-3, odd == 1), (-2, None), (2, None), (3, odd == 0)):
            if u < 4:
                shift = o if wanted is None else (-3 * odd if o < 0 else 3 * (1 - odd))
                count = ROW >> u
                place = (i >> u) + shift
                place = jnp.where(
                    place < 0,
                    PREV + 2 + 2 * u + place,
                    jnp.where(place < count, BASES[u] + place, NEXT + 2 * u - count + place),
                )
            else:
                place = (30, 38)[u - 4] + ((g + o + number) & (number - 1))
            valid = (g + o >= 0) if o < 0 else (g + o < number)
            if wanted is not None:
                valid = jnp.logical_and(valid, wanted)
            keep = jnp.where(valid, 1.0, 0.0).astype(F32)
            parts.append((nodes[place].astype(F32) * keep).astype(BF))
        sources.append(lanes(*parts))
    coupled = nt(rows(*sources), rows(weights, weights))
    left_side, right_side = [], []
    for u in range(1, 6):
        tile = hilo(coupled[16 * u : 16 * u + 16])
        left_side.append(tile)
        right_side.append(path_hi[u - 1])
        if u > 1:
            left_side.append(tile)
            right_side.append(path_lo[u - 1])
    matrix = lanes(*right_side)
    down = coupled[0:16] + nt(lanes(*left_side), rows(matrix, matrix))
    down = hilo(down)
    down = lanes(down, down)

    wait_for(near_in.at[0:3], recv_sem.at[9])
    for j in range(8):
        local = nt(down, lanes(r0_hi[j], r0_lo[j]))
        leaf_down = (local + far_out[j]).astype(BF)
        block = basis_v[:, 128 * j : 128 * j + 128]
        none = jnp.zeros_like(block)
        value = nn(leaf_down, rows(halves(block, none), halves(none, block)))
        out_ref[:, 128 * j : 128 * j + 128] = (value + near_in[j // 2, j % 2].astype(F32)).astype(BF)

    wait_for(points.at[8:16, 0, 0:48], send_sem.at[0])
    wait_for(nodes.at[0:15], send_sem.at[1])
    wait_for(coeffs.at[0:8, 0], send_sem.at[2])
    wait_for(coeffs.at[0:8, 0], send_sem.at[3])
    wait_for(points.at[0:8, 0], send_sem.at[4])
    wait_for(points.at[0:8, 0], send_sem.at[5])
    wait_for(nodes.at[0:9], send_sem.at[6])
    wait_for(nodes.at[0:9], send_sem.at[7])
    wait_for(nodes.at[0:5], send_sem.at[8])
    wait_for(near_out.at[0:3], send_sem.at[9])


def shards(vectors, leaf_basis, local_transfer, upper_transfer, upper_coupling, leaf_coupling, far_list, near_list, near_tiles):
    tile = (16, 128)
    scratch = [
        pltpu.VMEM(vectors.shape, BF),
        pltpu.VMEM(leaf_basis.shape, BF),
        pltpu.VMEM(local_transfer.shape, BF),
        pltpu.VMEM((64, 2432), BF),
        pltpu.VMEM(upper_coupling.shape, BF),
        pltpu.VMEM(leaf_coupling.shape, BF),
        pltpu.SMEM(far_list.shape, jnp.int32),
        pltpu.SMEM(near_list.shape, jnp.int32),
        pltpu.VMEM(near_tiles.shape, BF),
        pltpu.VMEM((24, 2, 64, 128), BF),
        pltpu.VMEM((24, 2) + tile, BF),
        pltpu.VMEM((60,) + tile, BF),
        pltpu.VMEM((9,) + tile, BF),
        pltpu.VMEM((9,) + tile, BF),
        pltpu.VMEM((38, 64, 128), BF),
        pltpu.VMEM((5, 64, 128), BF),
        pltpu.VMEM((5, 64, 128), BF),
        pltpu.VMEM((8, 128, 128), BF),
        pltpu.VMEM((8, 128, 128), BF),
        pltpu.VMEM((8,) + tile, F32),
        pltpu.VMEM((4, 2) + tile, BF),
        pltpu.VMEM((4, 2) + tile, BF),
        pltpu.SemaphoreType.DMA((13,)),
        pltpu.SemaphoreType.DMA((10,)),
        pltpu.SemaphoreType.DMA((10,)),
    ]
    return pl.pallas_call(
        kernel,
        out_shape=pltpu.VMEM(vectors.shape, BF),
        in_specs=[pl.BlockSpec(memory_space=pl.ANY)] * 9,
        out_specs=pl.BlockSpec(memory_space=pltpu.VMEM),
        scratch_shapes=scratch,
        compiler_params=pltpu.CompilerParams(
            collective_id=0, has_side_effects=True, vmem_limit_bytes=62 * 1024 * 1024
        ),
    )(vectors, leaf_basis, local_transfer, upper_transfer, upper_coupling, leaf_coupling, far_list, near_list, near_tiles)


def solution(mesh):
    placed = (
        P("vec", "leaf"),
        P(None, "leaf"),
        P(None, "leaf"),
        P(),
        P(),
        P(None, "leaf"),
        P(None, "leaf"),
        P(None, "leaf"),
        P(("leaf", "vec"), None, None),
    )
    return jax.shard_map(
        shards, mesh=mesh, in_specs=placed, out_specs=P("vec", "leaf"), check_vma=False
    )
```

```python
import jax
import jax.numpy as jnp
from jax import lax
from jax.experimental import pallas as pl
from jax.experimental.pallas import tpu as pltpu
from jax.sharding import PartitionSpec as P

MESH = pl.DeviceIdType.MESH
BF = jnp.bfloat16
F32 = jnp.float32
ROW = 16
ROWS = 8
LEAF_COUNT = ROW * ROWS
BASES = (0, 16, 24, 28, 30)
PREV = 42
NEXT = 51
FAR_ORDER = (8, 9, 7, 10, 6, 11, 5, 12, 4, 13, 3, 14, 2, 15, 1)


def low(shape):
    return lax.broadcasted_iota(jnp.int32, shape, 1) < 64


def halves(a, b):
    return jnp.where(low(a.shape), a, b)


def turned(tile):
    return pltpu.roll(tile.astype(F32), 64, 1).astype(tile.dtype)


def rounded(x):
    return x.astype(BF).astype(F32)


def hilo(x):
    hi = rounded(x)
    return halves(hi, x - hi).astype(BF)


def two_terms(x):
    hi = rounded(x)
    return hi.astype(BF), (x - hi).astype(BF)


def nn(a, b):
    return jnp.dot(a, b, preferred_element_type=F32)


def nt(a, b):
    return lax.dot_general(a, b, (((1,), (1,)), ((), ())), preferred_element_type=F32)


def rows(*parts):
    return jnp.concatenate(parts, axis=0)


def lanes(*parts):
    return jnp.concatenate(parts, axis=1)


def kernel(
    vec_h, basis_h, lt_h, ut_h, uc_h, lc_h, far_h, near_h, tiles_h, out_ref,
    vec_v, basis_v, lt_v, ut_v, uc_v, lc_v, far_s, near_s, tiles_v,
    points, coeffs, nodes, heads, tails,
    dup, path_hi, path_lo, r0_hi, r0_lo, far_out, near_out, near_in,
    in_sem, send_sem, recv_sem,
):
    d = lax.axis_index("leaf")
    x = lax.axis_index("vec")
    y = d >> 4
    i = d & 15

    right = (d + 1) & (LEAF_COUNT - 1)
    left = (d + LEAF_COUNT - 1) & (LEAF_COUNT - 1)
    row_peers = [ROW * y + ((i + k) & (ROW - 1)) for k in FAR_ORDER]
    column_peers = [(d + ROW * k) & (LEAF_COUNT - 1) for k in (4, 3, 5, 2, 1, 6, 7)]
    vec_peers = [(x + k) & 3 for k in (2, 1, 3)]

    barrier = pltpu.get_barrier_semaphore()
    for peer in row_peers + column_peers + [right, left]:
        pl.semaphore_signal(barrier, inc=1, device_id={"leaf": peer, "vec": x}, device_id_type=MESH)
    for peer in vec_peers:
        pl.semaphore_signal(barrier, inc=1, device_id={"leaf": d, "vec": peer}, device_id_type=MESH)

    def load(src, dst, n):
        copy = pltpu.make_async_copy(src, dst, in_sem.at[n])
        copy.start()
        return copy

    vec_in = load(vec_h, vec_v, 0)
    basis_in = load(basis_h, basis_v, 1)
    lt_in = load(lt_h, lt_v, 2)
    ut_in = [
        load(ut_h.at[:, pl.ds(pl.multiple_of(1024 * y, 128), 1024)], ut_v.at[:, 0:1024], 3),
        load(ut_h.at[:, pl.ds(pl.multiple_of(8192 + 512 * y, 128), 512)], ut_v.at[:, 1024:1536], 4),
        load(ut_h.at[:, pl.ds(pl.multiple_of(12288 + 256 * y, 128), 256)], ut_v.at[:, 1536:1792], 5),
        load(ut_h.at[:, pl.ds(pl.multiple_of(14336 + 128 * y, 128), 128)], ut_v.at[:, 1792:1920], 6),
        load(ut_h.at[:, 15360:15872], ut_v.at[:, 1920:2432], 7),
    ]
    def send(src, dst, n_send, n_recv, leaf, vec):
        copy = pltpu.make_async_remote_copy(
            src_ref=src, dst_ref=dst, send_sem=send_sem.at[n_send], recv_sem=recv_sem.at[n_recv],
            device_id={"leaf": leaf, "vec": vec}, device_id_type=MESH,
        )
        copy.start()
        return copy

    def wait_for(ref, sem):
        pltpu.make_async_copy(ref, ref, sem).wait()

    own = pl.ds(pl.multiple_of(16 * x, 16), 16)
    vec_in.wait()
    for j in range(8):
        points[8 + j, 0, own, :] = vec_v[:, 128 * j : 128 * j + 128]

    basis_in.wait()
    lt_in.wait()
    transfer = lt_v[:, 1792:1920]
    crossed = turned(transfer)
    top = (halves(transfer, crossed), halves(crossed, transfer))

    zero = jnp.zeros((16, 128), BF)
    leaves = []
    for j in range(8):
        tile = vec_v[:, 128 * j : 128 * j + 128]
        block = basis_v[:, 128 * j : 128 * j + 128]
        leaves.append(nt(rows(halves(tile, zero), halves(zero, tile)), rows(block, block)))
    current = []
    for j in range(8):
        coeff = leaves[j]
        first, second = coeff[0:16], coeff[16:32]
        coeffs[8 + j, 0] = halves(first, second).astype(BF)
        coeffs[8 + j, 1] = halves(second, first).astype(BF)
        transfer = lt_v[:, 128 * j : 128 * j + 128]
        lifted = nn(hilo(coeff), rows(transfer, transfer))
        current.append(halves(lifted[0:16], lifted[16:32]))
    for start in (1024, 1536):
        following = []
        for m in range(len(current) // 2):
            hi, lo = two_terms(rows(current[2 * m], current[2 * m + 1]))
            transfer = lt_v[:, start + 128 * m : start + 128 * m + 128]
            lifted = nn(lanes(hi, lo), rows(transfer, transfer, transfer, transfer))
            following.append(halves(lifted[0:16], lifted[16:32]))
        current = following
    first_hi, first_lo = two_terms(current[0])
    second_hi, second_lo = two_terms(current[1])
    root = nn(lanes(first_hi, first_lo, second_hi, second_lo), rows(*([top[0]] * 4 + [top[1]] * 4)))
    nodes[i] = hilo(root)
    pl.semaphore_wait(barrier, 27)
    for peer in row_peers:
        send(nodes.at[i], nodes.at[i], 1, 1, peer, x)
    for peer in vec_peers:
        send(points.at[8:16, 0, own], points.at[8:16, 0, own], 0, 0, d, peer)
    uc_in = load(uc_h, uc_v, 8)
    lc_in = load(lc_h, lc_v, 9)
    far_in_s = load(far_h, far_s, 10)
    near_in_s = load(near_h, near_s, 11)
    tiles_in = load(tiles_h, tiles_v, 12)

    send(coeffs.at[8:16, 0], coeffs.at[0:8, 0], 2, 2, right, x)
    send(coeffs.at[8:16, 0], coeffs.at[16:24, 0], 3, 3, left, x)
    wait_for(points.at[8:16, 0, 0:48], recv_sem.at[0])
    send(points.at[8:16, 0], points.at[0:8, 0], 4, 4, right, x)
    send(points.at[8:16, 0], points.at[16:24, 0], 5, 5, left, x)

    for copy in ut_in:
        copy.wait()
    for p in range(19):
        pair = ut_v[:, 128 * p : 128 * p + 128]
        swapped = turned(pair)
        dup[2 * p] = halves(pair, swapped)
        dup[2 * p + 1] = halves(swapped, pair)

    path = dup[i]
    path_hi[0] = path
    path = path.astype(F32)
    below = [(top[0], None), (top[1], None)]

    def path_step(path, u):
        matrix = dup[BASES[u] + (i >> u if u < 4 else y)]
        path = nn(hilo(path), rows(matrix, matrix))
        path_hi[u], path_lo[u] = two_terms(path)
        return path

    def product_step(below, start):
        following = []
        for m, (hi, lo) in enumerate(below):
            pair = lt_v[:, start + 128 * m : start + 128 * m + 128]
            none = jnp.zeros_like(pair)
            left_side = rows(halves(pair, none), halves(none, pair))
            if lo is None:
                product = nn(left_side, rows(hi, hi))
            else:
                product = nn(lanes(left_side, left_side), rows(hi, hi, lo, lo))
            hi, lo = two_terms(product)
            if start == 0:
                r0_hi[m] = hi
                r0_lo[m] = lo
            following += [(hi[0:64], lo[0:64]), (hi[64:128], lo[64:128])]
        return following

    for u, start in ((1, 1536), (2, 1024), (3, 0)):
        path = path_step(path, u)
        below = product_step(below, start)
    path_step(path, 4)

    wait_for(nodes.at[0:15], recv_sem.at[1])
    for u in range(4):
        base, count = BASES[u], ROW >> u
        for m in range(count // 2):
            left_m, right_m = dup[base + 2 * m], dup[base + 2 * m + 1]
            value = nn(lanes(nodes[base + 2 * m], nodes[base + 2 * m + 1]), rows(left_m, left_m, right_m, right_m))
            if u < 3:
                nodes[BASES[u + 1] + m] = hilo(value)
            else:
                top_tile = hilo(value)
                nodes[30 + y] = top_tile
                heads[8] = top_tile
                tails[8] = top_tile
    for u in range(4):
        for e in range(2):
            heads[2 * u + e] = nodes[BASES[u] + e]
            tails[2 * u + e] = nodes[BASES[u + 1] - 2 + e]
    send(tails, nodes.at[PREV : PREV + 9], 6, 6, column_peers[4], x)
    send(heads, nodes.at[NEXT : NEXT + 9], 7, 7, column_peers[6], x)
    for peer in column_peers[:4] + column_peers[5:6]:
        send(nodes.at[30 + y], nodes.at[30 + y], 8, 8, peer, x)

    near_in_s.wait()
    tiles_in.wait()
    wait_for(points.at[0:8, 0], recv_sem.at[4])
    wait_for(points.at[16:24, 0], recv_sem.at[5])
    for p in range(24):
        points[p, 1] = turned(points[p, 0])
    first_leaf = ROW * d - ROW

    def chosen(table, lists, slots, column):
        parts = []
        for s in range(0, slots, 2):
            a = jnp.clip(lists[s, column] - first_leaf, 0, 3 * ROW - 1)
            b = jnp.clip(lists[s + 1, column] - first_leaf, 0, 3 * ROW - 1)
            parts.append(halves(table[a >> 1, a & 1], table[b >> 1, 1 - (b & 1)]))
        return lanes(*parts)

    for q in range(2):
        source = rows(*[chosen(points, near_s, 6, 4 * x + 2 * q + e) for e in range(2)])
        value = nt(source, rows(tiles_v[2 * q], tiles_v[2 * q + 1]))
        value = halves(value[0:64], value[64:128]).astype(BF)
        for v in range(4):
            near_out[v, q] = value[16 * v : 16 * v + 16]
    for n, peer in enumerate(vec_peers):
        send(near_out.at[peer], near_in.at[x], 9, 9, d, peer)
    near_in[x] = near_out[x]

    far_in_s.wait()
    lc_in.wait()
    wait_for(coeffs.at[0:8, 0], recv_sem.at[2])
    wait_for(coeffs.at[16:24, 0], recv_sem.at[3])
    for p in list(range(8)) + list(range(16, 24)):
        coeffs[p, 1] = turned(coeffs[p, 0])
    for j in range(8):
        source = rows(*[chosen(coeffs, far_s, 6, 2 * j + e) for e in range(2)])
        value = nt(source, rows(lc_v[:, 768 * j : 768 * j + 384], lc_v[:, 768 * j + 384 : 768 * j + 768]))
        far_out[j] = halves(value[0:16], value[16:32])

    uc_in.wait()
    weights = []
    for o in range(2):
        pair = uc_v[:, 128 * o : 128 * o + 128]
        swapped = turned(pair)
        weights += [halves(pair, swapped), halves(swapped, pair)]
    weights = lanes(*weights)
    wait_for(nodes.at[0:9], recv_sem.at[6])
    wait_for(nodes.at[0:9], recv_sem.at[7])
    wait_for(nodes.at[0:5], recv_sem.at[8])
    nodes[30 + ((y + 7) & 7)] = nodes[PREV + 8]
    nodes[30 + ((y + 1) & 7)] = nodes[NEXT + 8]
    for m in range(4):
        left_m, right_m = dup[30 + 2 * m], dup[31 + 2 * m]
        value = nn(lanes(nodes[30 + 2 * m], nodes[31 + 2 * m]), rows(left_m, left_m, right_m, right_m))
        nodes[38 + m] = hilo(value)
    sources = []
    for u in range(6):
        g = d >> u
        odd = g & 1
        number = LEAF_COUNT >> u
        parts = []
        for o, wanted in ((-3, odd == 1), (-2, None), (2, None), (3, odd == 0)):
            if u < 4:
                shift = o if wanted is None else (-3 * odd if o < 0 else 3 * (1 - odd))
                count = ROW >> u
                place = (i >> u) + shift
                place = jnp.where(
                    place < 0,
                    PREV + 2 + 2 * u + place,
                    jnp.where(place < count, BASES[u] + place, NEXT + 2 * u - count + place),
                )
            else:
                place = (30, 38)[u - 4] + ((g + o + number) & (number - 1))
            valid = (g + o >= 0) if o < 0 else (g + o < number)
            if wanted is not None:
                valid = jnp.logical_and(valid, wanted)
            keep = jnp.where(valid, 1.0, 0.0).astype(F32)
            parts.append((nodes[place].astype(F32) * keep).astype(BF))
        sources.append(lanes(*parts))
    coupled = nt(rows(*sources), rows(weights, weights))
    left_side, right_side = [], []
    for u in range(1, 6):
        tile = hilo(coupled[16 * u : 16 * u + 16])
        left_side.append(tile)
        right_side.append(path_hi[u - 1])
        if u > 1:
            left_side.append(tile)
            right_side.append(path_lo[u - 1])
    matrix = lanes(*right_side)
    down = coupled[0:16] + nt(lanes(*left_side), rows(matrix, matrix))
    down = hilo(down)
    down = lanes(down, down)

    wait_for(near_in.at[0:3], recv_sem.at[9])
    for j in range(8):
        local = nt(down, lanes(r0_hi[j], r0_lo[j]))
        leaf_down = (local + far_out[j]).astype(BF)
        block = basis_v[:, 128 * j : 128 * j + 128]
        none = jnp.zeros_like(block)
        value = nn(leaf_down, rows(halves(block, none), halves(none, block)))
        out_ref[:, 128 * j : 128 * j + 128] = (value + near_in[j // 2, j % 2].astype(F32)).astype(BF)

    wait_for(points.at[8:16, 0, 0:48], send_sem.at[0])
    wait_for(nodes.at[0:15], send_sem.at[1])
    wait_for(coeffs.at[0:8, 0], send_sem.at[2])
    wait_for(coeffs.at[0:8, 0], send_sem.at[3])
    wait_for(points.at[0:8, 0], send_sem.at[4])
    wait_for(points.at[0:8, 0], send_sem.at[5])
    wait_for(nodes.at[0:9], send_sem.at[6])
    wait_for(nodes.at[0:9], send_sem.at[7])
    wait_for(nodes.at[0:5], send_sem.at[8])
    wait_for(near_out.at[0:3], send_sem.at[9])


def shards(vectors, leaf_basis, local_transfer, upper_transfer, upper_coupling, leaf_coupling, far_list, near_list, near_tiles):
    tile = (16, 128)
    scratch = [
        pltpu.VMEM(vectors.shape, BF),
        pltpu.VMEM(leaf_basis.shape, BF),
        pltpu.VMEM(local_transfer.shape, BF),
        pltpu.VMEM((64, 2432), BF),
        pltpu.VMEM(upper_coupling.shape, BF),
        pltpu.VMEM(leaf_coupling.shape, BF),
        pltpu.SMEM(far_list.shape, jnp.int32),
        pltpu.SMEM(near_list.shape, jnp.int32),
        pltpu.VMEM(near_tiles.shape, BF),
        pltpu.VMEM((24, 2, 64, 128), BF),
        pltpu.VMEM((24, 2) + tile, BF),
        pltpu.VMEM((60,) + tile, BF),
        pltpu.VMEM((9,) + tile, BF),
        pltpu.VMEM((9,) + tile, BF),
        pltpu.VMEM((38, 64, 128), BF),
        pltpu.VMEM((5, 64, 128), BF),
        pltpu.VMEM((5, 64, 128), BF),
        pltpu.VMEM((8, 128, 128), BF),
        pltpu.VMEM((8, 128, 128), BF),
        pltpu.VMEM((8,) + tile, F32),
        pltpu.VMEM((4, 2) + tile, BF),
        pltpu.VMEM((4, 2) + tile, BF),
        pltpu.SemaphoreType.DMA((13,)),
        pltpu.SemaphoreType.DMA((10,)),
        pltpu.SemaphoreType.DMA((10,)),
    ]
    return pl.pallas_call(
        kernel,
        out_shape=pltpu.VMEM(vectors.shape, BF),
        in_specs=[pl.BlockSpec(memory_space=pl.ANY)] * 9,
        out_specs=pl.BlockSpec(memory_space=pltpu.VMEM),
        scratch_shapes=scratch,
        compiler_params=pltpu.CompilerParams(
            collective_id=0, has_side_effects=True, vmem_limit_bytes=62 * 1024 * 1024
        ),
    )(vectors, leaf_basis, local_transfer, upper_transfer, upper_coupling, leaf_coupling, far_list, near_list, near_tiles)


def solution(mesh):
    placed = (
        P("vec", "leaf"),
        P(None, "leaf"),
        P(None, "leaf"),
        P(),
        P(),
        P(None, "leaf"),
        P(None, "leaf"),
        P(None, "leaf"),
        P(("leaf", "vec"), None, None),
    )
    return jax.shard_map(
        shards, mesh=mesh, in_specs=placed, out_specs=P("vec", "leaf"), check_vma=False
    )
```

```python
import jax
import jax.numpy as jnp
from jax import lax
from jax.experimental import pallas as pl
from jax.experimental.pallas import tpu as pltpu
from jax.sharding import PartitionSpec as P

MESH = pl.DeviceIdType.MESH
BF = jnp.bfloat16
F32 = jnp.float32
ROW = 16
ROWS = 8
LEAF_COUNT = ROW * ROWS
BASES = (0, 16, 24, 28, 30)
PREV = 42
NEXT = 51


def low(shape):
    return lax.broadcasted_iota(jnp.int32, shape, 1) < 64


def halves(a, b):
    return jnp.where(low(a.shape), a, b)


def turned(tile):
    return pltpu.roll(tile.astype(F32), 64, 1).astype(tile.dtype)


def rounded(x):
    return x.astype(BF).astype(F32)


def hilo(x):
    hi = rounded(x)
    return halves(hi, x - hi).astype(BF)


def two_terms(x):
    hi = rounded(x)
    return hi.astype(BF), (x - hi).astype(BF)


def nn(a, b):
    return jnp.dot(a, b, preferred_element_type=F32)


def nt(a, b):
    return lax.dot_general(a, b, (((1,), (1,)), ((), ())), preferred_element_type=F32)


def rows(*parts):
    return jnp.concatenate(parts, axis=0)


def lanes(*parts):
    return jnp.concatenate(parts, axis=1)


def kernel(
    vec_h, basis_h, lt_h, ut_h, uc_h, lc_h, far_h, near_h, tiles_h, out_ref,
    vec_v, basis_v, lt_v, ut_v, uc_v, lc_v, far_s, near_s, tiles_v,
    points, coeffs, root_tile, nodes, heads, tails,
    dup, path_hi, path_lo, r0_hi, r0_lo, far_out, near_out, near_in,
    in_sem, send_sem, recv_sem, flag_0, flag_1,
):
    d = lax.axis_index("leaf")
    x = lax.axis_index("vec")
    y = d >> 4
    i = d & 15
    z = i >> 1
    c = i & 1

    def load(src, dst, n):
        copy = pltpu.make_async_copy(src, dst, in_sem.at[n])
        copy.start()
        return copy

    vec_in = load(vec_h, vec_v, 0)
    basis_in = load(basis_h, basis_v, 1)
    lt_in = load(lt_h, lt_v, 2)

    right = (d + 1) & (LEAF_COUNT - 1)
    left = (d + LEAF_COUNT - 1) & (LEAF_COUNT - 1)
    sibling = d + 1 - 2 * c
    column_peers = [(d + ROW * k) & (LEAF_COUNT - 1) for k in (4, 3, 5, 2, 1, 6, 7)]
    vec_peers = [(x + k) & 3 for k in (2, 1, 3)]

    barrier = pltpu.get_barrier_semaphore()

    def announce(leaf, vec):
        pl.semaphore_signal(barrier, inc=1, device_id={"leaf": leaf, "vec": vec}, device_id_type=MESH)

    @pl.when(z < 4)
    def _():
        for k in range(1, 8):
            announce(ROW * y + 2 * ((z + k) & 7), x)

    announce(sibling, x)
    announce((d + LEAF_COUNT - 2 + 4 * c) & (LEAF_COUNT - 1), x)
    for peer in vec_peers:
        announce(d - c, peer)
    for peer in column_peers:
        announce(peer - c + 1, x)

    def tell(flag):
        pl.semaphore_signal(flag, inc=1, device_id={"leaf": sibling, "vec": x}, device_id_type=MESH)

    ut_in = [
        load(ut_h.at[:, pl.ds(pl.multiple_of(1024 * y, 128), 1024)], ut_v.at[:, 0:1024], 3),
        load(ut_h.at[:, pl.ds(pl.multiple_of(8192 + 512 * y, 128), 512)], ut_v.at[:, 1024:1536], 4),
        load(ut_h.at[:, pl.ds(pl.multiple_of(12288 + 256 * y, 128), 256)], ut_v.at[:, 1536:1792], 5),
        load(ut_h.at[:, pl.ds(pl.multiple_of(14336 + 128 * y, 128), 128)], ut_v.at[:, 1792:1920], 6),
        load(ut_h.at[:, 15360:15872], ut_v.at[:, 1920:2432], 7),
    ]

    def send(src, dst, n_send, n_recv, leaf, vec):
        copy = pltpu.make_async_remote_copy(
            src_ref=src, dst_ref=dst, send_sem=send_sem.at[n_send], recv_sem=recv_sem.at[n_recv],
            device_id={"leaf": leaf, "vec": vec}, device_id_type=MESH,
        )
        copy.start()
        return copy

    def wait_for(ref, sem):
        pltpu.make_async_copy(ref, ref, sem).wait()

    own = pl.ds(pl.multiple_of(16 * x, 16), 16)
    vec_in.wait()
    for j in range(8):
        points[8 + j, 0, own, :] = vec_v[:, 128 * j : 128 * j + 128]

    basis_in.wait()
    lt_in.wait()
    transfer = lt_v[:, 1792:1920]
    crossed = turned(transfer)
    top = (halves(transfer, crossed), halves(crossed, transfer))

    zero = jnp.zeros((16, 128), BF)
    leaves = []
    for j in range(8):
        tile = vec_v[:, 128 * j : 128 * j + 128]
        block = basis_v[:, 128 * j : 128 * j + 128]
        leaves.append(nt(rows(halves(tile, zero), halves(zero, tile)), rows(block, block)))
    current = []
    for j in range(8):
        coeff = leaves[j]
        first, second = coeff[0:16], coeff[16:32]
        coeffs[8 + j, 0] = halves(first, second).astype(BF)
        coeffs[8 + j, 1] = halves(second, first).astype(BF)
        transfer = lt_v[:, 128 * j : 128 * j + 128]
        lifted = nn(hilo(coeff), rows(transfer, transfer))
        current.append(halves(lifted[0:16], lifted[16:32]))
    for start in (1024, 1536):
        following = []
        for m in range(len(current) // 2):
            hi, lo = two_terms(rows(current[2 * m], current[2 * m + 1]))
            transfer = lt_v[:, start + 128 * m : start + 128 * m + 128]
            lifted = nn(lanes(hi, lo), rows(transfer, transfer, transfer, transfer))
            following.append(halves(lifted[0:16], lifted[16:32]))
        current = following
    first_hi, first_lo = two_terms(current[0])
    second_hi, second_lo = two_terms(current[1])
    root = nn(lanes(first_hi, first_lo, second_hi, second_lo), rows(*([top[0]] * 4 + [top[1]] * 4)))
    root_tile[...] = hilo(root)

    @pl.when(z < 4)
    def _():
        nodes[i] = root_tile[...]

    @pl.when(c == 0)
    def _():
        pl.semaphore_wait(barrier, 14 + 2 * (z >> 2))
        tell(flag_0)

    @pl.when(c == 1)
    def _():
        pl.semaphore_wait(flag_0, 1)

    for k in (1, 2, 3, 4, 5, 6, 7):
        send(root_tile, nodes.at[i], 1, 1, ROW * y + ((i + k) & 7), x)

    @pl.when(z >= 4)
    def _():
        send(root_tile, nodes.at[i], 11, 1, ROW * y + (i & 7), x)

    for peer in vec_peers:
        send(points.at[8:16, 0, own], points.at[8:16, 0, own], 0, 0, d, peer)
    send(coeffs.at[8:16, 0], coeffs.at[0:8, 0], 2, 2, right, x)
    uc_in = load(uc_h, uc_v, 8)
    lc_in = load(lc_h, lc_v, 9)
    far_in_s = load(far_h, far_s, 10)
    near_in_s = load(near_h, near_s, 11)
    tiles_in = load(tiles_h, tiles_v, 12)

    for copy in ut_in:
        copy.wait()
    for p in range(19):
        pair = ut_v[:, 128 * p : 128 * p + 128]
        swapped = turned(pair)
        dup[2 * p] = halves(pair, swapped)
        dup[2 * p + 1] = halves(swapped, pair)

    path = dup[i]
    path_hi[0] = path
    path = path.astype(F32)
    below = [(top[0], None), (top[1], None)]

    def path_step(path, u):
        matrix = dup[BASES[u] + (i >> u if u < 4 else y)]
        path = nn(hilo(path), rows(matrix, matrix))
        path_hi[u], path_lo[u] = two_terms(path)
        return path

    def product_step(below, start):
        following = []
        for m, (hi, lo) in enumerate(below):
            pair = lt_v[:, start + 128 * m : start + 128 * m + 128]
            none = jnp.zeros_like(pair)
            left_side = rows(halves(pair, none), halves(none, pair))
            if lo is None:
                product = nn(left_side, rows(hi, hi))
            else:
                product = nn(lanes(left_side, left_side), rows(hi, hi, lo, lo))
            hi, lo = two_terms(product)
            if start == 0:
                r0_hi[m] = hi
                r0_lo[m] = lo
            following += [(hi[0:64], lo[0:64]), (hi[64:128], lo[64:128])]
        return following

    for u, start in ((1, 1536), (2, 1024), (3, 0)):
        path = path_step(path, u)
        below = product_step(below, start)
    path_step(path, 4)

    wait_for(points.at[8:16, 0, 0:48], recv_sem.at[0])
    send(points.at[8:16, 0], points.at[0:8, 0], 4, 4, right, x)

    @pl.when(c == 1)
    def _():
        pl.semaphore_wait(barrier, 16)
        tell(flag_1)

    @pl.when(c == 0)
    def _():
        pl.semaphore_wait(flag_1, 1)

    send(coeffs.at[8:16, 0], coeffs.at[16:24, 0], 3, 3, left, x)
    send(points.at[8:16, 0], points.at[16:24, 0], 5, 5, left, x)

    @pl.when(z < 4)
    def _():
        wait_for(nodes.at[0:15], recv_sem.at[1])
        send(nodes.at[0:ROW], nodes.at[0:ROW], 10, 10, ROW * y + 14 - i + 2 * c, x)

    @pl.when(z >= 4)
    def _():
        wait_for(nodes.at[0:ROW], recv_sem.at[10])

    for u in range(4):
        base, count = BASES[u], ROW >> u
        for m in range(count // 2):
            left_m, right_m = dup[base + 2 * m], dup[base + 2 * m + 1]
            value = nn(lanes(nodes[base + 2 * m], nodes[base + 2 * m + 1]), rows(left_m, left_m, right_m, right_m))
            if u < 3:
                nodes[BASES[u + 1] + m] = hilo(value)
            else:
                top_tile = hilo(value)
                nodes[30 + y] = top_tile
                heads[8] = top_tile
                tails[8] = top_tile
    for u in range(4):
        for e in range(2):
            heads[2 * u + e] = nodes[BASES[u] + e]
            tails[2 * u + e] = nodes[BASES[u + 1] - 2 + e]
    send(tails, nodes.at[PREV : PREV + 9], 6, 6, column_peers[4], x)
    send(heads, nodes.at[NEXT : NEXT + 9], 7, 7, column_peers[6], x)
    for peer in column_peers[:4] + column_peers[5:6]:
        send(nodes.at[30 + y], nodes.at[30 + y], 8, 8, peer, x)

    near_in_s.wait()
    tiles_in.wait()
    wait_for(points.at[0:8, 0], recv_sem.at[4])
    wait_for(points.at[16:24, 0], recv_sem.at[5])
    for p in range(24):
        points[p, 1] = turned(points[p, 0])
    first_leaf = ROW * d - ROW

    def chosen(table, lists, slots, column):
        parts = []
        for s in range(0, slots, 2):
            a = jnp.clip(lists[s, column] - first_leaf, 0, 3 * ROW - 1)
            b = jnp.clip(lists[s + 1, column] - first_leaf, 0, 3 * ROW - 1)
            parts.append(halves(table[a >> 1, a & 1], table[b >> 1, 1 - (b & 1)]))
        return lanes(*parts)

    for q in range(2):
        source = rows(*[chosen(points, near_s, 6, 4 * x + 2 * q + e) for e in range(2)])
        value = nt(source, rows(tiles_v[2 * q], tiles_v[2 * q + 1]))
        value = halves(value[0:64], value[64:128]).astype(BF)
        for v in range(4):
            near_out[v, q] = value[16 * v : 16 * v + 16]
    for n, peer in enumerate(vec_peers):
        send(near_out.at[peer], near_in.at[x], 9, 9, d, peer)
    near_in[x] = near_out[x]

    far_in_s.wait()
    lc_in.wait()
    wait_for(coeffs.at[0:8, 0], recv_sem.at[2])
    wait_for(coeffs.at[16:24, 0], recv_sem.at[3])
    for p in list(range(8)) + list(range(16, 24)):
        coeffs[p, 1] = turned(coeffs[p, 0])
    for j in range(8):
        source = rows(*[chosen(coeffs, far_s, 6, 2 * j + e) for e in range(2)])
        value = nt(source, rows(lc_v[:, 768 * j : 768 * j + 384], lc_v[:, 768 * j + 384 : 768 * j + 768]))
        far_out[j] = halves(value[0:16], value[16:32])

    uc_in.wait()
    weights = []
    for o in range(2):
        pair = uc_v[:, 128 * o : 128 * o + 128]
        swapped = turned(pair)
        weights += [halves(pair, swapped), halves(swapped, pair)]
    weights = lanes(*weights)
    wait_for(nodes.at[0:9], recv_sem.at[6])
    wait_for(nodes.at[0:9], recv_sem.at[7])
    wait_for(nodes.at[0:5], recv_sem.at[8])
    nodes[30 + ((y + 7) & 7)] = nodes[PREV + 8]
    nodes[30 + ((y + 1) & 7)] = nodes[NEXT + 8]
    for m in range(4):
        left_m, right_m = dup[30 + 2 * m], dup[31 + 2 * m]
        value = nn(lanes(nodes[30 + 2 * m], nodes[31 + 2 * m]), rows(left_m, left_m, right_m, right_m))
        nodes[38 + m] = hilo(value)
    sources = []
    for u in range(6):
        g = d >> u
        odd = g & 1
        number = LEAF_COUNT >> u
        parts = []
        for o, wanted in ((-3, odd == 1), (-2, None), (2, None), (3, odd == 0)):
            if u < 4:
                shift = o if wanted is None else (-3 * odd if o < 0 else 3 * (1 - odd))
                count = ROW >> u
                place = (i >> u) + shift
                place = jnp.where(
                    place < 0,
                    PREV + 2 + 2 * u + place,
                    jnp.where(place < count, BASES[u] + place, NEXT + 2 * u - count + place),
                )
            else:
                place = (30, 38)[u - 4] + ((g + o + number) & (number - 1))
            valid = (g + o >= 0) if o < 0 else (g + o < number)
            if wanted is not None:
                valid = jnp.logical_and(valid, wanted)
            keep = jnp.where(valid, 1.0, 0.0).astype(F32)
            parts.append((nodes[place].astype(F32) * keep).astype(BF))
        sources.append(lanes(*parts))
    coupled = nt(rows(*sources), rows(weights, weights))
    left_side, right_side = [], []
    for u in range(1, 6):
        tile = hilo(coupled[16 * u : 16 * u + 16])
        left_side.append(tile)
        right_side.append(path_hi[u - 1])
        if u > 1:
            left_side.append(tile)
            right_side.append(path_lo[u - 1])
    matrix = lanes(*right_side)
    down = coupled[0:16] + nt(lanes(*left_side), rows(matrix, matrix))
    down = hilo(down)
    down = lanes(down, down)

    wait_for(near_in.at[0:3], recv_sem.at[9])
    for j in range(8):
        local = nt(down, lanes(r0_hi[j], r0_lo[j]))
        leaf_down = (local + far_out[j]).astype(BF)
        block = basis_v[:, 128 * j : 128 * j + 128]
        none = jnp.zeros_like(block)
        value = nn(leaf_down, rows(halves(block, none), halves(none, block)))
        out_ref[:, 128 * j : 128 * j + 128] = (value + near_in[j // 2, j % 2].astype(F32)).astype(BF)

    wait_for(points.at[8:16, 0, 0:48], send_sem.at[0])
    wait_for(nodes.at[0:7], send_sem.at[1])

    @pl.when(z < 4)
    def _():
        wait_for(nodes.at[0:ROW], send_sem.at[10])

    @pl.when(z >= 4)
    def _():
        wait_for(root_tile, send_sem.at[11])

    wait_for(coeffs.at[0:8, 0], send_sem.at[2])
    wait_for(coeffs.at[0:8, 0], send_sem.at[3])
    wait_for(points.at[0:8, 0], send_sem.at[4])
    wait_for(points.at[0:8, 0], send_sem.at[5])
    wait_for(nodes.at[0:9], send_sem.at[6])
    wait_for(nodes.at[0:9], send_sem.at[7])
    wait_for(nodes.at[0:5], send_sem.at[8])
    wait_for(near_out.at[0:3], send_sem.at[9])


def shards(vectors, leaf_basis, local_transfer, upper_transfer, upper_coupling, leaf_coupling, far_list, near_list, near_tiles):
    tile = (16, 128)
    scratch = [
        pltpu.VMEM(vectors.shape, BF),
        pltpu.VMEM(leaf_basis.shape, BF),
        pltpu.VMEM(local_transfer.shape, BF),
        pltpu.VMEM((64, 2432), BF),
        pltpu.VMEM(upper_coupling.shape, BF),
        pltpu.VMEM(leaf_coupling.shape, BF),
        pltpu.SMEM(far_list.shape, jnp.int32),
        pltpu.SMEM(near_list.shape, jnp.int32),
        pltpu.VMEM(near_tiles.shape, BF),
        pltpu.VMEM((24, 2, 64, 128), BF),
        pltpu.VMEM((24, 2) + tile, BF),
        pltpu.VMEM(tile, BF),
        pltpu.VMEM((60,) + tile, BF),
        pltpu.VMEM((9,) + tile, BF),
        pltpu.VMEM((9,) + tile, BF),
        pltpu.VMEM((38, 64, 128), BF),
        pltpu.VMEM((5, 64, 128), BF),
        pltpu.VMEM((5, 64, 128), BF),
        pltpu.VMEM((8, 128, 128), BF),
        pltpu.VMEM((8, 128, 128), BF),
        pltpu.VMEM((8,) + tile, F32),
        pltpu.VMEM((4, 2) + tile, BF),
        pltpu.VMEM((4, 2) + tile, BF),
        pltpu.SemaphoreType.DMA((13,)),
        pltpu.SemaphoreType.DMA((12,)),
        pltpu.SemaphoreType.DMA((12,)),
        pltpu.SemaphoreType.REGULAR,
        pltpu.SemaphoreType.REGULAR,
    ]
    return pl.pallas_call(
        kernel,
        out_shape=pltpu.VMEM(vectors.shape, BF),
        in_specs=[pl.BlockSpec(memory_space=pl.ANY)] * 9,
        out_specs=pl.BlockSpec(memory_space=pltpu.VMEM),
        scratch_shapes=scratch,
        compiler_params=pltpu.CompilerParams(
            collective_id=0, has_side_effects=True, vmem_limit_bytes=62 * 1024 * 1024
        ),
    )(vectors, leaf_basis, local_transfer, upper_transfer, upper_coupling, leaf_coupling, far_list, near_list, near_tiles)


def solution(mesh):
    placed = (
        P("vec", "leaf"),
        P(None, "leaf"),
        P(None, "leaf"),
        P(),
        P(),
        P(None, "leaf"),
        P(None, "leaf"),
        P(None, "leaf"),
        P(("leaf", "vec"), None, None),
    )
    return jax.shard_map(
        shards, mesh=mesh, in_specs=placed, out_specs=P("vec", "leaf"), check_vma=False
    )
```

```python
import jax
import jax.numpy as jnp
from jax import lax
from jax.experimental import pallas as pl
from jax.experimental.pallas import tpu as pltpu
from jax.sharding import PartitionSpec as P

MESH = pl.DeviceIdType.MESH
BF = jnp.bfloat16
F32 = jnp.float32
ROW = 16
ROWS = 8
LEAF_COUNT = ROW * ROWS
BASES = (0, 16, 24, 28, 30)
PREV = 42
NEXT = 51


def low(shape):
    return lax.broadcasted_iota(jnp.int32, shape, 1) < 64


def halves(a, b):
    return jnp.where(low(a.shape), a, b)


def turned(tile):
    return pltpu.roll(tile.astype(F32), 64, 1).astype(tile.dtype)


def rounded(x):
    return x.astype(BF).astype(F32)


def hilo(x):
    hi = rounded(x)
    return halves(hi, x - hi).astype(BF)


def two_terms(x):
    hi = rounded(x)
    return hi.astype(BF), (x - hi).astype(BF)


def nn(a, b):
    return jnp.dot(a, b, preferred_element_type=F32)


def nt(a, b):
    return lax.dot_general(a, b, (((1,), (1,)), ((), ())), preferred_element_type=F32)


def rows(*parts):
    return jnp.concatenate(parts, axis=0)


def lanes(*parts):
    return jnp.concatenate(parts, axis=1)


def kernel(
    vec_h, basis_h, lt_h, ut_h, uc_h, lc_h, far_h, near_h, tiles_h, out_ref,
    basis_v, lt_v, ut_v, uc_v, lc_v, far_s, near_s, tiles_v,
    arrived, points, coeffs, root_tile, nodes, heads, tails,
    dup, path_hi, path_lo, r0_hi, r0_lo, far_out, near_out, near_in,
    in_sem, send_sem, recv_sem, flag_0, flag_1,
):
    d = lax.axis_index("leaf")
    x = lax.axis_index("vec")
    y = d >> 4
    i = d & 15
    z = i >> 1
    c = i & 1

    def load(src, dst, n):
        copy = pltpu.make_async_copy(src, dst, in_sem.at[n])
        copy.start()
        return copy

    own = pl.ds(pl.multiple_of(16 * x, 16), 16)
    vec_in = load(vec_h, arrived.at[1, own], 0)
    basis_in = load(basis_h, basis_v, 1)
    lt_in = load(lt_h, lt_v, 2)

    right = (d + 1) & (LEAF_COUNT - 1)
    left = (d + LEAF_COUNT - 1) & (LEAF_COUNT - 1)
    sibling = d + 1 - 2 * c
    column_peers = [(d + ROW * k) & (LEAF_COUNT - 1) for k in (4, 3, 5, 2, 1, 6, 7)]
    vec_peers = [(x + k) & 3 for k in (2, 1, 3)]

    barrier = pltpu.get_barrier_semaphore()

    def announce(leaf, vec):
        pl.semaphore_signal(barrier, inc=1, device_id={"leaf": leaf, "vec": vec}, device_id_type=MESH)

    @pl.when(z < 4)
    def _():
        for k in range(1, 8):
            announce(ROW * y + 2 * ((z + k) & 7), x)

    @pl.when(z >= 4)
    def _():
        for k in range(1, 8):
            announce(ROW * y + 2 * ((z + k) & 7) + 1, x)

    announce(sibling, x)
    first = jnp.where(z == 0, 1, 0)
    last = jnp.where(z == 7, 1, 0)
    announce((d + LEAF_COUNT - 1 - first + c * (3 + first)) & (LEAF_COUNT - 1), x)
    for peer in vec_peers:
        announce(d - c, peer)
    for peer in column_peers:
        announce(peer - c + 1, x)

    def tell(flag):
        pl.semaphore_signal(flag, inc=1, device_id={"leaf": sibling, "vec": x}, device_id_type=MESH)

    ut_in = [
        load(ut_h.at[:, pl.ds(pl.multiple_of(1024 * y, 128), 1024)], ut_v.at[:, 0:1024], 3),
        load(ut_h.at[:, pl.ds(pl.multiple_of(8192 + 512 * y, 128), 512)], ut_v.at[:, 1024:1536], 4),
        load(ut_h.at[:, pl.ds(pl.multiple_of(12288 + 256 * y, 128), 256)], ut_v.at[:, 1536:1792], 5),
        load(ut_h.at[:, pl.ds(pl.multiple_of(14336 + 128 * y, 128), 128)], ut_v.at[:, 1792:1920], 6),
        load(ut_h.at[:, 15360:15872], ut_v.at[:, 1920:2432], 7),
    ]

    def send(src, dst, n_send, n_recv, leaf, vec):
        copy = pltpu.make_async_remote_copy(
            src_ref=src, dst_ref=dst, send_sem=send_sem.at[n_send], recv_sem=recv_sem.at[n_recv],
            device_id={"leaf": leaf, "vec": vec}, device_id_type=MESH,
        )
        copy.start()
        return copy

    def wait_for(ref, sem):
        pltpu.make_async_copy(ref, ref, sem).wait()

    @pl.when(c == 0)
    def _():
        pl.semaphore_wait(barrier, 13 + 2 * (z >> 2) + last)
        tell(flag_0)

    @pl.when(c == 1)
    def _():
        pl.semaphore_wait(flag_0, 1)

    for peer in vec_peers:
        send(vec_h, arrived.at[1, own], 0, 0, d, peer)

    vec_in.wait()
    basis_in.wait()
    lt_in.wait()
    transfer = lt_v[:, 1792:1920]
    crossed = turned(transfer)
    top = (halves(transfer, crossed), halves(crossed, transfer))

    zero = jnp.zeros((16, 128), BF)
    leaves = []
    for j in range(8):
        tile = arrived[1, own, 128 * j : 128 * j + 128]
        block = basis_v[:, 128 * j : 128 * j + 128]
        leaves.append(nt(rows(halves(tile, zero), halves(zero, tile)), rows(block, block)))
    current = []
    for j in range(8):
        coeff = leaves[j]
        first, second = coeff[0:16], coeff[16:32]
        coeffs[8 + j, 0] = halves(first, second).astype(BF)
        coeffs[8 + j, 1] = halves(second, first).astype(BF)
        transfer = lt_v[:, 128 * j : 128 * j + 128]
        lifted = nn(hilo(coeff), rows(transfer, transfer))
        current.append(halves(lifted[0:16], lifted[16:32]))
    for start in (1024, 1536):
        following = []
        for m in range(len(current) // 2):
            hi, lo = two_terms(rows(current[2 * m], current[2 * m + 1]))
            transfer = lt_v[:, start + 128 * m : start + 128 * m + 128]
            lifted = nn(lanes(hi, lo), rows(transfer, transfer, transfer, transfer))
            following.append(halves(lifted[0:16], lifted[16:32]))
        current = following
    first_hi, first_lo = two_terms(current[0])
    second_hi, second_lo = two_terms(current[1])
    root = nn(lanes(first_hi, first_lo, second_hi, second_lo), rows(*([top[0]] * 4 + [top[1]] * 4)))
    root_tile[...] = hilo(root)
    nodes[i] = root_tile[...]

    def send_root(t):
        send(root_tile, nodes.at[i], 1, 1, ROW * y + t, x)

    def to_right():
        send(arrived.at[1], arrived.at[0], 4, 4, right, x)
        send(coeffs.at[8:16, 0], coeffs.at[0:8, 0], 2, 2, right, x)

    def to_left():
        send(arrived.at[1], arrived.at[2], 5, 5, left, x)
        send(coeffs.at[8:16, 0], coeffs.at[16:24, 0], 3, 3, left, x)

    for k in range(1, 8):
        send_root((i + k) & 7)

    @pl.when(z >= 4)
    def _():
        send_root(i & 7)

    wait_for(arrived.at[1, 0:48], recv_sem.at[0])

    @pl.when(jnp.logical_or(c == 0, z == 7))
    def _():
        to_right()

    @pl.when(c == 1)
    def _():
        to_left()

    uc_in = load(uc_h, uc_v, 8)
    lc_in = load(lc_h, lc_v, 9)
    far_in_s = load(far_h, far_s, 10)
    near_in_s = load(near_h, near_s, 11)
    tiles_in = load(tiles_h, tiles_v, 12)

    for copy in ut_in:
        copy.wait()
    for p in range(19):
        pair = ut_v[:, 128 * p : 128 * p + 128]
        swapped = turned(pair)
        dup[2 * p] = halves(pair, swapped)
        dup[2 * p + 1] = halves(swapped, pair)

    path = dup[i]
    path_hi[0] = path
    path = path.astype(F32)
    below = [(top[0], None), (top[1], None)]

    def path_step(path, u):
        matrix = dup[BASES[u] + (i >> u if u < 4 else y)]
        path = nn(hilo(path), rows(matrix, matrix))
        path_hi[u], path_lo[u] = two_terms(path)
        return path

    def product_step(below, start):
        following = []
        for m, (hi, lo) in enumerate(below):
            pair = lt_v[:, start + 128 * m : start + 128 * m + 128]
            none = jnp.zeros_like(pair)
            left_side = rows(halves(pair, none), halves(none, pair))
            if lo is None:
                product = nn(left_side, rows(hi, hi))
            else:
                product = nn(lanes(left_side, left_side), rows(hi, hi, lo, lo))
            hi, lo = two_terms(product)
            if start == 0:
                r0_hi[m] = hi
                r0_lo[m] = lo
            following += [(hi[0:64], lo[0:64]), (hi[64:128], lo[64:128])]
        return following

    for u, start in ((1, 1536), (2, 1024), (3, 0)):
        path = path_step(path, u)
        below = product_step(below, start)
    path_step(path, 4)

    @pl.when(c == 1)
    def _():
        pl.semaphore_wait(barrier, 25 - 2 * (z >> 2) - last)
        tell(flag_1)

    @pl.when(c == 0)
    def _():
        pl.semaphore_wait(flag_1, 1)

    for k in range(1, 8):
        send_root(8 + ((i + k) & 7))

    @pl.when(z < 4)
    def _():
        send_root(8 + i)

    @pl.when(jnp.logical_and(c == 1, z < 7))
    def _():
        to_right()

    @pl.when(c == 0)
    def _():
        to_left()

    wait_for(nodes.at[0:15], recv_sem.at[1])
    for u in range(4):
        base, count = BASES[u], ROW >> u
        for m in range(count // 2):
            left_m, right_m = dup[base + 2 * m], dup[base + 2 * m + 1]
            value = nn(lanes(nodes[base + 2 * m], nodes[base + 2 * m + 1]), rows(left_m, left_m, right_m, right_m))
            if u < 3:
                nodes[BASES[u + 1] + m] = hilo(value)
            else:
                top_tile = hilo(value)
                nodes[30 + y] = top_tile
                heads[8] = top_tile
                tails[8] = top_tile
    for u in range(4):
        for e in range(2):
            heads[2 * u + e] = nodes[BASES[u] + e]
            tails[2 * u + e] = nodes[BASES[u + 1] - 2 + e]
    send(tails, nodes.at[PREV : PREV + 9], 6, 6, column_peers[4], x)
    send(heads, nodes.at[NEXT : NEXT + 9], 7, 7, column_peers[6], x)
    for peer in column_peers[:4] + column_peers[5:6]:
        send(nodes.at[30 + y], nodes.at[30 + y], 8, 8, peer, x)

    near_in_s.wait()
    tiles_in.wait()
    wait_for(arrived.at[0], recv_sem.at[4])
    wait_for(arrived.at[2], recv_sem.at[5])
    for w in range(3):
        for j in range(8):
            block = arrived[w, :, 128 * j : 128 * j + 128]
            points[8 * w + j, 0] = block
            points[8 * w + j, 1] = turned(block)
    first_leaf = ROW * d - ROW

    def chosen(table, lists, slots, column):
        parts = []
        for s in range(0, slots, 2):
            a = jnp.clip(lists[s, column] - first_leaf, 0, 3 * ROW - 1)
            b = jnp.clip(lists[s + 1, column] - first_leaf, 0, 3 * ROW - 1)
            parts.append(halves(table[a >> 1, a & 1], table[b >> 1, 1 - (b & 1)]))
        return lanes(*parts)

    for q in range(2):
        source = rows(*[chosen(points, near_s, 6, 4 * x + 2 * q + e) for e in range(2)])
        value = nt(source, rows(tiles_v[2 * q], tiles_v[2 * q + 1]))
        value = halves(value[0:64], value[64:128]).astype(BF)
        for v in range(4):
            near_out[v, q] = value[16 * v : 16 * v + 16]
    for n, peer in enumerate(vec_peers):
        send(near_out.at[peer], near_in.at[x], 9, 9, d, peer)
    near_in[x] = near_out[x]

    far_in_s.wait()
    lc_in.wait()
    wait_for(coeffs.at[0:8, 0], recv_sem.at[2])
    wait_for(coeffs.at[16:24, 0], recv_sem.at[3])
    for p in list(range(8)) + list(range(16, 24)):
        coeffs[p, 1] = turned(coeffs[p, 0])
    for j in range(8):
        source = rows(*[chosen(coeffs, far_s, 6, 2 * j + e) for e in range(2)])
        value = nt(source, rows(lc_v[:, 768 * j : 768 * j + 384], lc_v[:, 768 * j + 384 : 768 * j + 768]))
        far_out[j] = halves(value[0:16], value[16:32])

    uc_in.wait()
    weights = []
    for o in range(2):
        pair = uc_v[:, 128 * o : 128 * o + 128]
        swapped = turned(pair)
        weights += [halves(pair, swapped), halves(swapped, pair)]
    weights = lanes(*weights)
    wait_for(nodes.at[0:9], recv_sem.at[6])
    wait_for(nodes.at[0:9], recv_sem.at[7])
    wait_for(nodes.at[0:5], recv_sem.at[8])
    nodes[30 + ((y + 7) & 7)] = nodes[PREV + 8]
    nodes[30 + ((y + 1) & 7)] = nodes[NEXT + 8]
    for m in range(4):
        left_m, right_m = dup[30 + 2 * m], dup[31 + 2 * m]
        value = nn(lanes(nodes[30 + 2 * m], nodes[31 + 2 * m]), rows(left_m, left_m, right_m, right_m))
        nodes[38 + m] = hilo(value)
    sources = []
    for u in range(6):
        g = d >> u
        odd = g & 1
        number = LEAF_COUNT >> u
        parts = []
        for o, wanted in ((-3, odd == 1), (-2, None), (2, None), (3, odd == 0)):
            if u < 4:
                shift = o if wanted is None else (-3 * odd if o < 0 else 3 * (1 - odd))
                count = ROW >> u
                place = (i >> u) + shift
                place = jnp.where(
                    place < 0,
                    PREV + 2 + 2 * u + place,
                    jnp.where(place < count, BASES[u] + place, NEXT + 2 * u - count + place),
                )
            else:
                place = (30, 38)[u - 4] + ((g + o + number) & (number - 1))
            valid = (g + o >= 0) if o < 0 else (g + o < number)
            if wanted is not None:
                valid = jnp.logical_and(valid, wanted)
            keep = jnp.where(valid, 1.0, 0.0).astype(F32)
            parts.append((nodes[place].astype(F32) * keep).astype(BF))
        sources.append(lanes(*parts))
    coupled = nt(rows(*sources), rows(weights, weights))
    left_side, right_side = [], []
    for u in range(1, 6):
        tile = hilo(coupled[16 * u : 16 * u + 16])
        left_side.append(tile)
        right_side.append(path_hi[u - 1])
        if u > 1:
            left_side.append(tile)
            right_side.append(path_lo[u - 1])
    matrix = lanes(*right_side)
    down = coupled[0:16] + nt(lanes(*left_side), rows(matrix, matrix))
    down = hilo(down)
    down = lanes(down, down)

    wait_for(near_in.at[0:3], recv_sem.at[9])
    for j in range(8):
        local = nt(down, lanes(r0_hi[j], r0_lo[j]))
        leaf_down = (local + far_out[j]).astype(BF)
        block = basis_v[:, 128 * j : 128 * j + 128]
        none = jnp.zeros_like(block)
        value = nn(leaf_down, rows(halves(block, none), halves(none, block)))
        out_ref[:, 128 * j : 128 * j + 128] = (value + near_in[j // 2, j % 2].astype(F32)).astype(BF)

    wait_for(arrived.at[1, 0:48], send_sem.at[0])
    wait_for(nodes.at[0:15], send_sem.at[1])
    wait_for(coeffs.at[0:8, 0], send_sem.at[2])
    wait_for(coeffs.at[0:8, 0], send_sem.at[3])
    wait_for(arrived.at[0], send_sem.at[4])
    wait_for(arrived.at[2], send_sem.at[5])
    wait_for(nodes.at[0:9], send_sem.at[6])
    wait_for(nodes.at[0:9], send_sem.at[7])
    wait_for(nodes.at[0:5], send_sem.at[8])
    wait_for(near_out.at[0:3], send_sem.at[9])


def shards(vectors, leaf_basis, local_transfer, upper_transfer, upper_coupling, leaf_coupling, far_list, near_list, near_tiles):
    tile = (16, 128)
    scratch = [
        pltpu.VMEM(leaf_basis.shape, BF),
        pltpu.VMEM(local_transfer.shape, BF),
        pltpu.VMEM((64, 2432), BF),
        pltpu.VMEM(upper_coupling.shape, BF),
        pltpu.VMEM(leaf_coupling.shape, BF),
        pltpu.SMEM(far_list.shape, jnp.int32),
        pltpu.SMEM(near_list.shape, jnp.int32),
        pltpu.VMEM(near_tiles.shape, BF),
        pltpu.VMEM((3, 64, 1024), BF),
        pltpu.VMEM((24, 2, 64, 128), BF),
        pltpu.VMEM((24, 2) + tile, BF),
        pltpu.VMEM(tile, BF),
        pltpu.VMEM((60,) + tile, BF),
        pltpu.VMEM((9,) + tile, BF),
        pltpu.VMEM((9,) + tile, BF),
        pltpu.VMEM((38, 64, 128), BF),
        pltpu.VMEM((5, 64, 128), BF),
        pltpu.VMEM((5, 64, 128), BF),
        pltpu.VMEM((8, 128, 128), BF),
        pltpu.VMEM((8, 128, 128), BF),
        pltpu.VMEM((8,) + tile, F32),
        pltpu.VMEM((4, 2) + tile, BF),
        pltpu.VMEM((4, 2) + tile, BF),
        pltpu.SemaphoreType.DMA((13,)),
        pltpu.SemaphoreType.DMA((10,)),
        pltpu.SemaphoreType.DMA((10,)),
        pltpu.SemaphoreType.REGULAR,
        pltpu.SemaphoreType.REGULAR,
    ]
    return pl.pallas_call(
        kernel,
        out_shape=pltpu.VMEM(vectors.shape, BF),
        in_specs=[pl.BlockSpec(memory_space=pl.ANY)] * 9,
        out_specs=pl.BlockSpec(memory_space=pltpu.VMEM),
        scratch_shapes=scratch,
        compiler_params=pltpu.CompilerParams(
            collective_id=0, has_side_effects=True, vmem_limit_bytes=62 * 1024 * 1024
        ),
    )(vectors, leaf_basis, local_transfer, upper_transfer, upper_coupling, leaf_coupling, far_list, near_list, near_tiles)


def solution(mesh):
    placed = (
        P("vec", "leaf"),
        P(None, "leaf"),
        P(None, "leaf"),
        P(),
        P(),
        P(None, "leaf"),
        P(None, "leaf"),
        P(None, "leaf"),
        P(("leaf", "vec"), None, None),
    )
    return jax.shard_map(
        shards, mesh=mesh, in_specs=placed, out_specs=P("vec", "leaf"), check_vma=False
    )
```

```python
import jax
import jax.numpy as jnp
from jax import lax
from jax.experimental import pallas as pl
from jax.experimental.pallas import tpu as pltpu
from jax.sharding import PartitionSpec as P

MESH = pl.DeviceIdType.MESH
BF = jnp.bfloat16
F32 = jnp.float32
ROW = 16
ROWS = 8
LEAF_COUNT = ROW * ROWS
BASES = (0, 16, 24, 28, 30)
PREV = 42
NEXT = 51


def low(shape):
    return lax.broadcasted_iota(jnp.int32, shape, 1) < 64


def halves(a, b):
    return jnp.where(low(a.shape), a, b)


def turned(tile):
    return pltpu.roll(tile, 64, 1)


def rounded(x):
    return x.astype(BF).astype(F32)


def hilo(x):
    hi = rounded(x)
    return halves(hi, x - hi).astype(BF)


def two_terms(x):
    hi = rounded(x)
    return hi.astype(BF), (x - hi).astype(BF)


def nn(a, b):
    return jnp.dot(a, b, preferred_element_type=F32)


def nt(a, b):
    return lax.dot_general(a, b, (((1,), (1,)), ((), ())), preferred_element_type=F32)


def rows(*parts):
    return jnp.concatenate(parts, axis=0)


def lanes(*parts):
    return jnp.concatenate(parts, axis=1)


def kernel(
    vec_h, basis_h, lt_h, ut_h, uc_h, lc_h, far_h, near_h, tiles_h, out_ref,
    basis_v, lt_v, ut_v, uc_v, lc_v, far_s, near_s, tiles_v,
    arrived, points, coeffs, root_tile, nodes, heads, tails,
    dup, path_hi, path_lo, r0_hi, r0_lo, far_out, near_out, near_in,
    in_sem, send_sem, recv_sem, flag_0, flag_1,
):
    d = lax.axis_index("leaf")
    x = lax.axis_index("vec")
    y = d >> 4
    i = d & 15
    z = i >> 1
    c = i & 1

    def load(src, dst, n):
        copy = pltpu.make_async_copy(src, dst, in_sem.at[n])
        copy.start()
        return copy

    own = pl.ds(pl.multiple_of(16 * x, 16), 16)
    vec_in = load(vec_h, arrived.at[1, own], 0)
    basis_in = load(basis_h, basis_v, 1)
    lt_in = load(lt_h, lt_v, 2)

    right = (d + 1) & (LEAF_COUNT - 1)
    left = (d + LEAF_COUNT - 1) & (LEAF_COUNT - 1)
    sibling = d + 1 - 2 * c
    column_peers = [(d + ROW * k) & (LEAF_COUNT - 1) for k in (4, 3, 5, 2, 1, 6, 7)]
    vec_peers = [(x + k) & 3 for k in (2, 1, 3)]

    barrier = pltpu.get_barrier_semaphore()

    def announce(leaf, vec):
        pl.semaphore_signal(barrier, inc=1, device_id={"leaf": leaf, "vec": vec}, device_id_type=MESH)

    @pl.when(z < 4)
    def _():
        for k in range(1, 8):
            announce(ROW * y + 2 * ((z + k) & 7), x)

    @pl.when(z >= 4)
    def _():
        for k in range(1, 8):
            announce(ROW * y + 2 * ((z + k) & 7) + 1, x)

    announce(sibling, x)
    at_start = jnp.where(z == 0, 1, 0)
    at_end = jnp.where(z == 7, 1, 0)
    announce((d + jnp.where(c == 0, LEAF_COUNT - 1 - at_start, 1 + at_end)) & (LEAF_COUNT - 1), x)
    for peer in vec_peers:
        announce(d - c, peer)
    for peer in column_peers:
        announce(peer - c + 1, x)

    def tell(flag):
        pl.semaphore_signal(flag, inc=1, device_id={"leaf": sibling, "vec": x}, device_id_type=MESH)

    ut_in = [
        load(ut_h.at[:, pl.ds(pl.multiple_of(1024 * y, 128), 1024)], ut_v.at[:, 0:1024], 3),
        load(ut_h.at[:, pl.ds(pl.multiple_of(8192 + 512 * y, 128), 512)], ut_v.at[:, 1024:1536], 4),
        load(ut_h.at[:, pl.ds(pl.multiple_of(12288 + 256 * y, 128), 256)], ut_v.at[:, 1536:1792], 5),
        load(ut_h.at[:, pl.ds(pl.multiple_of(14336 + 128 * y, 128), 128)], ut_v.at[:, 1792:1920], 6),
        load(ut_h.at[:, 15360:15872], ut_v.at[:, 1920:2432], 7),
    ]

    def send(src, dst, n_send, n_recv, leaf, vec):
        copy = pltpu.make_async_remote_copy(
            src_ref=src, dst_ref=dst, send_sem=send_sem.at[n_send], recv_sem=recv_sem.at[n_recv],
            device_id={"leaf": leaf, "vec": vec}, device_id_type=MESH,
        )
        copy.start()
        return copy

    def wait_for(ref, sem):
        pltpu.make_async_copy(ref, ref, sem).wait()

    vec_in.wait()
    basis_in.wait()
    lt_in.wait()
    transfer = lt_v[:, 1792:1920]
    crossed = turned(transfer)
    top = (halves(transfer, crossed), halves(crossed, transfer))

    zero = jnp.zeros((16, 128), BF)
    leaves = []
    for j in range(8):
        tile = arrived[1, own, 128 * j : 128 * j + 128]
        block = basis_v[:, 128 * j : 128 * j + 128]
        leaves.append(nt(rows(halves(tile, zero), halves(zero, tile)), rows(block, block)))
    current = []
    for j in range(8):
        coeff = leaves[j]
        first, second = coeff[0:16], coeff[16:32]
        coeffs[8 + j, 0] = halves(first, second).astype(BF)
        coeffs[8 + j, 1] = halves(second, first).astype(BF)
        transfer = lt_v[:, 128 * j : 128 * j + 128]
        lifted = nn(hilo(coeff), rows(transfer, transfer))
        current.append(halves(lifted[0:16], lifted[16:32]))
    for start in (1024, 1536):
        following = []
        for m in range(len(current) // 2):
            hi, lo = two_terms(rows(current[2 * m], current[2 * m + 1]))
            transfer = lt_v[:, start + 128 * m : start + 128 * m + 128]
            lifted = nn(lanes(hi, lo), rows(transfer, transfer, transfer, transfer))
            following.append(halves(lifted[0:16], lifted[16:32]))
        current = following
    first_hi, first_lo = two_terms(current[0])
    second_hi, second_lo = two_terms(current[1])
    root = nn(lanes(first_hi, first_lo, second_hi, second_lo), rows(*([top[0]] * 4 + [top[1]] * 4)))
    root_tile[...] = hilo(root)
    nodes[i] = root_tile[...]

    @pl.when(c == 0)
    def _():
        pl.semaphore_wait(barrier, 14 + 2 * (z >> 2) + at_end - at_start)
        tell(flag_0)

    @pl.when(c == 1)
    def _():
        pl.semaphore_wait(flag_0, 1)

    def send_root(t):
        send(root_tile, nodes.at[i], 1, 1, ROW * y + t, x)

    def to_right():
        send(arrived.at[1], arrived.at[0], 4, 4, right, x)
        send(coeffs.at[8:16, 0], coeffs.at[0:8, 0], 2, 2, right, x)

    def to_left():
        send(arrived.at[1], arrived.at[2], 5, 5, left, x)
        send(coeffs.at[8:16, 0], coeffs.at[16:24, 0], 3, 3, left, x)

    for k in range(1, 8):
        send_root((i + k) & 7)

    @pl.when(z >= 4)
    def _():
        send_root(i & 7)

    for peer in vec_peers:
        send(vec_h, arrived.at[1, own], 0, 0, d, peer)

    wait_for(arrived.at[1, 0:48], recv_sem.at[0])

    @pl.when(jnp.logical_or(c == 0, z == 7))
    def _():
        to_right()

    @pl.when(jnp.logical_or(c == 1, z > 0))
    def _():
        to_left()

    uc_in = load(uc_h, uc_v, 8)
    lc_in = load(lc_h, lc_v, 9)
    far_in_s = load(far_h, far_s, 10)
    near_in_s = load(near_h, near_s, 11)
    tiles_in = load(tiles_h, tiles_v, 12)

    for copy in ut_in:
        copy.wait()
    for p in range(19):
        pair = ut_v[:, 128 * p : 128 * p + 128]
        swapped = turned(pair)
        dup[2 * p] = halves(pair, swapped)
        dup[2 * p + 1] = halves(swapped, pair)

    path = dup[i]
    path_hi[0] = path
    path = path.astype(F32)
    below = [(top[0], None), (top[1], None)]

    def path_step(path, u):
        matrix = dup[BASES[u] + (i >> u if u < 4 else y)]
        path = nn(hilo(path), rows(matrix, matrix))
        path_hi[u], path_lo[u] = two_terms(path)
        return path

    def product_step(below, start):
        following = []
        for m, (hi, lo) in enumerate(below):
            pair = lt_v[:, start + 128 * m : start + 128 * m + 128]
            none = jnp.zeros_like(pair)
            left_side = rows(halves(pair, none), halves(none, pair))
            if lo is None:
                product = nn(left_side, rows(hi, hi))
            else:
                product = nn(lanes(left_side, left_side), rows(hi, hi, lo, lo))
            hi, lo = two_terms(product)
            if start == 0:
                r0_hi[m] = hi
                r0_lo[m] = lo
            following += [(hi[0:64], lo[0:64]), (hi[64:128], lo[64:128])]
        return following

    for u, start in ((1, 1536), (2, 1024), (3, 0)):
        path = path_step(path, u)
        below = product_step(below, start)
    path_step(path, 4)

    @pl.when(c == 1)
    def _():
        pl.semaphore_wait(barrier, 24 - 2 * (z >> 2) - at_end + at_start)
        tell(flag_1)

    @pl.when(c == 0)
    def _():
        pl.semaphore_wait(flag_1, 1)

    for k in range(1, 8):
        send_root(8 + ((i + k) & 7))

    @pl.when(z < 4)
    def _():
        send_root(8 + i)

    @pl.when(jnp.logical_and(c == 1, z < 7))
    def _():
        to_right()

    @pl.when(jnp.logical_and(c == 0, z == 0))
    def _():
        to_left()

    first_leaf = ROW * d - ROW

    def chosen(table, lists, slots, column):
        parts = []
        for s in range(0, slots, 2):
            a = jnp.clip(lists[s, column] - first_leaf, 0, 3 * ROW - 1)
            b = jnp.clip(lists[s + 1, column] - first_leaf, 0, 3 * ROW - 1)
            parts.append(halves(table[a >> 1, a & 1], table[b >> 1, 1 - (b & 1)]))
        return lanes(*parts)

    def far_part():
        far_in_s.wait()
        lc_in.wait()
        wait_for(coeffs.at[0:8, 0], recv_sem.at[2])
        wait_for(coeffs.at[16:24, 0], recv_sem.at[3])
        for p in list(range(8)) + list(range(16, 24)):
            coeffs[p, 1] = turned(coeffs[p, 0])
        for j in range(8):
            source = rows(*[chosen(coeffs, far_s, 6, 2 * j + e) for e in range(2)])
            value = nt(source, rows(lc_v[:, 768 * j : 768 * j + 384], lc_v[:, 768 * j + 384 : 768 * j + 768]))
            far_out[j] = halves(value[0:16], value[16:32])

    def near_part():
        near_in_s.wait()
        tiles_in.wait()
        wait_for(arrived.at[0], recv_sem.at[4])
        wait_for(arrived.at[2], recv_sem.at[5])
        for w in range(3):
            for j in range(8):
                block = arrived[w, :, 128 * j : 128 * j + 128]
                points[8 * w + j, 0] = block
                points[8 * w + j, 1] = turned(block)
        for q in range(2):
            source = rows(*[chosen(points, near_s, 6, 4 * x + 2 * q + e) for e in range(2)])
            value = nt(source, rows(tiles_v[2 * q], tiles_v[2 * q + 1]))
            value = halves(value[0:64], value[64:128]).astype(BF)
            for v in range(4):
                near_out[v, q] = value[16 * v : 16 * v + 16]
        for n, peer in enumerate(vec_peers):
            send(near_out.at[peer], near_in.at[x], 9, 9, d, peer)
        near_in[x] = near_out[x]

    @pl.when(c == 1)
    def _():
        far_part()
        near_part()

    wait_for(nodes.at[0:15], recv_sem.at[1])
    for u in range(4):
        base, count = BASES[u], ROW >> u
        for m in range(count // 2):
            left_m, right_m = dup[base + 2 * m], dup[base + 2 * m + 1]
            value = nn(lanes(nodes[base + 2 * m], nodes[base + 2 * m + 1]), rows(left_m, left_m, right_m, right_m))
            if u < 3:
                nodes[BASES[u + 1] + m] = hilo(value)
            else:
                top_tile = hilo(value)
                nodes[30 + y] = top_tile
                heads[8] = top_tile
                tails[8] = top_tile
    for u in range(4):
        for e in range(2):
            heads[2 * u + e] = nodes[BASES[u] + e]
            tails[2 * u + e] = nodes[BASES[u + 1] - 2 + e]
    send(tails, nodes.at[PREV : PREV + 9], 6, 6, column_peers[4], x)
    send(heads, nodes.at[NEXT : NEXT + 9], 7, 7, column_peers[6], x)
    for peer in column_peers[:4] + column_peers[5:6]:
        send(nodes.at[30 + y], nodes.at[30 + y], 8, 8, peer, x)

    @pl.when(c == 0)
    def _():
        far_part()
        near_part()

    uc_in.wait()
    weights = []
    for o in range(2):
        pair = uc_v[:, 128 * o : 128 * o + 128]
        swapped = turned(pair)
        weights += [halves(pair, swapped), halves(swapped, pair)]
    weights = lanes(*weights)
    wait_for(nodes.at[0:9], recv_sem.at[6])
    wait_for(nodes.at[0:9], recv_sem.at[7])
    wait_for(nodes.at[0:5], recv_sem.at[8])
    nodes[30 + ((y + 7) & 7)] = nodes[PREV + 8]
    nodes[30 + ((y + 1) & 7)] = nodes[NEXT + 8]
    for m in range(4):
        left_m, right_m = dup[30 + 2 * m], dup[31 + 2 * m]
        value = nn(lanes(nodes[30 + 2 * m], nodes[31 + 2 * m]), rows(left_m, left_m, right_m, right_m))
        nodes[38 + m] = hilo(value)
    sources = []
    for u in range(6):
        g = d >> u
        odd = g & 1
        number = LEAF_COUNT >> u
        parts = []
        for o, wanted in ((-3, odd == 1), (-2, None), (2, None), (3, odd == 0)):
            if u < 4:
                shift = o if wanted is None else (-3 * odd if o < 0 else 3 * (1 - odd))
                count = ROW >> u
                place = (i >> u) + shift
                place = jnp.where(
                    place < 0,
                    PREV + 2 + 2 * u + place,
                    jnp.where(place < count, BASES[u] + place, NEXT + 2 * u - count + place),
                )
            else:
                place = (30, 38)[u - 4] + ((g + o + number) & (number - 1))
            valid = (g + o >= 0) if o < 0 else (g + o < number)
            if wanted is not None:
                valid = jnp.logical_and(valid, wanted)
            keep = jnp.where(valid, 1.0, 0.0).astype(F32)
            parts.append((nodes[place].astype(F32) * keep).astype(BF))
        sources.append(lanes(*parts))
    coupled = nt(rows(*sources), rows(weights, weights))
    left_side, right_side = [], []
    for u in range(1, 6):
        tile = hilo(coupled[16 * u : 16 * u + 16])
        left_side.append(tile)
        right_side.append(path_hi[u - 1])
        if u > 1:
            left_side.append(tile)
            right_side.append(path_lo[u - 1])
    matrix = lanes(*right_side)
    down = coupled[0:16] + nt(lanes(*left_side), rows(matrix, matrix))
    down = hilo(down)
    down = lanes(down, down)

    wait_for(near_in.at[0:3], recv_sem.at[9])
    for j in range(8):
        local = nt(down, lanes(r0_hi[j], r0_lo[j]))
        leaf_down = (local + far_out[j]).astype(BF)
        block = basis_v[:, 128 * j : 128 * j + 128]
        none = jnp.zeros_like(block)
        value = nn(leaf_down, rows(halves(block, none), halves(none, block)))
        out_ref[:, 128 * j : 128 * j + 128] = (value + near_in[j // 2, j % 2].astype(F32)).astype(BF)

    wait_for(arrived.at[1, 0:48], send_sem.at[0])
    wait_for(nodes.at[0:15], send_sem.at[1])
    wait_for(coeffs.at[0:8, 0], send_sem.at[2])
    wait_for(coeffs.at[0:8, 0], send_sem.at[3])
    wait_for(arrived.at[0], send_sem.at[4])
    wait_for(arrived.at[2], send_sem.at[5])
    wait_for(nodes.at[0:9], send_sem.at[6])
    wait_for(nodes.at[0:9], send_sem.at[7])
    wait_for(nodes.at[0:5], send_sem.at[8])
    wait_for(near_out.at[0:3], send_sem.at[9])


def shards(vectors, leaf_basis, local_transfer, upper_transfer, upper_coupling, leaf_coupling, far_list, near_list, near_tiles):
    tile = (16, 128)
    scratch = [
        pltpu.VMEM(leaf_basis.shape, BF),
        pltpu.VMEM(local_transfer.shape, BF),
        pltpu.VMEM((64, 2432), BF),
        pltpu.VMEM(upper_coupling.shape, BF),
        pltpu.VMEM(leaf_coupling.shape, BF),
        pltpu.SMEM(far_list.shape, jnp.int32),
        pltpu.SMEM(near_list.shape, jnp.int32),
        pltpu.VMEM(near_tiles.shape, BF),
        pltpu.VMEM((3, 64, 1024), BF),
        pltpu.VMEM((24, 2, 64, 128), BF),
        pltpu.VMEM((24, 2) + tile, BF),
        pltpu.VMEM(tile, BF),
        pltpu.VMEM((60,) + tile, BF),
        pltpu.VMEM((9,) + tile, BF),
        pltpu.VMEM((9,) + tile, BF),
        pltpu.VMEM((38, 64, 128), BF),
        pltpu.VMEM((5, 64, 128), BF),
        pltpu.VMEM((5, 64, 128), BF),
        pltpu.VMEM((8, 128, 128), BF),
        pltpu.VMEM((8, 128, 128), BF),
        pltpu.VMEM((8,) + tile, F32),
        pltpu.VMEM((4, 2) + tile, BF),
        pltpu.VMEM((4, 2) + tile, BF),
        pltpu.SemaphoreType.DMA((13,)),
        pltpu.SemaphoreType.DMA((10,)),
        pltpu.SemaphoreType.DMA((10,)),
        pltpu.SemaphoreType.REGULAR,
        pltpu.SemaphoreType.REGULAR,
    ]
    return pl.pallas_call(
        kernel,
        out_shape=pltpu.VMEM(vectors.shape, BF),
        in_specs=[pl.BlockSpec(memory_space=pl.ANY)] * 9,
        out_specs=pl.BlockSpec(memory_space=pltpu.VMEM),
        scratch_shapes=scratch,
        compiler_params=pltpu.CompilerParams(
            collective_id=0, has_side_effects=True, vmem_limit_bytes=62 * 1024 * 1024
        ),
    )(vectors, leaf_basis, local_transfer, upper_transfer, upper_coupling, leaf_coupling, far_list, near_list, near_tiles)


def solution(mesh):
    placed = (
        P("vec", "leaf"),
        P(None, "leaf"),
        P(None, "leaf"),
        P(),
        P(),
        P(None, "leaf"),
        P(None, "leaf"),
        P(None, "leaf"),
        P(("leaf", "vec"), None, None),
    )
    return jax.shard_map(
        shards, mesh=mesh, in_specs=placed, out_specs=P("vec", "leaf"), check_vma=False
    )
```

```python
import jax
import jax.numpy as jnp
from jax import lax
from jax.experimental import pallas as pl
from jax.experimental.pallas import tpu as pltpu
from jax.sharding import PartitionSpec as P

MESH = pl.DeviceIdType.MESH
BF = jnp.bfloat16
F32 = jnp.float32
ROW = 16
ROWS = 8
LEAF_COUNT = ROW * ROWS
BASES = (0, 16, 24, 28, 30)
PREV = 42
NEXT = 51


def low(shape):
    return lax.broadcasted_iota(jnp.int32, shape, 1) < 64


def halves(a, b):
    return jnp.where(low(a.shape), a, b)


def turned(tile):
    return pltpu.roll(tile, 64, 1)


def rounded(x):
    return x.astype(BF).astype(F32)


def hilo(x):
    hi = rounded(x)
    return halves(hi, x - hi).astype(BF)


def two_terms(x):
    hi = rounded(x)
    return hi.astype(BF), (x - hi).astype(BF)


def nn(a, b):
    return jnp.dot(a, b, preferred_element_type=F32)


def nt(a, b):
    return lax.dot_general(a, b, (((1,), (1,)), ((), ())), preferred_element_type=F32)


def tn(a, b):
    return lax.dot_general(a, b, (((0,), (0,)), ((), ())), preferred_element_type=F32)


def diagonal(block):
    none = jnp.zeros_like(block)
    return rows(halves(block, none), halves(none, block))


def rows(*parts):
    return jnp.concatenate(parts, axis=0)


def lanes(*parts):
    return jnp.concatenate(parts, axis=1)


def kernel(
    vec_h, basis_h, lt_h, ut_h, uc_h, lc_h, far_h, near_h, tiles_h, out_ref,
    basis_v, lt_v, ut_v, uc_v, lc_v, far_s, near_s, tiles_v,
    arrived, points, coeffs, root_tile, nodes, heads, tails,
    dup, path_hi, path_lo, r0_hi, r0_lo, to_points, lifted_couplings, from_top, far_out, near_out, near_in,
    in_sem, send_sem, recv_sem, flag_0, flag_1,
):
    d = lax.axis_index("leaf")
    x = lax.axis_index("vec")
    y = d >> 4
    i = d & 15
    z = i >> 1
    c = i & 1

    def load(src, dst, n):
        copy = pltpu.make_async_copy(src, dst, in_sem.at[n])
        copy.start()
        return copy

    own = pl.ds(pl.multiple_of(16 * x, 16), 16)
    vec_in = load(vec_h, arrived.at[1, own], 0)
    basis_in = load(basis_h, basis_v, 1)
    lt_in = load(lt_h, lt_v, 2)

    right = (d + 1) & (LEAF_COUNT - 1)
    left = (d + LEAF_COUNT - 1) & (LEAF_COUNT - 1)
    sibling = d + 1 - 2 * c
    column_peers = [(d + ROW * k) & (LEAF_COUNT - 1) for k in (4, 3, 5, 2, 1, 6, 7)]
    vec_peers = [(x + k) & 3 for k in (2, 1, 3)]

    barrier = pltpu.get_barrier_semaphore()

    def announce(leaf, vec):
        pl.semaphore_signal(barrier, inc=1, device_id={"leaf": leaf, "vec": vec}, device_id_type=MESH)

    @pl.when(z < 4)
    def _():
        for k in range(1, 8):
            announce(ROW * y + 2 * ((z + k) & 7), x)

    @pl.when(z >= 4)
    def _():
        for k in range(1, 8):
            announce(ROW * y + 2 * ((z + k) & 7) + 1, x)

    announce(sibling, x)
    at_start = jnp.where(z == 0, 1, 0)
    at_end = jnp.where(z == 7, 1, 0)
    announce((d + jnp.where(c == 0, LEAF_COUNT - 1 - at_start, 1 + at_end)) & (LEAF_COUNT - 1), x)
    for peer in vec_peers:
        announce(d - c, peer)
    for peer in column_peers:
        announce(peer - c + 1, x)

    def tell(flag):
        pl.semaphore_signal(flag, inc=1, device_id={"leaf": sibling, "vec": x}, device_id_type=MESH)

    ut_in = [
        load(ut_h.at[:, pl.ds(pl.multiple_of(1024 * y, 128), 1024)], ut_v.at[:, 0:1024], 3),
        load(ut_h.at[:, pl.ds(pl.multiple_of(8192 + 512 * y, 128), 512)], ut_v.at[:, 1024:1536], 4),
        load(ut_h.at[:, pl.ds(pl.multiple_of(12288 + 256 * y, 128), 256)], ut_v.at[:, 1536:1792], 5),
        load(ut_h.at[:, pl.ds(pl.multiple_of(14336 + 128 * y, 128), 128)], ut_v.at[:, 1792:1920], 6),
        load(ut_h.at[:, 15360:15872], ut_v.at[:, 1920:2432], 7),
    ]

    def send(src, dst, n_send, n_recv, leaf, vec):
        copy = pltpu.make_async_remote_copy(
            src_ref=src, dst_ref=dst, send_sem=send_sem.at[n_send], recv_sem=recv_sem.at[n_recv],
            device_id={"leaf": leaf, "vec": vec}, device_id_type=MESH,
        )
        copy.start()
        return copy

    def wait_for(ref, sem):
        pltpu.make_async_copy(ref, ref, sem).wait()

    vec_in.wait()
    basis_in.wait()
    lt_in.wait()
    transfer = lt_v[:, 1792:1920]
    crossed = turned(transfer)
    top = (halves(transfer, crossed), halves(crossed, transfer))

    zero = jnp.zeros((16, 128), BF)
    leaves = []
    for j in range(8):
        tile = arrived[1, own, 128 * j : 128 * j + 128]
        block = basis_v[:, 128 * j : 128 * j + 128]
        leaves.append(nt(rows(halves(tile, zero), halves(zero, tile)), rows(block, block)))
    current = []
    for j in range(8):
        coeff = leaves[j]
        first, second = coeff[0:16], coeff[16:32]
        coeffs[8 + j, 0] = halves(first, second).astype(BF)
        coeffs[8 + j, 1] = halves(second, first).astype(BF)
        transfer = lt_v[:, 128 * j : 128 * j + 128]
        lifted = nn(hilo(coeff), rows(transfer, transfer))
        current.append(halves(lifted[0:16], lifted[16:32]))
    for start in (1024, 1536):
        following = []
        for m in range(len(current) // 2):
            hi, lo = two_terms(rows(current[2 * m], current[2 * m + 1]))
            transfer = lt_v[:, start + 128 * m : start + 128 * m + 128]
            lifted = nn(lanes(hi, lo), rows(transfer, transfer, transfer, transfer))
            following.append(halves(lifted[0:16], lifted[16:32]))
        current = following
    first_hi, first_lo = two_terms(current[0])
    second_hi, second_lo = two_terms(current[1])
    root = nn(lanes(first_hi, first_lo, second_hi, second_lo), rows(*([top[0]] * 4 + [top[1]] * 4)))
    root_tile[...] = hilo(root)
    nodes[i] = root_tile[...]

    @pl.when(c == 0)
    def _():
        pl.semaphore_wait(barrier, 14 + 2 * (z >> 2) + at_end - at_start)
        tell(flag_0)

    @pl.when(c == 1)
    def _():
        pl.semaphore_wait(flag_0, 1)

    def send_root(t):
        send(root_tile, nodes.at[i], 1, 1, ROW * y + t, x)

    def to_right():
        send(arrived.at[1], arrived.at[0], 4, 4, right, x)
        send(coeffs.at[8:16, 0], coeffs.at[0:8, 0], 2, 2, right, x)

    def to_left():
        send(arrived.at[1], arrived.at[2], 5, 5, left, x)
        send(coeffs.at[8:16, 0], coeffs.at[16:24, 0], 3, 3, left, x)

    for k in range(1, 8):
        send_root((i + k) & 7)

    @pl.when(z >= 4)
    def _():
        send_root(i & 7)

    for peer in vec_peers:
        send(vec_h, arrived.at[1, own], 0, 0, d, peer)

    @pl.when(z == 7)
    def _():
        wait_for(arrived.at[1, 0:48], recv_sem.at[0])
        to_right()

    uc_in = load(uc_h, uc_v, 8)
    lc_in = load(lc_h, lc_v, 9)
    far_in_s = load(far_h, far_s, 10)
    near_in_s = load(near_h, near_s, 11)
    tiles_in = load(tiles_h, tiles_v, 12)

    for copy in ut_in:
        copy.wait()
    for p in range(19):
        pair = ut_v[:, 128 * p : 128 * p + 128]
        swapped = turned(pair)
        dup[2 * p] = halves(pair, swapped)
        dup[2 * p + 1] = halves(swapped, pair)

    path = dup[i]
    path_hi[0] = path
    path = path.astype(F32)
    below = [(top[0], None), (top[1], None)]

    def path_step(path, u):
        matrix = dup[BASES[u] + (i >> u if u < 4 else y)]
        path = nn(hilo(path), rows(matrix, matrix))
        path_hi[u], path_lo[u] = two_terms(path)
        return path

    def product_step(below, start):
        following = []
        for m, (hi, lo) in enumerate(below):
            pair = lt_v[:, start + 128 * m : start + 128 * m + 128]
            none = jnp.zeros_like(pair)
            left_side = rows(halves(pair, none), halves(none, pair))
            if lo is None:
                product = nn(left_side, rows(hi, hi))
            else:
                product = nn(lanes(left_side, left_side), rows(hi, hi, lo, lo))
            hi, lo = two_terms(product)
            if start == 0:
                r0_hi[m] = hi
                r0_lo[m] = lo
            following += [(hi[0:64], lo[0:64]), (hi[64:128], lo[64:128])]
        return following

    for u, start in ((1, 1536), (2, 1024), (3, 0)):
        path = path_step(path, u)
        below = product_step(below, start)
    path_step(path, 4)

    def fold(j, carry):
        at = pl.ds(pl.multiple_of(128 * j, 128), 128)
        block = diagonal(basis_v[:, at])
        hi, lo = two_terms(tn(r0_hi[j], block) + tn(r0_lo[j], block))
        to_points[0:128, at] = hi
        to_points[128:256, at] = lo
        return carry

    lax.fori_loop(0, 8, fold, 0)

    uc_in.wait()
    couplings = rows(uc_v[...], uc_v[...])
    for e in range(2):
        value = nn(halves(path_hi[3 + e], path_lo[3 + e]), couplings)
        value = jnp.transpose(rows(value, value))
        for o in range(4):
            lifted_couplings[e, o] = value[64 * o : 64 * o + 64]

    def slot(offset, odd):
        index = jnp.where(offset == -3, 0, jnp.where(offset == -2, 1, jnp.where(offset == 2, 2, 3)))
        wide = jnp.logical_or(
            jnp.logical_and(offset == -3, odd == 1), jnp.logical_and(offset == 3, odd == 0)
        )
        valid = jnp.logical_or(jnp.logical_or(offset == -2, offset == 2), wide)
        return index, jnp.where(valid, 1.0, 0.0).astype(F32)

    def gather_top(n, carry):
        index, keep = slot(n - y, y & 1)
        value = lifted_couplings[0, index] * keep
        index, keep = slot((n >> 1) - (y >> 1), (y >> 1) & 1)
        hi, lo = two_terms(lifted_couplings[1, index] * keep)
        hi, lo = two_terms(value + nn(dup[30 + n], rows(hi, lo)))
        from_top[0, n] = rows(hi, hi)
        from_top[1, n] = rows(lo, lo)
        return carry

    lax.fori_loop(0, 8, gather_top, 0)

    @pl.when(z < 7)
    def _():
        wait_for(arrived.at[1, 0:48], recv_sem.at[0])

    @pl.when(jnp.logical_and(c == 0, z < 7))
    def _():
        to_right()

    @pl.when(jnp.logical_or(c == 1, z > 0))
    def _():
        to_left()

    def fill(w):
        def step(j, carry):
            block = arrived[w, :, pl.ds(pl.multiple_of(128 * j, 128), 128)]
            points[8 * w + j, 0] = block
            points[8 * w + j, 1] = turned(block)
            return carry

        lax.fori_loop(0, 8, step, 0, unroll=2)

    fill(1)

    @pl.when(c == 1)
    def _():
        pl.semaphore_wait(barrier, 24 - 2 * (z >> 2) - at_end + at_start)
        tell(flag_1)

    @pl.when(c == 0)
    def _():
        pl.semaphore_wait(flag_1, 1)

    for k in range(1, 8):
        send_root(8 + ((i + k) & 7))

    @pl.when(z < 4)
    def _():
        send_root(8 + i)

    @pl.when(jnp.logical_and(c == 1, z < 7))
    def _():
        to_right()

    @pl.when(jnp.logical_and(c == 0, z == 0))
    def _():
        to_left()

    first_leaf = ROW * d - ROW

    def chosen(table, lists, slots, column):
        parts = []
        for s in range(0, slots, 2):
            a = jnp.clip(lists[s, column] - first_leaf, 0, 3 * ROW - 1)
            b = jnp.clip(lists[s + 1, column] - first_leaf, 0, 3 * ROW - 1)
            parts.append(halves(table[a >> 1, a & 1], table[b >> 1, 1 - (b & 1)]))
        return lanes(*parts)

    def far_part():
        far_in_s.wait()
        lc_in.wait()
        wait_for(coeffs.at[0:8, 0], recv_sem.at[2])
        wait_for(coeffs.at[16:24, 0], recv_sem.at[3])
        for p in list(range(8)) + list(range(16, 24)):
            coeffs[p, 1] = turned(coeffs[p, 0])
        for j in range(8):
            source = rows(*[chosen(coeffs, far_s, 6, 2 * j + e) for e in range(2)])
            value = nt(source, rows(lc_v[:, 768 * j : 768 * j + 384], lc_v[:, 768 * j + 384 : 768 * j + 768]))
            hi, lo = two_terms(halves(value[0:16], value[16:32]))
            block = diagonal(basis_v[:, 128 * j : 128 * j + 128])
            far_out[j] = nn(lanes(hi, lo), rows(block, block))

    def near_part():
        near_in_s.wait()
        tiles_in.wait()
        wait_for(arrived.at[0], recv_sem.at[4])
        wait_for(arrived.at[2], recv_sem.at[5])
        fill(0)
        fill(2)
        for q in range(2):
            source = rows(*[chosen(points, near_s, 6, 4 * x + 2 * q + e) for e in range(2)])
            value = nt(source, rows(tiles_v[2 * q], tiles_v[2 * q + 1]))
            value = halves(value[0:64], value[64:128]).astype(BF)
            for v in range(4):
                near_out[v, q] = value[16 * v : 16 * v + 16]
        for n, peer in enumerate(vec_peers):
            send(near_out.at[peer], near_in.at[x], 9, 9, d, peer)
        near_in[x] = near_out[x]

    wait_for(nodes.at[0:15], recv_sem.at[1])
    for u in range(4):
        base, count = BASES[u], ROW >> u
        for m in range(count // 2):
            left_m, right_m = dup[base + 2 * m], dup[base + 2 * m + 1]
            value = nn(lanes(nodes[base + 2 * m], nodes[base + 2 * m + 1]), rows(left_m, left_m, right_m, right_m))
            if u < 3:
                nodes[BASES[u + 1] + m] = hilo(value)
            else:
                top_tile = hilo(value)
                nodes[30 + y] = top_tile
                heads[8] = top_tile
                tails[8] = top_tile
    for u in range(4):
        for e in range(2):
            heads[2 * u + e] = nodes[BASES[u] + e]
            tails[2 * u + e] = nodes[BASES[u + 1] - 2 + e]
    send(tails, nodes.at[PREV : PREV + 9], 6, 6, column_peers[4], x)
    send(heads, nodes.at[NEXT : NEXT + 9], 7, 7, column_peers[6], x)
    for peer in column_peers[:4] + column_peers[5:6]:
        send(nodes.at[30 + y], nodes.at[30 + y], 8, 8, peer, x)

    far_part()
    near_part()

    weights = []
    for o in range(2):
        pair = uc_v[:, 128 * o : 128 * o + 128]
        swapped = turned(pair)
        weights += [halves(pair, swapped), halves(swapped, pair)]
    weights = lanes(*weights)
    wait_for(nodes.at[0:9], recv_sem.at[6])
    wait_for(nodes.at[0:9], recv_sem.at[7])
    sources = []
    for u in range(4):
        g = d >> u
        odd = g & 1
        number = LEAF_COUNT >> u
        count = ROW >> u
        parts = []
        for o, wanted in ((-3, odd == 1), (-2, None), (2, None), (3, odd == 0)):
            shift = o if wanted is None else (-3 * odd if o < 0 else 3 * (1 - odd))
            place = (i >> u) + shift
            place = jnp.where(
                place < 0,
                PREV + 2 + 2 * u + place,
                jnp.where(place < count, BASES[u] + place, NEXT + 2 * u - count + place),
            )
            valid = (g + o >= 0) if o < 0 else (g + o < number)
            if wanted is not None:
                valid = jnp.logical_and(valid, wanted)
            keep = jnp.where(valid, 1.0, 0.0).astype(F32)
            parts.append((nodes[place].astype(F32) * keep).astype(BF))
        sources.append(lanes(*parts))
    coupled = nt(rows(*sources), rows(weights, weights))
    left_side, right_side = [], []
    for u in range(1, 4):
        tile = hilo(coupled[16 * u : 16 * u + 16])
        left_side.append(tile)
        right_side.append(path_hi[u - 1])
        if u > 1:
            left_side.append(tile)
            right_side.append(path_lo[u - 1])
    matrix = lanes(*right_side)
    down = coupled[0:16] + nt(lanes(*left_side), rows(matrix, matrix))

    nodes[30 + ((y + 7) & 7)] = nodes[PREV + 8]
    nodes[30 + ((y + 1) & 7)] = nodes[NEXT + 8]
    wait_for(nodes.at[0:5], recv_sem.at[8])
    tops = lanes(*[nodes[30 + n] for n in range(8)])
    down = down + nn(tops, from_top[0].reshape(1024, 128)) + nn(tops, from_top[1].reshape(1024, 128))
    down = hilo(down)
    value = nn(lanes(down, down), to_points[...])
    wait_for(near_in.at[0:3], recv_sem.at[9])
    for j in range(8):
        at = slice(128 * j, 128 * j + 128)
        out_ref[:, at] = (value[:, at] + far_out[j] + near_in[j // 2, j % 2].astype(F32)).astype(BF)

    wait_for(arrived.at[1, 0:48], send_sem.at[0])
    wait_for(nodes.at[0:15], send_sem.at[1])
    wait_for(coeffs.at[0:8, 0], send_sem.at[2])
    wait_for(coeffs.at[0:8, 0], send_sem.at[3])
    wait_for(arrived.at[0], send_sem.at[4])
    wait_for(arrived.at[2], send_sem.at[5])
    wait_for(nodes.at[0:9], send_sem.at[6])
    wait_for(nodes.at[0:9], send_sem.at[7])
    wait_for(nodes.at[0:5], send_sem.at[8])
    wait_for(near_out.at[0:3], send_sem.at[9])


def shards(vectors, leaf_basis, local_transfer, upper_transfer, upper_coupling, leaf_coupling, far_list, near_list, near_tiles):
    tile = (16, 128)
    scratch = [
        pltpu.VMEM(leaf_basis.shape, BF),
        pltpu.VMEM(local_transfer.shape, BF),
        pltpu.VMEM((64, 2432), BF),
        pltpu.VMEM(upper_coupling.shape, BF),
        pltpu.VMEM(leaf_coupling.shape, BF),
        pltpu.SMEM(far_list.shape, jnp.int32),
        pltpu.SMEM(near_list.shape, jnp.int32),
        pltpu.VMEM(near_tiles.shape, BF),
        pltpu.VMEM((3, 64, 1024), BF),
        pltpu.VMEM((24, 2, 64, 128), BF),
        pltpu.VMEM((24, 2) + tile, BF),
        pltpu.VMEM(tile, BF),
        pltpu.VMEM((60,) + tile, BF),
        pltpu.VMEM((9,) + tile, BF),
        pltpu.VMEM((9,) + tile, BF),
        pltpu.VMEM((38, 64, 128), BF),
        pltpu.VMEM((5, 64, 128), BF),
        pltpu.VMEM((5, 64, 128), BF),
        pltpu.VMEM((8, 128, 128), BF),
        pltpu.VMEM((8, 128, 128), BF),
        pltpu.VMEM((256, 1024), BF),
        pltpu.VMEM((2, 4, 64, 128), F32),
        pltpu.VMEM((2, 8, 128, 128), BF),
        pltpu.VMEM((8,) + tile, F32),
        pltpu.VMEM((4, 2) + tile, BF),
        pltpu.VMEM((4, 2) + tile, BF),
        pltpu.SemaphoreType.DMA((13,)),
        pltpu.SemaphoreType.DMA((10,)),
        pltpu.SemaphoreType.DMA((10,)),
        pltpu.SemaphoreType.REGULAR,
        pltpu.SemaphoreType.REGULAR,
    ]
    return pl.pallas_call(
        kernel,
        out_shape=pltpu.VMEM(vectors.shape, BF),
        in_specs=[pl.BlockSpec(memory_space=pl.ANY)] * 9,
        out_specs=pl.BlockSpec(memory_space=pltpu.VMEM),
        scratch_shapes=scratch,
        compiler_params=pltpu.CompilerParams(
            collective_id=0, has_side_effects=True, vmem_limit_bytes=62 * 1024 * 1024
        ),
    )(vectors, leaf_basis, local_transfer, upper_transfer, upper_coupling, leaf_coupling, far_list, near_list, near_tiles)


def solution(mesh):
    placed = (
        P("vec", "leaf"),
        P(None, "leaf"),
        P(None, "leaf"),
        P(),
        P(),
        P(None, "leaf"),
        P(None, "leaf"),
        P(None, "leaf"),
        P(("leaf", "vec"), None, None),
    )
    return jax.shard_map(
        shards, mesh=mesh, in_specs=placed, out_specs=P("vec", "leaf"), check_vma=False
    )
```

```python
import jax
import jax.numpy as jnp
from jax import lax
from jax.experimental import pallas as pl
from jax.experimental.pallas import tpu as pltpu
from jax.sharding import PartitionSpec as P

MESH = pl.DeviceIdType.MESH
BF = jnp.bfloat16
F32 = jnp.float32
ROW = 16
ROWS = 8
LEAF_COUNT = ROW * ROWS
BASES = (0, 16, 24, 28, 30)
PREV = 42
NEXT = 51


def low(shape):
    return lax.broadcasted_iota(jnp.int32, shape, 1) < 64


def halves(a, b):
    return jnp.where(low(a.shape), a, b)


def turned(tile):
    return pltpu.roll(tile, 64, 1)


def rounded(x):
    return x.astype(BF).astype(F32)


def hilo(x):
    hi = rounded(x)
    return halves(hi, x - hi).astype(BF)


def two_terms(x):
    hi = rounded(x)
    return hi.astype(BF), (x - hi).astype(BF)


def nn(a, b):
    return jnp.dot(a, b, preferred_element_type=F32)


def nt(a, b):
    return lax.dot_general(a, b, (((1,), (1,)), ((), ())), preferred_element_type=F32)


def tn(a, b):
    return lax.dot_general(a, b, (((0,), (0,)), ((), ())), preferred_element_type=F32)


def diagonal(block):
    none = jnp.zeros_like(block)
    return rows(halves(block, none), halves(none, block))


def rows(*parts):
    return jnp.concatenate(parts, axis=0)


def lanes(*parts):
    return jnp.concatenate(parts, axis=1)


def kernel(
    vec_h, basis_h, lt_h, ut_h, uc_h, lc_h, far_h, near_h, tiles_h, out_ref,
    basis_v, lt_v, ut_v, uc_v, lc_v, far_s, near_s, tiles_v,
    arrived, points, coeffs, root_tile, nodes, heads, tails,
    dup, path_hi, path_lo, r0_hi, r0_lo, to_points, lifted_couplings, from_top, far_out, near_out, near_in,
    in_sem, send_sem, recv_sem, flag_0, flag_1,
):
    d = lax.axis_index("leaf")
    x = lax.axis_index("vec")
    y = d >> 4
    i = d & 15
    z = i >> 1
    c = i & 1

    def load(src, dst, n):
        copy = pltpu.make_async_copy(src, dst, in_sem.at[n])
        copy.start()
        return copy

    own = pl.ds(pl.multiple_of(16 * x, 16), 16)
    vec_in = load(vec_h, arrived.at[1, own], 0)
    basis_in = load(basis_h, basis_v, 1)
    lt_in = load(lt_h, lt_v, 2)

    right = (d + 1) & (LEAF_COUNT - 1)
    left = (d + LEAF_COUNT - 1) & (LEAF_COUNT - 1)
    sibling = d + 1 - 2 * c
    column_peers = [(d + ROW * k) & (LEAF_COUNT - 1) for k in (4, 3, 5, 2, 1, 6, 7)]
    vec_peers = [(x + k) & 3 for k in (2, 1, 3)]

    barrier = pltpu.get_barrier_semaphore()

    def announce(leaf, vec):
        pl.semaphore_signal(barrier, inc=1, device_id={"leaf": leaf, "vec": vec}, device_id_type=MESH)

    @pl.when(z < 4)
    def _():
        for k in range(1, 8):
            announce(ROW * y + 2 * ((z + k) & 7), x)

    @pl.when(z >= 4)
    def _():
        for k in range(1, 8):
            announce(ROW * y + 2 * ((z + k) & 7) + 1, x)

    announce(sibling, x)
    at_start = jnp.where(z == 0, 1, 0)
    at_end = jnp.where(z == 7, 1, 0)
    announce((d + jnp.where(c == 0, LEAF_COUNT - 1 - at_start, 1 + at_end)) & (LEAF_COUNT - 1), x)
    for peer in vec_peers:
        announce(d - c + 1, peer)
    for peer in column_peers:
        announce(peer - c + 1, x)

    def tell(flag):
        pl.semaphore_signal(flag, inc=1, device_id={"leaf": sibling, "vec": x}, device_id_type=MESH)

    ut_in = [
        load(ut_h.at[:, pl.ds(pl.multiple_of(1024 * y, 128), 1024)], ut_v.at[:, 0:1024], 3),
        load(ut_h.at[:, pl.ds(pl.multiple_of(8192 + 512 * y, 128), 512)], ut_v.at[:, 1024:1536], 4),
        load(ut_h.at[:, pl.ds(pl.multiple_of(12288 + 256 * y, 128), 256)], ut_v.at[:, 1536:1792], 5),
        load(ut_h.at[:, pl.ds(pl.multiple_of(14336 + 128 * y, 128), 128)], ut_v.at[:, 1792:1920], 6),
        load(ut_h.at[:, 15360:15872], ut_v.at[:, 1920:2432], 7),
    ]

    def send(src, dst, n_send, n_recv, leaf, vec):
        copy = pltpu.make_async_remote_copy(
            src_ref=src, dst_ref=dst, send_sem=send_sem.at[n_send], recv_sem=recv_sem.at[n_recv],
            device_id={"leaf": leaf, "vec": vec}, device_id_type=MESH,
        )
        copy.start()
        return copy

    def wait_for(ref, sem):
        pltpu.make_async_copy(ref, ref, sem).wait()

    vec_in.wait()
    basis_in.wait()
    lt_in.wait()
    transfer = lt_v[:, 1792:1920]
    crossed = turned(transfer)
    top = (halves(transfer, crossed), halves(crossed, transfer))

    zero = jnp.zeros((16, 128), BF)
    leaves = []
    for j in range(8):
        tile = arrived[1, own, 128 * j : 128 * j + 128]
        block = basis_v[:, 128 * j : 128 * j + 128]
        leaves.append(nt(rows(halves(tile, zero), halves(zero, tile)), rows(block, block)))
    current = []
    for j in range(8):
        coeff = leaves[j]
        first, second = coeff[0:16], coeff[16:32]
        coeffs[8 + j, 0] = halves(first, second).astype(BF)
        coeffs[8 + j, 1] = halves(second, first).astype(BF)
        transfer = lt_v[:, 128 * j : 128 * j + 128]
        lifted = nn(hilo(coeff), rows(transfer, transfer))
        current.append(halves(lifted[0:16], lifted[16:32]))
    for start in (1024, 1536):
        following = []
        for m in range(len(current) // 2):
            hi, lo = two_terms(rows(current[2 * m], current[2 * m + 1]))
            transfer = lt_v[:, start + 128 * m : start + 128 * m + 128]
            lifted = nn(lanes(hi, lo), rows(transfer, transfer, transfer, transfer))
            following.append(halves(lifted[0:16], lifted[16:32]))
        current = following
    first_hi, first_lo = two_terms(current[0])
    second_hi, second_lo = two_terms(current[1])
    root = nn(lanes(first_hi, first_lo, second_hi, second_lo), rows(*([top[0]] * 4 + [top[1]] * 4)))
    root_tile[...] = hilo(root)
    nodes[i] = root_tile[...]

    @pl.when(c == 0)
    def _():
        pl.semaphore_wait(barrier, 8 + 2 * (z >> 2) + at_end - at_start)
        tell(flag_0)

    @pl.when(c == 1)
    def _():
        pl.semaphore_wait(flag_0, 1)

    def send_root(t):
        send(root_tile, nodes.at[i], 1, 1, ROW * y + t, x)

    def far_right():
        send(coeffs.at[8:16, 0], coeffs.at[0:8, 0], 2, 2, right, x)

    def near_right():
        send(arrived.at[1], arrived.at[0], 4, 4, right, x)

    row_end = jnp.logical_and(c == 1, z == 7)
    row_start = jnp.logical_and(c == 0, z == 0)

    for k in range(1, 8):
        send_root((i + k) & 7)

    @pl.when(z >= 4)
    def _():
        send_root(i & 7)

    @pl.when(row_end)
    def _():
        send(vec_h, arrived.at[0, own], 10, 4, right, x)
        far_right()

    uc_in = load(uc_h, uc_v, 8)
    lc_in = load(lc_h, lc_v, 9)
    far_in_s = load(far_h, far_s, 10)
    near_in_s = load(near_h, near_s, 11)
    tiles_in = load(tiles_h, tiles_v, 12)

    for copy in ut_in:
        copy.wait()
    for p in range(19):
        pair = ut_v[:, 128 * p : 128 * p + 128]
        swapped = turned(pair)
        dup[2 * p] = halves(pair, swapped)
        dup[2 * p + 1] = halves(swapped, pair)

    path = dup[i]
    path_hi[0] = path
    path = path.astype(F32)
    below = [(top[0], None), (top[1], None)]

    def path_step(path, u):
        matrix = dup[BASES[u] + (i >> u if u < 4 else y)]
        path = nn(hilo(path), rows(matrix, matrix))
        path_hi[u], path_lo[u] = two_terms(path)
        return path

    def product_step(below, start):
        following = []
        for m, (hi, lo) in enumerate(below):
            pair = lt_v[:, start + 128 * m : start + 128 * m + 128]
            none = jnp.zeros_like(pair)
            left_side = rows(halves(pair, none), halves(none, pair))
            if lo is None:
                product = nn(left_side, rows(hi, hi))
            else:
                product = nn(lanes(left_side, left_side), rows(hi, hi, lo, lo))
            hi, lo = two_terms(product)
            if start == 0:
                r0_hi[m] = hi
                r0_lo[m] = lo
            following += [(hi[0:64], lo[0:64]), (hi[64:128], lo[64:128])]
        return following

    for u, start in ((1, 1536), (2, 1024), (3, 0)):
        path = path_step(path, u)
        below = product_step(below, start)
    path_step(path, 4)

    def fold(j, carry):
        at = pl.ds(pl.multiple_of(128 * j, 128), 128)
        block = diagonal(basis_v[:, at])
        hi, lo = two_terms(tn(r0_hi[j], block) + tn(r0_lo[j], block))
        to_points[0:128, at] = hi
        to_points[128:256, at] = lo
        return carry

    lax.fori_loop(0, 8, fold, 0)

    uc_in.wait()
    couplings = rows(uc_v[...], uc_v[...])
    for e in range(2):
        value = nn(halves(path_hi[3 + e], path_lo[3 + e]), couplings)
        value = jnp.transpose(rows(value, value))
        for o in range(4):
            lifted_couplings[e, o] = value[64 * o : 64 * o + 64]

    def slot(offset, odd):
        index = jnp.where(offset == -3, 0, jnp.where(offset == -2, 1, jnp.where(offset == 2, 2, 3)))
        wide = jnp.logical_or(
            jnp.logical_and(offset == -3, odd == 1), jnp.logical_and(offset == 3, odd == 0)
        )
        valid = jnp.logical_or(jnp.logical_or(offset == -2, offset == 2), wide)
        return index, jnp.where(valid, 1.0, 0.0).astype(F32)

    def gather_top(n, carry):
        index, keep = slot(n - y, y & 1)
        value = lifted_couplings[0, index] * keep
        index, keep = slot((n >> 1) - (y >> 1), (y >> 1) & 1)
        hi, lo = two_terms(lifted_couplings[1, index] * keep)
        hi, lo = two_terms(value + nn(dup[30 + n], rows(hi, lo)))
        from_top[0, n] = rows(hi, hi)
        from_top[1, n] = rows(lo, lo)
        return carry

    lax.fori_loop(0, 8, gather_top, 0)

    def fill(w):
        def step(j, carry):
            block = arrived[w, :, pl.ds(pl.multiple_of(128 * j, 128), 128)]
            points[8 * w + j, 0] = block
            points[8 * w + j, 1] = turned(block)
            return carry

        lax.fori_loop(0, 8, step, 0, unroll=2)

    @pl.when(c == 1)
    def _():
        pl.semaphore_wait(barrier, 30 - 2 * (z >> 2) - at_end + at_start)
        tell(flag_1)

    @pl.when(c == 0)
    def _():
        pl.semaphore_wait(flag_1, 1)

    for k in range(1, 8):
        send_root(8 + ((i + k) & 7))

    @pl.when(z < 4)
    def _():
        send_root(8 + i)

    for peer in vec_peers:
        send(vec_h, arrived.at[1, own], 0, 0, d, peer)
    send(coeffs.at[8:16, 0], coeffs.at[16:24, 0], 3, 3, left, x)

    @pl.when(jnp.logical_not(row_end))
    def _():
        far_right()

    wait_for(arrived.at[1, 0:48], recv_sem.at[0])
    send(arrived.at[1], arrived.at[2], 5, 5, left, x)

    @pl.when(jnp.logical_not(row_end))
    def _():
        near_right()

    fill(1)

    first_leaf = ROW * d - ROW

    def chosen(table, lists, slots, column):
        parts = []
        for s in range(0, slots, 2):
            a = jnp.clip(lists[s, column] - first_leaf, 0, 3 * ROW - 1)
            b = jnp.clip(lists[s + 1, column] - first_leaf, 0, 3 * ROW - 1)
            parts.append(halves(table[a >> 1, a & 1], table[b >> 1, 1 - (b & 1)]))
        return lanes(*parts)

    def far_part():
        far_in_s.wait()
        lc_in.wait()
        wait_for(coeffs.at[0:8, 0], recv_sem.at[2])
        wait_for(coeffs.at[16:24, 0], recv_sem.at[3])
        for p in list(range(8)) + list(range(16, 24)):
            coeffs[p, 1] = turned(coeffs[p, 0])
        for j in range(8):
            source = rows(*[chosen(coeffs, far_s, 6, 2 * j + e) for e in range(2)])
            value = nt(source, rows(lc_v[:, 768 * j : 768 * j + 384], lc_v[:, 768 * j + 384 : 768 * j + 768]))
            hi, lo = two_terms(halves(value[0:16], value[16:32]))
            block = diagonal(basis_v[:, 128 * j : 128 * j + 128])
            far_out[j] = nn(lanes(hi, lo), rows(block, block))

    def near_part():
        near_in_s.wait()
        tiles_in.wait()

        @pl.when(row_start)
        def _():
            wait_for(arrived.at[0, 0:48], recv_sem.at[10])

        @pl.when(jnp.logical_not(row_start))
        def _():
            wait_for(arrived.at[0], recv_sem.at[4])

        wait_for(arrived.at[2], recv_sem.at[5])
        fill(0)
        fill(2)
        for q in range(2):
            source = rows(*[chosen(points, near_s, 6, 4 * x + 2 * q + e) for e in range(2)])
            value = nt(source, rows(tiles_v[2 * q], tiles_v[2 * q + 1]))
            value = halves(value[0:64], value[64:128]).astype(BF)
            for v in range(4):
                near_out[v, q] = value[16 * v : 16 * v + 16]
        for n, peer in enumerate(vec_peers):
            send(near_out.at[peer], near_in.at[x], 9, 9, d, peer)
        near_in[x] = near_out[x]

    wait_for(nodes.at[0:15], recv_sem.at[1])
    for u in range(4):
        base, count = BASES[u], ROW >> u
        for m in range(count // 2):
            left_m, right_m = dup[base + 2 * m], dup[base + 2 * m + 1]
            value = nn(lanes(nodes[base + 2 * m], nodes[base + 2 * m + 1]), rows(left_m, left_m, right_m, right_m))
            if u < 3:
                nodes[BASES[u + 1] + m] = hilo(value)
            else:
                top_tile = hilo(value)
                nodes[30 + y] = top_tile
                heads[8] = top_tile
                tails[8] = top_tile
    for u in range(4):
        for e in range(2):
            heads[2 * u + e] = nodes[BASES[u] + e]
            tails[2 * u + e] = nodes[BASES[u + 1] - 2 + e]
    send(tails, nodes.at[PREV : PREV + 9], 6, 6, column_peers[4], x)
    send(heads, nodes.at[NEXT : NEXT + 9], 7, 7, column_peers[6], x)
    for peer in column_peers[:4] + column_peers[5:6]:
        send(nodes.at[30 + y], nodes.at[30 + y], 8, 8, peer, x)

    @pl.when(row_start)
    def _():
        wait_for(arrived.at[0, 0:16], recv_sem.at[4])
        for peer in vec_peers:
            send(arrived.at[0, own], arrived.at[0, own], 10, 10, d, peer)

    far_part()
    near_part()

    weights = []
    for o in range(2):
        pair = uc_v[:, 128 * o : 128 * o + 128]
        swapped = turned(pair)
        weights += [halves(pair, swapped), halves(swapped, pair)]
    weights = lanes(*weights)
    wait_for(nodes.at[0:9], recv_sem.at[6])
    wait_for(nodes.at[0:9], recv_sem.at[7])
    sources = []
    for u in range(4):
        g = d >> u
        odd = g & 1
        number = LEAF_COUNT >> u
        count = ROW >> u
        parts = []
        for o, wanted in ((-3, odd == 1), (-2, None), (2, None), (3, odd == 0)):
            shift = o if wanted is None else (-3 * odd if o < 0 else 3 * (1 - odd))
            place = (i >> u) + shift
            place = jnp.where(
                place < 0,
                PREV + 2 + 2 * u + place,
                jnp.where(place < count, BASES[u] + place, NEXT + 2 * u - count + place),
            )
            valid = (g + o >= 0) if o < 0 else (g + o < number)
            if wanted is not None:
                valid = jnp.logical_and(valid, wanted)
            keep = jnp.where(valid, 1.0, 0.0).astype(F32)
            parts.append((nodes[place].astype(F32) * keep).astype(BF))
        sources.append(lanes(*parts))
    coupled = nt(rows(*sources), rows(weights, weights))
    left_side, right_side = [], []
    for u in range(1, 4):
        tile = hilo(coupled[16 * u : 16 * u + 16])
        left_side.append(tile)
        right_side.append(path_hi[u - 1])
        if u > 1:
            left_side.append(tile)
            right_side.append(path_lo[u - 1])
    matrix = lanes(*right_side)
    down = coupled[0:16] + nt(lanes(*left_side), rows(matrix, matrix))

    nodes[30 + ((y + 7) & 7)] = nodes[PREV + 8]
    nodes[30 + ((y + 1) & 7)] = nodes[NEXT + 8]
    wait_for(nodes.at[0:5], recv_sem.at[8])
    tops = lanes(*[nodes[30 + n] for n in range(8)])
    down = down + nn(tops, from_top[0].reshape(1024, 128)) + nn(tops, from_top[1].reshape(1024, 128))
    down = hilo(down)
    value = nn(lanes(down, down), to_points[...])
    wait_for(near_in.at[0:3], recv_sem.at[9])
    for j in range(8):
        at = slice(128 * j, 128 * j + 128)
        out_ref[:, at] = (value[:, at] + far_out[j] + near_in[j // 2, j % 2].astype(F32)).astype(BF)

    wait_for(arrived.at[1, 0:48], send_sem.at[0])
    wait_for(nodes.at[0:15], send_sem.at[1])
    wait_for(coeffs.at[0:8, 0], send_sem.at[2])
    wait_for(coeffs.at[0:8, 0], send_sem.at[3])

    @pl.when(row_end)
    def _():
        wait_for(arrived.at[0, 0:16], send_sem.at[10])

    @pl.when(row_start)
    def _():
        wait_for(arrived.at[0, 0:48], send_sem.at[10])

    @pl.when(jnp.logical_not(row_end))
    def _():
        wait_for(arrived.at[0], send_sem.at[4])

    wait_for(arrived.at[2], send_sem.at[5])
    wait_for(nodes.at[0:9], send_sem.at[6])
    wait_for(nodes.at[0:9], send_sem.at[7])
    wait_for(nodes.at[0:5], send_sem.at[8])
    wait_for(near_out.at[0:3], send_sem.at[9])


def shards(vectors, leaf_basis, local_transfer, upper_transfer, upper_coupling, leaf_coupling, far_list, near_list, near_tiles):
    tile = (16, 128)
    scratch = [
        pltpu.VMEM(leaf_basis.shape, BF),
        pltpu.VMEM(local_transfer.shape, BF),
        pltpu.VMEM((64, 2432), BF),
        pltpu.VMEM(upper_coupling.shape, BF),
        pltpu.VMEM(leaf_coupling.shape, BF),
        pltpu.SMEM(far_list.shape, jnp.int32),
        pltpu.SMEM(near_list.shape, jnp.int32),
        pltpu.VMEM(near_tiles.shape, BF),
        pltpu.VMEM((3, 64, 1024), BF),
        pltpu.VMEM((24, 2, 64, 128), BF),
        pltpu.VMEM((24, 2) + tile, BF),
        pltpu.VMEM(tile, BF),
        pltpu.VMEM((60,) + tile, BF),
        pltpu.VMEM((9,) + tile, BF),
        pltpu.VMEM((9,) + tile, BF),
        pltpu.VMEM((38, 64, 128), BF),
        pltpu.VMEM((5, 64, 128), BF),
        pltpu.VMEM((5, 64, 128), BF),
        pltpu.VMEM((8, 128, 128), BF),
        pltpu.VMEM((8, 128, 128), BF),
        pltpu.VMEM((256, 1024), BF),
        pltpu.VMEM((2, 4, 64, 128), F32),
        pltpu.VMEM((2, 8, 128, 128), BF),
        pltpu.VMEM((8,) + tile, F32),
        pltpu.VMEM((4, 2) + tile, BF),
        pltpu.VMEM((4, 2) + tile, BF),
        pltpu.SemaphoreType.DMA((13,)),
        pltpu.SemaphoreType.DMA((11,)),
        pltpu.SemaphoreType.DMA((11,)),
        pltpu.SemaphoreType.REGULAR,
        pltpu.SemaphoreType.REGULAR,
    ]
    return pl.pallas_call(
        kernel,
        out_shape=pltpu.VMEM(vectors.shape, BF),
        in_specs=[pl.BlockSpec(memory_space=pl.ANY)] * 9,
        out_specs=pl.BlockSpec(memory_space=pltpu.VMEM),
        scratch_shapes=scratch,
        compiler_params=pltpu.CompilerParams(
            collective_id=0, has_side_effects=True, vmem_limit_bytes=62 * 1024 * 1024
        ),
    )(vectors, leaf_basis, local_transfer, upper_transfer, upper_coupling, leaf_coupling, far_list, near_list, near_tiles)


def solution(mesh):
    placed = (
        P("vec", "leaf"),
        P(None, "leaf"),
        P(None, "leaf"),
        P(),
        P(),
        P(None, "leaf"),
        P(None, "leaf"),
        P(None, "leaf"),
        P(("leaf", "vec"), None, None),
    )
    return jax.shard_map(
        shards, mesh=mesh, in_specs=placed, out_specs=P("vec", "leaf"), check_vma=False
    )
```

```python
import jax
import jax.numpy as jnp
from jax import lax
from jax.experimental import pallas as pl
from jax.experimental.pallas import tpu as pltpu
from jax.sharding import PartitionSpec as P

MESH = pl.DeviceIdType.MESH
BF = jnp.bfloat16
F32 = jnp.float32
ROW = 16
ROWS = 8
LEAF_COUNT = ROW * ROWS
BASES = (0, 16, 24, 28, 30)
PREV = 42
NEXT = 51


def low(shape):
    return lax.broadcasted_iota(jnp.int32, shape, 1) < 64


def halves(a, b):
    return jnp.where(low(a.shape), a, b)


def turned(tile):
    return pltpu.roll(tile, 64, 1)


def rounded(x):
    return x.astype(BF).astype(F32)


def hilo(x):
    hi = rounded(x)
    return halves(hi, x - hi).astype(BF)


def two_terms(x):
    hi = rounded(x)
    return hi.astype(BF), (x - hi).astype(BF)


def nn(a, b):
    return jnp.dot(a, b, preferred_element_type=F32)


def nt(a, b):
    return lax.dot_general(a, b, (((1,), (1,)), ((), ())), preferred_element_type=F32)


def tn(a, b):
    return lax.dot_general(a, b, (((0,), (0,)), ((), ())), preferred_element_type=F32)


def diagonal(block):
    none = jnp.zeros_like(block)
    return rows(halves(block, none), halves(none, block))


def rows(*parts):
    return jnp.concatenate(parts, axis=0)


def lanes(*parts):
    return jnp.concatenate(parts, axis=1)


def kernel(
    vec_h, basis_h, lt_h, ut_h, uc_h, lc_h, far_h, near_h, tiles_h, out_ref,
    basis_v, lt_v, ut_v, uc_v, lc_v, far_s, near_s, tiles_v,
    arrived, points, coeffs, root_tile, nodes, heads, tails,
    dup, path_hi, path_lo, r0_hi, r0_lo, to_points, lifted_couplings, from_top, far_out, near_out, near_in,
    in_sem, send_sem, recv_sem, flag_0, flag_1,
):
    d = lax.axis_index("leaf")
    x = lax.axis_index("vec")
    y = d >> 4
    i = d & 15
    z = i >> 1
    c = i & 1

    def load(src, dst, n):
        copy = pltpu.make_async_copy(src, dst, in_sem.at[n])
        copy.start()
        return copy

    own = pl.ds(pl.multiple_of(16 * x, 16), 16)
    vec_in = load(vec_h, arrived.at[1, own], 0)
    basis_in = load(basis_h, basis_v, 1)
    lt_in = load(lt_h, lt_v, 2)

    right = (d + 1) & (LEAF_COUNT - 1)
    left = (d + LEAF_COUNT - 1) & (LEAF_COUNT - 1)
    sibling = d + 1 - 2 * c
    column_peers = [(d + ROW * k) & (LEAF_COUNT - 1) for k in (4, 3, 5, 2, 1, 6, 7)]
    vec_peers = [(x + k) & 3 for k in (2, 1, 3)]

    barrier = pltpu.get_barrier_semaphore()

    def announce(leaf, vec):
        pl.semaphore_signal(barrier, inc=1, device_id={"leaf": leaf, "vec": vec}, device_id_type=MESH)

    @pl.when(z < 4)
    def _():
        for k in range(1, 8):
            announce(ROW * y + 2 * ((z + k) & 7), x)

    @pl.when(z >= 4)
    def _():
        for k in range(1, 8):
            announce(ROW * y + 2 * ((z + k) & 7) + 1, x)

    announce(sibling, x)
    near_start = z < 4
    announce((d + jnp.where(c == 0, LEAF_COUNT - 2 + (z >> 2), jnp.where(z == 7, 2, 1))) & (LEAF_COUNT - 1), x)
    for peer in vec_peers:
        announce(d - c + (z >> 2), peer)
    for peer in column_peers:
        announce(peer - c + 1, x)

    ends = jnp.where(jnp.logical_or(z == 0, z == 3), 1, 0)
    last = jnp.where(z == 7, 1, 0)
    count_0 = jnp.where(near_start, 15 - ends, 10 + last)
    count_1 = jnp.where(near_start, 23 + ends, 28 - last)

    def tell(flag):
        pl.semaphore_signal(flag, inc=1, device_id={"leaf": sibling, "vec": x}, device_id_type=MESH)

    ut_in = [
        load(ut_h.at[:, pl.ds(pl.multiple_of(1024 * y, 128), 1024)], ut_v.at[:, 0:1024], 3),
        load(ut_h.at[:, pl.ds(pl.multiple_of(8192 + 512 * y, 128), 512)], ut_v.at[:, 1024:1536], 4),
        load(ut_h.at[:, pl.ds(pl.multiple_of(12288 + 256 * y, 128), 256)], ut_v.at[:, 1536:1792], 5),
        load(ut_h.at[:, pl.ds(pl.multiple_of(14336 + 128 * y, 128), 128)], ut_v.at[:, 1792:1920], 6),
        load(ut_h.at[:, 15360:15872], ut_v.at[:, 1920:2432], 7),
    ]

    def send(src, dst, n_send, n_recv, leaf, vec):
        copy = pltpu.make_async_remote_copy(
            src_ref=src, dst_ref=dst, send_sem=send_sem.at[n_send], recv_sem=recv_sem.at[n_recv],
            device_id={"leaf": leaf, "vec": vec}, device_id_type=MESH,
        )
        copy.start()
        return copy

    def wait_for(ref, sem):
        pltpu.make_async_copy(ref, ref, sem).wait()

    vec_in.wait()
    basis_in.wait()
    lt_in.wait()
    transfer = lt_v[:, 1792:1920]
    crossed = turned(transfer)
    top = (halves(transfer, crossed), halves(crossed, transfer))

    zero = jnp.zeros((16, 128), BF)
    leaves = []
    for j in range(8):
        tile = arrived[1, own, 128 * j : 128 * j + 128]
        block = basis_v[:, 128 * j : 128 * j + 128]
        leaves.append(nt(rows(halves(tile, zero), halves(zero, tile)), rows(block, block)))
    current = []
    for j in range(8):
        coeff = leaves[j]
        first, second = coeff[0:16], coeff[16:32]
        coeffs[8 + j, 0] = halves(first, second).astype(BF)
        coeffs[8 + j, 1] = halves(second, first).astype(BF)
        transfer = lt_v[:, 128 * j : 128 * j + 128]
        lifted = nn(hilo(coeff), rows(transfer, transfer))
        current.append(halves(lifted[0:16], lifted[16:32]))
    for start in (1024, 1536):
        following = []
        for m in range(len(current) // 2):
            hi, lo = two_terms(rows(current[2 * m], current[2 * m + 1]))
            transfer = lt_v[:, start + 128 * m : start + 128 * m + 128]
            lifted = nn(lanes(hi, lo), rows(transfer, transfer, transfer, transfer))
            following.append(halves(lifted[0:16], lifted[16:32]))
        current = following
    first_hi, first_lo = two_terms(current[0])
    second_hi, second_lo = two_terms(current[1])
    root = nn(lanes(first_hi, first_lo, second_hi, second_lo), rows(*([top[0]] * 4 + [top[1]] * 4)))
    root_tile[...] = hilo(root)
    nodes[i] = root_tile[...]

    @pl.when(c == 0)
    def _():
        pl.semaphore_wait(barrier, count_0)
        tell(flag_0)

    @pl.when(c == 1)
    def _():
        pl.semaphore_wait(flag_0, 1)

    def send_root(t):
        send(root_tile, nodes.at[i], 1, 1, ROW * y + t, x)

    def to_vec_peers():
        for peer in vec_peers:
            send(vec_h, arrived.at[1, own], 0, 0, d, peer)

    def far_right():
        send(coeffs.at[8:16, 0], coeffs.at[0:8, 0], 2, 2, right, x)

    def far_left():
        send(coeffs.at[8:16, 0], coeffs.at[16:24, 0], 3, 3, left, x)

    def near_right():
        send(arrived.at[1], arrived.at[0], 4, 4, right, x)

    def near_left():
        send(arrived.at[1], arrived.at[2], 5, 5, left, x)

    row_end = jnp.logical_and(c == 1, z == 7)
    row_start = jnp.logical_and(c == 0, z == 0)
    left_now = jnp.logical_and(near_start, jnp.logical_or(c == 1, z > 0))
    right_now = jnp.logical_and(near_start, jnp.logical_or(c == 0, z < 3))
    right_later = jnp.logical_not(jnp.logical_or(right_now, row_end))

    for k in range(1, 8):
        send_root((i + k) & 7)

    @pl.when(z >= 4)
    def _():
        send_root(i & 7)

    @pl.when(row_end)
    def _():
        send(vec_h, arrived.at[0, own], 10, 4, right, x)
        far_right()

    @pl.when(near_start)
    def _():
        to_vec_peers()

    @pl.when(left_now)
    def _():
        far_left()

    @pl.when(right_now)
    def _():
        far_right()

    @pl.when(near_start)
    def _():
        wait_for(arrived.at[1, 0:48], recv_sem.at[0])

    @pl.when(left_now)
    def _():
        near_left()

    @pl.when(right_now)
    def _():
        near_right()

    uc_in = load(uc_h, uc_v, 8)
    lc_in = load(lc_h, lc_v, 9)
    far_in_s = load(far_h, far_s, 10)
    near_in_s = load(near_h, near_s, 11)
    tiles_in = load(tiles_h, tiles_v, 12)

    for copy in ut_in:
        copy.wait()
    for p in range(19):
        pair = ut_v[:, 128 * p : 128 * p + 128]
        swapped = turned(pair)
        dup[2 * p] = halves(pair, swapped)
        dup[2 * p + 1] = halves(swapped, pair)

    path = dup[i]
    path_hi[0] = path
    path = path.astype(F32)
    below = [(top[0], None), (top[1], None)]

    def path_step(path, u):
        matrix = dup[BASES[u] + (i >> u if u < 4 else y)]
        path = nn(hilo(path), rows(matrix, matrix))
        path_hi[u], path_lo[u] = two_terms(path)
        return path

    def product_step(below, start):
        following = []
        for m, (hi, lo) in enumerate(below):
            pair = lt_v[:, start + 128 * m : start + 128 * m + 128]
            none = jnp.zeros_like(pair)
            left_side = rows(halves(pair, none), halves(none, pair))
            if lo is None:
                product = nn(left_side, rows(hi, hi))
            else:
                product = nn(lanes(left_side, left_side), rows(hi, hi, lo, lo))
            hi, lo = two_terms(product)
            if start == 0:
                r0_hi[m] = hi
                r0_lo[m] = lo
            following += [(hi[0:64], lo[0:64]), (hi[64:128], lo[64:128])]
        return following

    for u, start in ((1, 1536), (2, 1024), (3, 0)):
        path = path_step(path, u)
        below = product_step(below, start)
    path_step(path, 4)

    def fold(j, carry):
        at = pl.ds(pl.multiple_of(128 * j, 128), 128)
        block = diagonal(basis_v[:, at])
        hi, lo = two_terms(tn(r0_hi[j], block) + tn(r0_lo[j], block))
        to_points[0:128, at] = hi
        to_points[128:256, at] = lo
        return carry

    lax.fori_loop(0, 8, fold, 0, unroll=2)

    uc_in.wait()
    couplings = rows(uc_v[...], uc_v[...])
    for e in range(2):
        value = nn(halves(path_hi[3 + e], path_lo[3 + e]), couplings)
        value = jnp.transpose(rows(value, value))
        for o in range(4):
            lifted_couplings[e, o] = value[64 * o : 64 * o + 64]

    def slot(offset, odd):
        index = jnp.where(offset == -3, 0, jnp.where(offset == -2, 1, jnp.where(offset == 2, 2, 3)))
        wide = jnp.logical_or(
            jnp.logical_and(offset == -3, odd == 1), jnp.logical_and(offset == 3, odd == 0)
        )
        valid = jnp.logical_or(jnp.logical_or(offset == -2, offset == 2), wide)
        return index, jnp.where(valid, 1.0, 0.0).astype(F32)

    def gather_top(n, carry):
        index, keep = slot(n - y, y & 1)
        value = lifted_couplings[0, index] * keep
        index, keep = slot((n >> 1) - (y >> 1), (y >> 1) & 1)
        hi, lo = two_terms(lifted_couplings[1, index] * keep)
        hi, lo = two_terms(value + nn(dup[30 + n], rows(hi, lo)))
        from_top[0, n] = rows(hi, hi)
        from_top[1, n] = rows(lo, lo)
        return carry

    lax.fori_loop(0, 8, gather_top, 0, unroll=4)

    def fill(w):
        def step(j, carry):
            block = arrived[w, :, pl.ds(pl.multiple_of(128 * j, 128), 128)]
            points[8 * w + j, 0] = block
            points[8 * w + j, 1] = turned(block)
            return carry

        lax.fori_loop(0, 8, step, 0, unroll=2)

    @pl.when(c == 1)
    def _():
        pl.semaphore_wait(barrier, count_1)
        tell(flag_1)

    @pl.when(c == 0)
    def _():
        pl.semaphore_wait(flag_1, 1)

    for k in range(1, 8):
        send_root(8 + ((i + k) & 7))

    @pl.when(z < 4)
    def _():
        send_root(8 + i)

    @pl.when(z >= 4)
    def _():
        to_vec_peers()

    @pl.when(jnp.logical_not(left_now))
    def _():
        far_left()

    @pl.when(right_later)
    def _():
        far_right()

    @pl.when(z >= 4)
    def _():
        wait_for(arrived.at[1, 0:48], recv_sem.at[0])

    @pl.when(jnp.logical_not(left_now))
    def _():
        near_left()

    @pl.when(right_later)
    def _():
        near_right()

    fill(1)

    first_leaf = ROW * d - ROW

    def chosen(table, lists, slots, column):
        parts = []
        for s in range(0, slots, 2):
            a = jnp.clip(lists[s, column] - first_leaf, 0, 3 * ROW - 1)
            b = jnp.clip(lists[s + 1, column] - first_leaf, 0, 3 * ROW - 1)
            parts.append(halves(table[a >> 1, a & 1], table[b >> 1, 1 - (b & 1)]))
        return lanes(*parts)

    def far_part():
        far_in_s.wait()
        lc_in.wait()
        wait_for(coeffs.at[0:8, 0], recv_sem.at[2])
        wait_for(coeffs.at[16:24, 0], recv_sem.at[3])
        for p in list(range(8)) + list(range(16, 24)):
            coeffs[p, 1] = turned(coeffs[p, 0])
        for j in range(8):
            source = rows(*[chosen(coeffs, far_s, 6, 2 * j + e) for e in range(2)])
            value = nt(source, rows(lc_v[:, 768 * j : 768 * j + 384], lc_v[:, 768 * j + 384 : 768 * j + 768]))
            hi, lo = two_terms(halves(value[0:16], value[16:32]))
            block = diagonal(basis_v[:, 128 * j : 128 * j + 128])
            far_out[j] = nn(lanes(hi, lo), rows(block, block))

    def near_part():
        near_in_s.wait()
        tiles_in.wait()

        @pl.when(row_start)
        def _():
            wait_for(arrived.at[0, 0:48], recv_sem.at[10])

        @pl.when(jnp.logical_not(row_start))
        def _():
            wait_for(arrived.at[0], recv_sem.at[4])

        wait_for(arrived.at[2], recv_sem.at[5])
        fill(0)
        fill(2)
        for q in range(2):
            source = rows(*[chosen(points, near_s, 6, 4 * x + 2 * q + e) for e in range(2)])
            value = nt(source, rows(tiles_v[2 * q], tiles_v[2 * q + 1]))
            value = halves(value[0:64], value[64:128]).astype(BF)
            for v in range(4):
                near_out[v, q] = value[16 * v : 16 * v + 16]
        for n, peer in enumerate(vec_peers):
            send(near_out.at[peer], near_in.at[x], 9, 9, d, peer)
        near_in[x] = near_out[x]

    wait_for(nodes.at[0:15], recv_sem.at[1])

    @pl.when(row_start)
    def _():
        wait_for(arrived.at[0, 0:16], recv_sem.at[4])
        for peer in vec_peers:
            send(arrived.at[0, own], arrived.at[0, own], 10, 10, d, peer)

    for u in range(4):
        base, count = BASES[u], ROW >> u
        for m in range(count // 2):
            left_m, right_m = dup[base + 2 * m], dup[base + 2 * m + 1]
            value = nn(lanes(nodes[base + 2 * m], nodes[base + 2 * m + 1]), rows(left_m, left_m, right_m, right_m))
            if u < 3:
                nodes[BASES[u + 1] + m] = hilo(value)
            else:
                top_tile = hilo(value)
                nodes[30 + y] = top_tile
                heads[8] = top_tile
                tails[8] = top_tile
    for u in range(4):
        for e in range(2):
            heads[2 * u + e] = nodes[BASES[u] + e]
            tails[2 * u + e] = nodes[BASES[u + 1] - 2 + e]
    send(tails, nodes.at[PREV : PREV + 9], 6, 6, column_peers[4], x)
    send(heads, nodes.at[NEXT : NEXT + 9], 7, 7, column_peers[6], x)
    for peer in column_peers[:4] + column_peers[5:6]:
        send(nodes.at[30 + y], nodes.at[30 + y], 8, 8, peer, x)

    near_part()
    far_part()

    weights = []
    for o in range(2):
        pair = uc_v[:, 128 * o : 128 * o + 128]
        swapped = turned(pair)
        weights += [halves(pair, swapped), halves(swapped, pair)]
    weights = lanes(*weights)
    wait_for(nodes.at[0:9], recv_sem.at[6])
    wait_for(nodes.at[0:9], recv_sem.at[7])
    sources = []
    for u in range(4):
        g = d >> u
        odd = g & 1
        number = LEAF_COUNT >> u
        count = ROW >> u
        parts = []
        for o, wanted in ((-3, odd == 1), (-2, None), (2, None), (3, odd == 0)):
            shift = o if wanted is None else (-3 * odd if o < 0 else 3 * (1 - odd))
            place = (i >> u) + shift
            place = jnp.where(
                place < 0,
                PREV + 2 + 2 * u + place,
                jnp.where(place < count, BASES[u] + place, NEXT + 2 * u - count + place),
            )
            valid = (g + o >= 0) if o < 0 else (g + o < number)
            if wanted is not None:
                valid = jnp.logical_and(valid, wanted)
            keep = jnp.where(valid, 1.0, 0.0).astype(F32)
            parts.append((nodes[place].astype(F32) * keep).astype(BF))
        sources.append(lanes(*parts))
    coupled = nt(rows(*sources), rows(weights, weights))
    left_side, right_side = [], []
    for u in range(1, 4):
        tile = hilo(coupled[16 * u : 16 * u + 16])
        left_side.append(tile)
        right_side.append(path_hi[u - 1])
        if u > 1:
            left_side.append(tile)
            right_side.append(path_lo[u - 1])
    matrix = lanes(*right_side)
    down = coupled[0:16] + nt(lanes(*left_side), rows(matrix, matrix))

    nodes[30 + ((y + 7) & 7)] = nodes[PREV + 8]
    nodes[30 + ((y + 1) & 7)] = nodes[NEXT + 8]
    wait_for(nodes.at[0:5], recv_sem.at[8])
    tops = lanes(*[nodes[30 + n] for n in range(8)])
    down = down + nn(tops, from_top[0].reshape(1024, 128)) + nn(tops, from_top[1].reshape(1024, 128))
    down = hilo(down)
    value = nn(lanes(down, down), to_points[...])
    wait_for(near_in.at[0:3], recv_sem.at[9])
    for j in range(8):
        at = slice(128 * j, 128 * j + 128)
        out_ref[:, at] = (value[:, at] + far_out[j] + near_in[j // 2, j % 2].astype(F32)).astype(BF)

    wait_for(arrived.at[1, 0:48], send_sem.at[0])
    wait_for(nodes.at[0:15], send_sem.at[1])
    wait_for(coeffs.at[0:8, 0], send_sem.at[2])
    wait_for(coeffs.at[0:8, 0], send_sem.at[3])

    @pl.when(row_end)
    def _():
        wait_for(arrived.at[0, 0:16], send_sem.at[10])

    @pl.when(row_start)
    def _():
        wait_for(arrived.at[0, 0:48], send_sem.at[10])

    @pl.when(jnp.logical_not(row_end))
    def _():
        wait_for(arrived.at[0], send_sem.at[4])

    wait_for(arrived.at[2], send_sem.at[5])
    wait_for(nodes.at[0:9], send_sem.at[6])
    wait_for(nodes.at[0:9], send_sem.at[7])
    wait_for(nodes.at[0:5], send_sem.at[8])
    wait_for(near_out.at[0:3], send_sem.at[9])


def shards(vectors, leaf_basis, local_transfer, upper_transfer, upper_coupling, leaf_coupling, far_list, near_list, near_tiles):
    tile = (16, 128)
    scratch = [
        pltpu.VMEM(leaf_basis.shape, BF),
        pltpu.VMEM(local_transfer.shape, BF),
        pltpu.VMEM((64, 2432), BF),
        pltpu.VMEM(upper_coupling.shape, BF),
        pltpu.VMEM(leaf_coupling.shape, BF),
        pltpu.SMEM(far_list.shape, jnp.int32),
        pltpu.SMEM(near_list.shape, jnp.int32),
        pltpu.VMEM(near_tiles.shape, BF),
        pltpu.VMEM((3, 64, 1024), BF),
        pltpu.VMEM((24, 2, 64, 128), BF),
        pltpu.VMEM((24, 2) + tile, BF),
        pltpu.VMEM(tile, BF),
        pltpu.VMEM((60,) + tile, BF),
        pltpu.VMEM((9,) + tile, BF),
        pltpu.VMEM((9,) + tile, BF),
        pltpu.VMEM((38, 64, 128), BF),
        pltpu.VMEM((5, 64, 128), BF),
        pltpu.VMEM((5, 64, 128), BF),
        pltpu.VMEM((8, 128, 128), BF),
        pltpu.VMEM((8, 128, 128), BF),
        pltpu.VMEM((256, 1024), BF),
        pltpu.VMEM((2, 4, 64, 128), F32),
        pltpu.VMEM((2, 8, 128, 128), BF),
        pltpu.VMEM((8,) + tile, F32),
        pltpu.VMEM((4, 2) + tile, BF),
        pltpu.VMEM((4, 2) + tile, BF),
        pltpu.SemaphoreType.DMA((13,)),
        pltpu.SemaphoreType.DMA((11,)),
        pltpu.SemaphoreType.DMA((11,)),
        pltpu.SemaphoreType.REGULAR,
        pltpu.SemaphoreType.REGULAR,
    ]
    return pl.pallas_call(
        kernel,
        out_shape=pltpu.VMEM(vectors.shape, BF),
        in_specs=[pl.BlockSpec(memory_space=pl.ANY)] * 9,
        out_specs=pl.BlockSpec(memory_space=pltpu.VMEM),
        scratch_shapes=scratch,
        compiler_params=pltpu.CompilerParams(
            collective_id=0, has_side_effects=True, vmem_limit_bytes=62 * 1024 * 1024
        ),
    )(vectors, leaf_basis, local_transfer, upper_transfer, upper_coupling, leaf_coupling, far_list, near_list, near_tiles)


def solution(mesh):
    placed = (
        P("vec", "leaf"),
        P(None, "leaf"),
        P(None, "leaf"),
        P(),
        P(),
        P(None, "leaf"),
        P(None, "leaf"),
        P(None, "leaf"),
        P(("leaf", "vec"), None, None),
    )
    return jax.shard_map(
        shards, mesh=mesh, in_specs=placed, out_specs=P("vec", "leaf"), check_vma=False
    )
```

```python
import jax
import jax.numpy as jnp
from jax import lax
from jax.experimental import pallas as pl
from jax.experimental.pallas import tpu as pltpu
from jax.sharding import PartitionSpec as P

MESH = pl.DeviceIdType.MESH
BF = jnp.bfloat16
F32 = jnp.float32
ROW = 16
ROWS = 8
LEAF_COUNT = ROW * ROWS
BASES = (0, 16, 24, 28, 30)
PREV = 42
NEXT = 51


def low(shape):
    return lax.broadcasted_iota(jnp.int32, shape, 1) < 64


def halves(a, b):
    return jnp.where(low(a.shape), a, b)


def turned(tile):
    return pltpu.roll(tile, 64, 1)


def rounded(x):
    return x.astype(BF).astype(F32)


def hilo(x):
    hi = rounded(x)
    return halves(hi, x - hi).astype(BF)


def two_terms(x):
    hi = rounded(x)
    return hi.astype(BF), (x - hi).astype(BF)


def nn(a, b):
    return jnp.dot(a, b, preferred_element_type=F32)


def nt(a, b):
    return lax.dot_general(a, b, (((1,), (1,)), ((), ())), preferred_element_type=F32)


def tn(a, b):
    return lax.dot_general(a, b, (((0,), (0,)), ((), ())), preferred_element_type=F32)


def diagonal(block):
    none = jnp.zeros_like(block)
    return rows(halves(block, none), halves(none, block))


def rows(*parts):
    return jnp.concatenate(parts, axis=0)


def lanes(*parts):
    return jnp.concatenate(parts, axis=1)


def kernel(
    vec_h, basis_h, lt_h, ut_h, uc_h, lc_h, far_h, near_h, tiles_h, out_ref,
    basis_v, lt_v, ut_v, uc_v, lc_v, far_s, near_s, tiles_v,
    arrived, points, coeffs, root_tile, nodes, heads, tails,
    dup, path_hi, path_lo, r0_hi, r0_lo, to_points, lifted_couplings, from_top, from_row, far_out, near_out, near_in,
    in_sem, send_sem, recv_sem, flag_0, flag_1,
):
    d = lax.axis_index("leaf")
    x = lax.axis_index("vec")
    y = d >> 4
    i = d & 15
    z = i >> 1
    c = i & 1

    def load(src, dst, n):
        copy = pltpu.make_async_copy(src, dst, in_sem.at[n])
        copy.start()
        return copy

    own = pl.ds(pl.multiple_of(16 * x, 16), 16)
    vec_in = load(vec_h, arrived.at[1, own], 0)
    basis_in = load(basis_h, basis_v, 1)
    lt_in = load(lt_h, lt_v, 2)

    right = (d + 1) & (LEAF_COUNT - 1)
    left = (d + LEAF_COUNT - 1) & (LEAF_COUNT - 1)
    sibling = d + 1 - 2 * c
    column_peers = [(d + ROW * k) & (LEAF_COUNT - 1) for k in (4, 3, 5, 2, 1, 6, 7)]
    vec_peers = [(x + k) & 3 for k in (2, 1, 3)]

    barrier = pltpu.get_barrier_semaphore()

    def announce(leaf, vec):
        pl.semaphore_signal(barrier, inc=1, device_id={"leaf": leaf, "vec": vec}, device_id_type=MESH)

    @pl.when(z < 4)
    def _():
        for k in range(1, 8):
            announce(ROW * y + 2 * ((z + k) & 7), x)

    @pl.when(z >= 4)
    def _():
        for k in range(1, 8):
            announce(ROW * y + 2 * ((z + k) & 7) + 1, x)

    announce(sibling, x)
    near_start = z < 4
    announce((d + jnp.where(c == 0, LEAF_COUNT - 2 + (z >> 2), jnp.where(z == 7, 2, 1))) & (LEAF_COUNT - 1), x)
    for peer in vec_peers:
        announce(d - c + (z >> 2), peer)
    for peer in column_peers:
        announce(peer - c + 1, x)

    ends = jnp.where(jnp.logical_or(z == 0, z == 3), 1, 0)
    last = jnp.where(z == 7, 1, 0)
    count_0 = jnp.where(near_start, 15 - ends, 10 + last)
    count_1 = jnp.where(near_start, 23 + ends, 28 - last)

    def tell(flag):
        pl.semaphore_signal(flag, inc=1, device_id={"leaf": sibling, "vec": x}, device_id_type=MESH)

    @pl.when(jnp.logical_and(c == 0, z == 7))
    def _():
        pl.semaphore_wait(barrier, count_0)
        tell(flag_0)

    ut_in = [
        load(ut_h.at[:, pl.ds(pl.multiple_of(1024 * y, 128), 1024)], ut_v.at[:, 0:1024], 3),
        load(ut_h.at[:, pl.ds(pl.multiple_of(8192 + 512 * y, 128), 512)], ut_v.at[:, 1024:1536], 4),
        load(ut_h.at[:, pl.ds(pl.multiple_of(12288 + 256 * y, 128), 256)], ut_v.at[:, 1536:1792], 5),
        load(ut_h.at[:, pl.ds(pl.multiple_of(14336 + 128 * y, 128), 128)], ut_v.at[:, 1792:1920], 6),
        load(ut_h.at[:, 15360:15872], ut_v.at[:, 1920:2432], 7),
    ]

    def send(src, dst, n_send, n_recv, leaf, vec):
        copy = pltpu.make_async_remote_copy(
            src_ref=src, dst_ref=dst, send_sem=send_sem.at[n_send], recv_sem=recv_sem.at[n_recv],
            device_id={"leaf": leaf, "vec": vec}, device_id_type=MESH,
        )
        copy.start()
        return copy

    def wait_for(ref, sem):
        pltpu.make_async_copy(ref, ref, sem).wait()

    def send_root(t):
        send(root_tile, nodes.at[i], 1, 1, ROW * y + t, x)

    def to_vec_peers():
        for peer in vec_peers:
            send(vec_h, arrived.at[1, own], 0, 0, d, peer)

    def far_right():
        send(coeffs.at[8:16, 0], coeffs.at[0:8, 0], 2, 2, right, x)

    def far_left():
        send(coeffs.at[8:16, 0], coeffs.at[16:24, 0], 3, 3, left, x)

    def near_right():
        send(arrived.at[1], arrived.at[0], 4, 4, right, x)

    def near_left():
        send(arrived.at[1], arrived.at[2], 5, 5, left, x)

    row_end = jnp.logical_and(c == 1, z == 7)
    row_start = jnp.logical_and(c == 0, z == 0)
    left_now = jnp.logical_and(near_start, jnp.logical_or(c == 1, z > 0))
    right_now = jnp.logical_and(near_start, jnp.logical_or(c == 0, z < 3))
    right_later = jnp.logical_not(jnp.logical_or(right_now, row_end))

    vec_in.wait()
    basis_in.wait()
    lt_in.wait()
    transfer = lt_v[:, 1792:1920]
    crossed = turned(transfer)
    top = (halves(transfer, crossed), halves(crossed, transfer))

    zero = jnp.zeros((16, 128), BF)
    leaves = []
    for j in range(8):
        tile = arrived[1, own, 128 * j : 128 * j + 128]
        block = basis_v[:, 128 * j : 128 * j + 128]
        leaves.append(nt(rows(halves(tile, zero), halves(zero, tile)), rows(block, block)))
    for j in range(8):
        first, second = leaves[j][0:16], leaves[j][16:32]
        coeffs[8 + j, 0] = halves(first, second).astype(BF)
        coeffs[8 + j, 1] = halves(second, first).astype(BF)

    @pl.when(row_end)
    def _():
        pl.semaphore_wait(flag_0, 1)
        send(vec_h, arrived.at[0, own], 10, 4, right, x)
        far_right()

    current = []
    for j in range(8):
        transfer = lt_v[:, 128 * j : 128 * j + 128]
        lifted = nn(hilo(leaves[j]), rows(transfer, transfer))
        current.append(halves(lifted[0:16], lifted[16:32]))
    for start in (1024, 1536):
        following = []
        for m in range(len(current) // 2):
            hi, lo = two_terms(rows(current[2 * m], current[2 * m + 1]))
            transfer = lt_v[:, start + 128 * m : start + 128 * m + 128]
            lifted = nn(lanes(hi, lo), rows(transfer, transfer, transfer, transfer))
            following.append(halves(lifted[0:16], lifted[16:32]))
        current = following
    first_hi, first_lo = two_terms(current[0])
    second_hi, second_lo = two_terms(current[1])
    root = nn(lanes(first_hi, first_lo, second_hi, second_lo), rows(*([top[0]] * 4 + [top[1]] * 4)))
    root_tile[...] = hilo(root)
    nodes[i] = root_tile[...]

    @pl.when(jnp.logical_and(c == 0, z < 7))
    def _():
        pl.semaphore_wait(barrier, count_0)
        tell(flag_0)

    @pl.when(jnp.logical_and(c == 1, z < 7))
    def _():
        pl.semaphore_wait(flag_0, 1)

    for k in range(1, 8):
        send_root((i + k) & 7)

    @pl.when(z >= 4)
    def _():
        send_root(i & 7)

    @pl.when(near_start)
    def _():
        to_vec_peers()

    @pl.when(left_now)
    def _():
        far_left()

    @pl.when(right_now)
    def _():
        far_right()

    @pl.when(near_start)
    def _():
        wait_for(arrived.at[1, 0:48], recv_sem.at[0])

    @pl.when(left_now)
    def _():
        near_left()

    @pl.when(right_now)
    def _():
        near_right()

    uc_in = load(uc_h, uc_v, 8)
    lc_in = load(lc_h, lc_v, 9)
    far_in_s = load(far_h, far_s, 10)
    near_in_s = load(near_h, near_s, 11)
    tiles_in = load(tiles_h, tiles_v, 12)

    for copy in ut_in:
        copy.wait()
    for p in range(19):
        pair = ut_v[:, 128 * p : 128 * p + 128]
        swapped = turned(pair)
        dup[2 * p] = halves(pair, swapped)
        dup[2 * p + 1] = halves(swapped, pair)

    path = dup[i]
    path_hi[0] = path
    path = path.astype(F32)
    below = [(top[0], None), (top[1], None)]
    row_below = [(dup[28], None), (dup[29], None)]

    def path_step(path, u):
        matrix = dup[BASES[u] + (i >> u if u < 4 else y)]
        path = nn(hilo(path), rows(matrix, matrix))
        path_hi[u], path_lo[u] = two_terms(path)
        return path

    def product_step(below, transfers, start):
        following = []
        for m, (hi, lo) in enumerate(below):
            left_side = diagonal(transfers[:, start + 128 * m : start + 128 * m + 128])
            if lo is None:
                product = nn(left_side, rows(hi, hi))
            else:
                product = nn(lanes(left_side, left_side), rows(hi, hi, lo, lo))
            hi, lo = two_terms(product)
            following += [(hi[0:64], lo[0:64]), (hi[64:128], lo[64:128])]
        return following

    for u, start in ((1, 1536), (2, 1024), (3, 0)):
        path = path_step(path, u)
        below = product_step(below, lt_v, start)
        row_below = product_step(row_below, ut_v, start)
    path_step(path, 4)
    for m in range(8):
        r0_hi[m] = rows(below[2 * m][0], below[2 * m + 1][0])
        r0_lo[m] = rows(below[2 * m][1], below[2 * m + 1][1])
    for m, (hi, lo) in enumerate(row_below):
        from_row[0, m] = rows(hi, hi)
        from_row[1, m] = rows(lo, lo)

    def fold(j, carry):
        at = pl.ds(pl.multiple_of(128 * j, 128), 128)
        block = diagonal(basis_v[:, at])
        hi, lo = two_terms(tn(r0_hi[j], block) + tn(r0_lo[j], block))
        to_points[0:128, at] = hi
        to_points[128:256, at] = lo
        return carry

    lax.fori_loop(0, 8, fold, 0, unroll=2)

    uc_in.wait()
    couplings = rows(uc_v[...], uc_v[...])
    for e in range(2):
        value = nn(halves(path_hi[3 + e], path_lo[3 + e]), couplings)
        value = jnp.transpose(rows(value, value))
        for o in range(4):
            lifted_couplings[e, o] = value[64 * o : 64 * o + 64]

    def slot(offset, odd):
        index = jnp.where(offset == -3, 0, jnp.where(offset == -2, 1, jnp.where(offset == 2, 2, 3)))
        wide = jnp.logical_or(
            jnp.logical_and(offset == -3, odd == 1), jnp.logical_and(offset == 3, odd == 0)
        )
        valid = jnp.logical_or(jnp.logical_or(offset == -2, offset == 2), wide)
        return index, jnp.where(valid, 1.0, 0.0).astype(F32)

    def gather_top(n, carry):
        index, keep = slot(n - y, y & 1)
        value = lifted_couplings[0, index] * keep
        index, keep = slot((n >> 1) - (y >> 1), (y >> 1) & 1)
        hi, lo = two_terms(lifted_couplings[1, index] * keep)
        hi, lo = two_terms(value + nn(dup[30 + n], rows(hi, lo)))
        from_top[0, n] = rows(hi, hi)
        from_top[1, n] = rows(lo, lo)
        return carry

    lax.fori_loop(0, 8, gather_top, 0, unroll=4)

    def fill(w):
        def step(j, carry):
            block = arrived[w, :, pl.ds(pl.multiple_of(128 * j, 128), 128)]
            points[8 * w + j, 0] = block
            points[8 * w + j, 1] = turned(block)
            return carry

        lax.fori_loop(0, 8, step, 0, unroll=2)

    @pl.when(c == 1)
    def _():
        pl.semaphore_wait(barrier, count_1)
        tell(flag_1)

    @pl.when(c == 0)
    def _():
        pl.semaphore_wait(flag_1, 1)

    for k in range(1, 8):
        send_root(8 + ((i + k) & 7))

    @pl.when(z < 4)
    def _():
        send_root(8 + i)

    @pl.when(z >= 4)
    def _():
        to_vec_peers()

    @pl.when(jnp.logical_not(left_now))
    def _():
        far_left()

    @pl.when(right_later)
    def _():
        far_right()

    @pl.when(z >= 4)
    def _():
        wait_for(arrived.at[1, 0:48], recv_sem.at[0])

    @pl.when(jnp.logical_not(left_now))
    def _():
        near_left()

    @pl.when(right_later)
    def _():
        near_right()

    fill(1)

    first_leaf = ROW * d - ROW

    def chosen(table, lists, slots, column):
        parts = []
        for s in range(0, slots, 2):
            a = jnp.clip(lists[s, column] - first_leaf, 0, 3 * ROW - 1)
            b = jnp.clip(lists[s + 1, column] - first_leaf, 0, 3 * ROW - 1)
            parts.append(halves(table[a >> 1, a & 1], table[b >> 1, 1 - (b & 1)]))
        return lanes(*parts)

    def far_part():
        far_in_s.wait()
        lc_in.wait()
        wait_for(coeffs.at[0:8, 0], recv_sem.at[2])
        wait_for(coeffs.at[16:24, 0], recv_sem.at[3])
        for p in list(range(8)) + list(range(16, 24)):
            coeffs[p, 1] = turned(coeffs[p, 0])
        for j in range(8):
            source = rows(*[chosen(coeffs, far_s, 6, 2 * j + e) for e in range(2)])
            value = nt(source, rows(lc_v[:, 768 * j : 768 * j + 384], lc_v[:, 768 * j + 384 : 768 * j + 768]))
            hi, lo = two_terms(halves(value[0:16], value[16:32]))
            block = diagonal(basis_v[:, 128 * j : 128 * j + 128])
            far_out[j] = nn(lanes(hi, lo), rows(block, block))

    def near_part():
        near_in_s.wait()
        tiles_in.wait()

        @pl.when(row_start)
        def _():
            wait_for(arrived.at[0, 0:48], recv_sem.at[10])

        @pl.when(jnp.logical_not(row_start))
        def _():
            wait_for(arrived.at[0], recv_sem.at[4])

        wait_for(arrived.at[2], recv_sem.at[5])
        fill(0)
        fill(2)
        for q in range(2):
            source = rows(*[chosen(points, near_s, 6, 4 * x + 2 * q + e) for e in range(2)])
            value = nt(source, rows(tiles_v[2 * q], tiles_v[2 * q + 1]))
            value = halves(value[0:64], value[64:128]).astype(BF)
            for v in range(4):
                near_out[v, q] = value[16 * v : 16 * v + 16]
        for n, peer in enumerate(vec_peers):
            send(near_out.at[peer], near_in.at[x], 9, 9, d, peer)
        near_in[x] = near_out[x]

    wait_for(nodes.at[0:15], recv_sem.at[1])

    @pl.when(row_start)
    def _():
        wait_for(arrived.at[0, 0:16], recv_sem.at[4])
        for peer in vec_peers:
            send(arrived.at[0, own], arrived.at[0, own], 10, 10, d, peer)

    roots = lanes(*[nodes[m] for m in range(ROW)])
    top_tile = hilo(nn(roots, from_row[0].reshape(2048, 128)) + nn(roots, from_row[1].reshape(2048, 128)))
    nodes[30 + y] = top_tile
    heads[8] = top_tile
    tails[8] = top_tile
    for peer in column_peers[:4] + column_peers[5:6]:
        send(nodes.at[30 + y], nodes.at[30 + y], 8, 8, peer, x)
    for u in range(3):
        base, count = BASES[u], ROW >> u
        for m in range(count // 2):
            left_m, right_m = dup[base + 2 * m], dup[base + 2 * m + 1]
            value = nn(lanes(nodes[base + 2 * m], nodes[base + 2 * m + 1]), rows(left_m, left_m, right_m, right_m))
            nodes[BASES[u + 1] + m] = hilo(value)
    for u in range(4):
        for e in range(2):
            heads[2 * u + e] = nodes[BASES[u] + e]
            tails[2 * u + e] = nodes[BASES[u + 1] - 2 + e]
    send(tails, nodes.at[PREV : PREV + 9], 6, 6, column_peers[4], x)
    send(heads, nodes.at[NEXT : NEXT + 9], 7, 7, column_peers[6], x)

    near_part()
    far_part()

    weights = []
    for o in range(2):
        pair = uc_v[:, 128 * o : 128 * o + 128]
        swapped = turned(pair)
        weights += [halves(pair, swapped), halves(swapped, pair)]
    weights = lanes(*weights)
    wait_for(nodes.at[0:9], recv_sem.at[6])
    wait_for(nodes.at[0:9], recv_sem.at[7])
    sources = []
    for u in range(4):
        g = d >> u
        odd = g & 1
        number = LEAF_COUNT >> u
        count = ROW >> u
        parts = []
        for o, wanted in ((-3, odd == 1), (-2, None), (2, None), (3, odd == 0)):
            shift = o if wanted is None else (-3 * odd if o < 0 else 3 * (1 - odd))
            place = (i >> u) + shift
            place = jnp.where(
                place < 0,
                PREV + 2 + 2 * u + place,
                jnp.where(place < count, BASES[u] + place, NEXT + 2 * u - count + place),
            )
            valid = (g + o >= 0) if o < 0 else (g + o < number)
            if wanted is not None:
                valid = jnp.logical_and(valid, wanted)
            keep = jnp.where(valid, 1.0, 0.0).astype(F32)
            parts.append((nodes[place].astype(F32) * keep).astype(BF))
        sources.append(lanes(*parts))
    coupled = nt(rows(*sources), rows(weights, weights))
    left_side, right_side = [], []
    for u in range(1, 4):
        tile = hilo(coupled[16 * u : 16 * u + 16])
        left_side.append(tile)
        right_side.append(path_hi[u - 1])
        if u > 1:
            left_side.append(tile)
            right_side.append(path_lo[u - 1])
    matrix = lanes(*right_side)
    down = coupled[0:16] + nt(lanes(*left_side), rows(matrix, matrix))

    nodes[30 + ((y + 7) & 7)] = nodes[PREV + 8]
    nodes[30 + ((y + 1) & 7)] = nodes[NEXT + 8]
    wait_for(nodes.at[0:5], recv_sem.at[8])
    tops = lanes(*[nodes[30 + n] for n in range(8)])
    down = down + nn(tops, from_top[0].reshape(1024, 128)) + nn(tops, from_top[1].reshape(1024, 128))
    down = hilo(down)
    value = nn(lanes(down, down), to_points[...])
    wait_for(near_in.at[0:3], recv_sem.at[9])
    for j in range(8):
        at = slice(128 * j, 128 * j + 128)
        out_ref[:, at] = (value[:, at] + far_out[j] + near_in[j // 2, j % 2].astype(F32)).astype(BF)

    wait_for(arrived.at[1, 0:48], send_sem.at[0])
    wait_for(nodes.at[0:15], send_sem.at[1])
    wait_for(coeffs.at[0:8, 0], send_sem.at[2])
    wait_for(coeffs.at[0:8, 0], send_sem.at[3])

    @pl.when(row_end)
    def _():
        wait_for(arrived.at[0, 0:16], send_sem.at[10])

    @pl.when(row_start)
    def _():
        wait_for(arrived.at[0, 0:48], send_sem.at[10])

    @pl.when(jnp.logical_not(row_end))
    def _():
        wait_for(arrived.at[0], send_sem.at[4])

    wait_for(arrived.at[2], send_sem.at[5])
    wait_for(nodes.at[0:9], send_sem.at[6])
    wait_for(nodes.at[0:9], send_sem.at[7])
    wait_for(nodes.at[0:5], send_sem.at[8])
    wait_for(near_out.at[0:3], send_sem.at[9])


def shards(vectors, leaf_basis, local_transfer, upper_transfer, upper_coupling, leaf_coupling, far_list, near_list, near_tiles):
    tile = (16, 128)
    scratch = [
        pltpu.VMEM(leaf_basis.shape, BF),
        pltpu.VMEM(local_transfer.shape, BF),
        pltpu.VMEM((64, 2432), BF),
        pltpu.VMEM(upper_coupling.shape, BF),
        pltpu.VMEM(leaf_coupling.shape, BF),
        pltpu.SMEM(far_list.shape, jnp.int32),
        pltpu.SMEM(near_list.shape, jnp.int32),
        pltpu.VMEM(near_tiles.shape, BF),
        pltpu.VMEM((3, 64, 1024), BF),
        pltpu.VMEM((24, 2, 64, 128), BF),
        pltpu.VMEM((24, 2) + tile, BF),
        pltpu.VMEM(tile, BF),
        pltpu.VMEM((60,) + tile, BF),
        pltpu.VMEM((9,) + tile, BF),
        pltpu.VMEM((9,) + tile, BF),
        pltpu.VMEM((38, 64, 128), BF),
        pltpu.VMEM((5, 64, 128), BF),
        pltpu.VMEM((5, 64, 128), BF),
        pltpu.VMEM((8, 128, 128), BF),
        pltpu.VMEM((8, 128, 128), BF),
        pltpu.VMEM((256, 1024), BF),
        pltpu.VMEM((2, 4, 64, 128), F32),
        pltpu.VMEM((2, 8, 128, 128), BF),
        pltpu.VMEM((2, ROW, 128, 128), BF),
        pltpu.VMEM((8,) + tile, F32),
        pltpu.VMEM((4, 2) + tile, BF),
        pltpu.VMEM((4, 2) + tile, BF),
        pltpu.SemaphoreType.DMA((13,)),
        pltpu.SemaphoreType.DMA((11,)),
        pltpu.SemaphoreType.DMA((11,)),
        pltpu.SemaphoreType.REGULAR,
        pltpu.SemaphoreType.REGULAR,
    ]
    return pl.pallas_call(
        kernel,
        out_shape=pltpu.VMEM(vectors.shape, BF),
        in_specs=[pl.BlockSpec(memory_space=pl.ANY)] * 9,
        out_specs=pl.BlockSpec(memory_space=pltpu.VMEM),
        scratch_shapes=scratch,
        compiler_params=pltpu.CompilerParams(
            collective_id=0, has_side_effects=True, vmem_limit_bytes=62 * 1024 * 1024
        ),
    )(vectors, leaf_basis, local_transfer, upper_transfer, upper_coupling, leaf_coupling, far_list, near_list, near_tiles)


def solution(mesh):
    placed = (
        P("vec", "leaf"),
        P(None, "leaf"),
        P(None, "leaf"),
        P(),
        P(),
        P(None, "leaf"),
        P(None, "leaf"),
        P(None, "leaf"),
        P(("leaf", "vec"), None, None),
    )
    return jax.shard_map(
        shards, mesh=mesh, in_specs=placed, out_specs=P("vec", "leaf"), check_vma=False
    )
```

```python
import jax
import jax.numpy as jnp
from jax import lax
from jax.experimental import pallas as pl
from jax.experimental.pallas import tpu as pltpu
from jax.sharding import PartitionSpec as P

MESH = pl.DeviceIdType.MESH
BF = jnp.bfloat16
F32 = jnp.float32
ROW = 16
ROWS = 8
LEAF_COUNT = ROW * ROWS
BASES = (0, 16, 24, 28, 30)
PREV = 42
NEXT = 51


def low(shape):
    return lax.broadcasted_iota(jnp.int32, shape, 1) < 64


def halves(a, b):
    return jnp.where(low(a.shape), a, b)


def turned(tile):
    return pltpu.roll(tile, 64, 1)


def rounded(x):
    return x.astype(BF).astype(F32)


def hilo(x):
    hi = rounded(x)
    return halves(hi, x - hi).astype(BF)


def two_terms(x):
    hi = rounded(x)
    return hi.astype(BF), (x - hi).astype(BF)


def nn(a, b):
    return jnp.dot(a, b, preferred_element_type=F32)


def nt(a, b):
    return lax.dot_general(a, b, (((1,), (1,)), ((), ())), preferred_element_type=F32)


def tn(a, b):
    return lax.dot_general(a, b, (((0,), (0,)), ((), ())), preferred_element_type=F32)


def diagonal(block):
    none = jnp.zeros_like(block)
    return rows(halves(block, none), halves(none, block))


def rows(*parts):
    return jnp.concatenate(parts, axis=0)


def lanes(*parts):
    return jnp.concatenate(parts, axis=1)


def kernel(
    vec_h, basis_h, lt_h, ut_h, uc_h, lc_h, far_h, near_h, tiles_h, out_ref,
    basis_v, lt_v, ut_v, uc_v, lc_v, far_s, near_s, tiles_v,
    arrived, points, coeffs, root_tile, nodes, heads, tails,
    dup, path_hi, path_lo, r0_hi, r0_lo, to_points, lifted_couplings, from_top, from_row, far_out, near_out, near_in,
    in_sem, send_sem, recv_sem, flag_0, flag_1,
):
    d = lax.axis_index("leaf")
    x = lax.axis_index("vec")
    y = d >> 4
    i = d & 15
    z = i >> 1
    c = i & 1

    def load(src, dst, n):
        copy = pltpu.make_async_copy(src, dst, in_sem.at[n])
        copy.start()
        return copy

    own = pl.ds(pl.multiple_of(16 * x, 16), 16)
    vec_in = load(vec_h, arrived.at[1, own], 0)
    basis_in = load(basis_h, basis_v, 1)
    lt_in = load(lt_h, lt_v, 2)

    right = (d + 1) & (LEAF_COUNT - 1)
    left = (d + LEAF_COUNT - 1) & (LEAF_COUNT - 1)
    sibling = d + 1 - 2 * c
    column_peers = [(d + ROW * k) & (LEAF_COUNT - 1) for k in (4, 3, 5, 2, 1, 6, 7)]
    vec_peers = [(x + k) & 3 for k in (2, 1, 3)]

    barrier = pltpu.get_barrier_semaphore()

    def announce(leaf, vec):
        pl.semaphore_signal(barrier, inc=1, device_id={"leaf": leaf, "vec": vec}, device_id_type=MESH)

    @pl.when(z < 4)
    def _():
        for k in range(1, 8):
            announce(ROW * y + 2 * ((z + k) & 7), x)

    @pl.when(z >= 4)
    def _():
        for k in range(1, 8):
            announce(ROW * y + 2 * ((z + k) & 7) + 1, x)

    announce(sibling, x)
    near_start = z < 4
    announce((d + jnp.where(c == 0, LEAF_COUNT - 2 + (z >> 2), jnp.where(z == 7, 2, 1))) & (LEAF_COUNT - 1), x)
    for peer in vec_peers:
        announce(d - c + (z >> 2), peer)
    for peer in column_peers:
        announce(peer - c + 1, x)

    ends = jnp.where(jnp.logical_or(z == 0, z == 3), 1, 0)
    last = jnp.where(z == 7, 1, 0)
    count_0 = jnp.where(near_start, 15 - ends, 10 + last)
    count_1 = jnp.where(near_start, 23 + ends, 28 - last)

    def tell(flag):
        pl.semaphore_signal(flag, inc=1, device_id={"leaf": sibling, "vec": x}, device_id_type=MESH)

    @pl.when(jnp.logical_and(c == 0, z == 7))
    def _():
        pl.semaphore_wait(barrier, count_0)
        tell(flag_0)

    ut_in = [
        load(ut_h.at[:, pl.ds(pl.multiple_of(1024 * y, 128), 1024)], ut_v.at[:, 0:1024], 3),
        load(ut_h.at[:, pl.ds(pl.multiple_of(8192 + 512 * y, 128), 512)], ut_v.at[:, 1024:1536], 4),
        load(ut_h.at[:, pl.ds(pl.multiple_of(12288 + 256 * y, 128), 256)], ut_v.at[:, 1536:1792], 5),
        load(ut_h.at[:, pl.ds(pl.multiple_of(14336 + 128 * y, 128), 128)], ut_v.at[:, 1792:1920], 6),
        load(ut_h.at[:, 15360:15872], ut_v.at[:, 1920:2432], 7),
    ]

    def send(src, dst, n_send, n_recv, leaf, vec):
        copy = pltpu.make_async_remote_copy(
            src_ref=src, dst_ref=dst, send_sem=send_sem.at[n_send], recv_sem=recv_sem.at[n_recv],
            device_id={"leaf": leaf, "vec": vec}, device_id_type=MESH,
        )
        copy.start()
        return copy

    def wait_for(ref, sem):
        pltpu.make_async_copy(ref, ref, sem).wait()

    def send_root(t):
        send(root_tile, nodes.at[i], 1, 1, ROW * y + t, x)

    def to_vec_peers():
        for peer in vec_peers:
            send(vec_h, arrived.at[1, own], 0, 0, d, peer)

    def far_right():
        send(coeffs.at[8:16, 0], coeffs.at[0:8, 0], 2, 2, right, x)

    def far_left():
        send(coeffs.at[8:16, 0], coeffs.at[16:24, 0], 3, 3, left, x)

    def near_right():
        send(arrived.at[1], arrived.at[0], 4, 4, right, x)

    def near_left():
        send(arrived.at[1], arrived.at[2], 5, 5, left, x)

    row_end = jnp.logical_and(c == 1, z == 7)
    row_start = jnp.logical_and(c == 0, z == 0)
    left_now = jnp.logical_and(near_start, jnp.logical_or(c == 1, z > 0))
    right_now = jnp.logical_and(near_start, jnp.logical_or(c == 0, z < 3))
    left_later = jnp.logical_not(jnp.logical_or(left_now, row_start))
    right_later = jnp.logical_not(jnp.logical_or(right_now, row_end))

    vec_in.wait()
    basis_in.wait()
    lt_in.wait()
    transfer = lt_v[:, 1792:1920]
    crossed = turned(transfer)
    top = (halves(transfer, crossed), halves(crossed, transfer))

    zero = jnp.zeros((16, 128), BF)
    leaves = []
    for j in range(8):
        tile = arrived[1, own, 128 * j : 128 * j + 128]
        block = basis_v[:, 128 * j : 128 * j + 128]
        leaves.append(nt(rows(halves(tile, zero), halves(zero, tile)), rows(block, block)))
    for j in range(8):
        first, second = leaves[j][0:16], leaves[j][16:32]
        coeffs[8 + j, 0] = halves(first, second).astype(BF)
        coeffs[8 + j, 1] = halves(second, first).astype(BF)

    @pl.when(row_end)
    def _():
        pl.semaphore_wait(flag_0, 1)
        send(vec_h, arrived.at[0, own], 10, 4, right, x)
        far_right()

    current = []
    for j in range(8):
        transfer = lt_v[:, 128 * j : 128 * j + 128]
        lifted = nn(hilo(leaves[j]), rows(transfer, transfer))
        current.append(halves(lifted[0:16], lifted[16:32]))
    for start in (1024, 1536):
        following = []
        for m in range(len(current) // 2):
            hi, lo = two_terms(rows(current[2 * m], current[2 * m + 1]))
            transfer = lt_v[:, start + 128 * m : start + 128 * m + 128]
            lifted = nn(lanes(hi, lo), rows(transfer, transfer, transfer, transfer))
            following.append(halves(lifted[0:16], lifted[16:32]))
        current = following
    first_hi, first_lo = two_terms(current[0])
    second_hi, second_lo = two_terms(current[1])
    root = nn(lanes(first_hi, first_lo, second_hi, second_lo), rows(*([top[0]] * 4 + [top[1]] * 4)))
    root_tile[...] = hilo(root)
    nodes[i] = root_tile[...]

    @pl.when(jnp.logical_and(c == 0, z < 7))
    def _():
        pl.semaphore_wait(barrier, count_0)
        tell(flag_0)

    @pl.when(jnp.logical_and(c == 1, z < 7))
    def _():
        pl.semaphore_wait(flag_0, 1)

    for k in range(1, 8):
        send_root((i + k) & 7)

    @pl.when(z >= 4)
    def _():
        send_root(i & 7)

    @pl.when(near_start)
    def _():
        to_vec_peers()

    @pl.when(left_now)
    def _():
        far_left()

    @pl.when(right_now)
    def _():
        far_right()

    @pl.when(near_start)
    def _():
        wait_for(arrived.at[1, 0:48], recv_sem.at[0])

    @pl.when(left_now)
    def _():
        near_left()

    @pl.when(right_now)
    def _():
        near_right()

    uc_in = load(uc_h, uc_v, 8)
    lc_in = load(lc_h, lc_v, 9)
    far_in_s = load(far_h, far_s, 10)
    near_in_s = load(near_h, near_s, 11)
    tiles_in = load(tiles_h, tiles_v, 12)

    for copy in ut_in:
        copy.wait()
    for p in range(19):
        pair = ut_v[:, 128 * p : 128 * p + 128]
        swapped = turned(pair)
        dup[2 * p] = halves(pair, swapped)
        dup[2 * p + 1] = halves(swapped, pair)

    path = dup[i]
    path_hi[0] = path
    path = path.astype(F32)
    below = [(top[0], None), (top[1], None)]
    row_below = [(dup[28], None), (dup[29], None)]

    def path_step(path, u):
        matrix = dup[BASES[u] + (i >> u if u < 4 else y)]
        path = nn(hilo(path), rows(matrix, matrix))
        path_hi[u], path_lo[u] = two_terms(path)
        return path

    def product_step(below, transfers, start):
        following = []
        for m, (hi, lo) in enumerate(below):
            left_side = diagonal(transfers[:, start + 128 * m : start + 128 * m + 128])
            if lo is None:
                product = nn(left_side, rows(hi, hi))
            else:
                product = nn(lanes(left_side, left_side), rows(hi, hi, lo, lo))
            hi, lo = two_terms(product)
            following += [(hi[0:64], lo[0:64]), (hi[64:128], lo[64:128])]
        return following

    for u, start in ((1, 1536), (2, 1024), (3, 0)):
        path = path_step(path, u)
        below = product_step(below, lt_v, start)
        row_below = product_step(row_below, ut_v, start)
    path_step(path, 4)
    for m in range(8):
        r0_hi[m] = rows(below[2 * m][0], below[2 * m + 1][0])
        r0_lo[m] = rows(below[2 * m][1], below[2 * m + 1][1])
    for m, (hi, lo) in enumerate(row_below):
        from_row[0, m] = rows(hi, hi)
        from_row[1, m] = rows(lo, lo)

    def fold(j, carry):
        at = pl.ds(pl.multiple_of(128 * j, 128), 128)
        block = diagonal(basis_v[:, at])
        hi, lo = two_terms(tn(r0_hi[j], block) + tn(r0_lo[j], block))
        to_points[0:128, at] = hi
        to_points[128:256, at] = lo
        return carry

    lax.fori_loop(0, 8, fold, 0, unroll=2)

    uc_in.wait()
    couplings = rows(uc_v[...], uc_v[...])
    for e in range(2):
        value = nn(halves(path_hi[3 + e], path_lo[3 + e]), couplings)
        value = jnp.transpose(rows(value, value))
        for o in range(4):
            lifted_couplings[e, o] = value[64 * o : 64 * o + 64]

    def slot(offset, odd):
        index = jnp.where(offset == -3, 0, jnp.where(offset == -2, 1, jnp.where(offset == 2, 2, 3)))
        wide = jnp.logical_or(
            jnp.logical_and(offset == -3, odd == 1), jnp.logical_and(offset == 3, odd == 0)
        )
        valid = jnp.logical_or(jnp.logical_or(offset == -2, offset == 2), wide)
        return index, jnp.where(valid, 1.0, 0.0).astype(F32)

    def gather_top(n, carry):
        index, keep = slot(n - y, y & 1)
        value = lifted_couplings[0, index] * keep
        index, keep = slot((n >> 1) - (y >> 1), (y >> 1) & 1)
        hi, lo = two_terms(lifted_couplings[1, index] * keep)
        hi, lo = two_terms(value + nn(dup[30 + n], rows(hi, lo)))
        from_top[0, n] = rows(hi, hi)
        from_top[1, n] = rows(lo, lo)
        return carry

    lax.fori_loop(0, 8, gather_top, 0, unroll=4)

    def fill(w):
        def step(j, carry):
            block = arrived[w, :, pl.ds(pl.multiple_of(128 * j, 128), 128)]
            points[8 * w + j, 0] = block
            points[8 * w + j, 1] = turned(block)
            return carry

        lax.fori_loop(0, 8, step, 0, unroll=2)

    @pl.when(c == 1)
    def _():
        pl.semaphore_wait(barrier, count_1)
        tell(flag_1)

    @pl.when(c == 0)
    def _():
        pl.semaphore_wait(flag_1, 1)

    for k in range(1, 8):
        send_root(8 + ((i + k) & 7))

    @pl.when(z < 4)
    def _():
        send_root(8 + i)

    @pl.when(z >= 4)
    def _():
        to_vec_peers()

    @pl.when(jnp.logical_not(left_now))
    def _():
        far_left()

    @pl.when(right_later)
    def _():
        far_right()

    @pl.when(z >= 4)
    def _():
        wait_for(arrived.at[1, 0:48], recv_sem.at[0])

    @pl.when(row_start)
    def _():
        send(vec_h, arrived.at[2, own], 11, 5, left, x)

    @pl.when(left_later)
    def _():
        near_left()

    @pl.when(right_later)
    def _():
        near_right()

    fill(1)

    first_leaf = ROW * d - ROW

    def chosen(table, lists, slots, column):
        parts = []
        for s in range(0, slots, 2):
            a = jnp.clip(lists[s, column] - first_leaf, 0, 3 * ROW - 1)
            b = jnp.clip(lists[s + 1, column] - first_leaf, 0, 3 * ROW - 1)
            parts.append(halves(table[a >> 1, a & 1], table[b >> 1, 1 - (b & 1)]))
        return lanes(*parts)

    def far_part():
        far_in_s.wait()
        lc_in.wait()
        wait_for(coeffs.at[0:8, 0], recv_sem.at[2])
        wait_for(coeffs.at[16:24, 0], recv_sem.at[3])
        for p in list(range(8)) + list(range(16, 24)):
            coeffs[p, 1] = turned(coeffs[p, 0])
        for j in range(8):
            source = rows(*[chosen(coeffs, far_s, 6, 2 * j + e) for e in range(2)])
            value = nt(source, rows(lc_v[:, 768 * j : 768 * j + 384], lc_v[:, 768 * j + 384 : 768 * j + 768]))
            hi, lo = two_terms(halves(value[0:16], value[16:32]))
            block = diagonal(basis_v[:, 128 * j : 128 * j + 128])
            far_out[j] = nn(lanes(hi, lo), rows(block, block))

    def near_part():
        near_in_s.wait()
        tiles_in.wait()

        @pl.when(row_start)
        def _():
            wait_for(arrived.at[0, 0:48], recv_sem.at[10])

        @pl.when(jnp.logical_not(row_start))
        def _():
            wait_for(arrived.at[0], recv_sem.at[4])

        @pl.when(row_end)
        def _():
            wait_for(arrived.at[2, 0:48], recv_sem.at[11])

        @pl.when(jnp.logical_not(row_end))
        def _():
            wait_for(arrived.at[2], recv_sem.at[5])

        fill(0)
        fill(2)
        for q in range(2):
            source = rows(*[chosen(points, near_s, 6, 4 * x + 2 * q + e) for e in range(2)])
            value = nt(source, rows(tiles_v[2 * q], tiles_v[2 * q + 1]))
            value = halves(value[0:64], value[64:128]).astype(BF)
            for v in range(4):
                near_out[v, q] = value[16 * v : 16 * v + 16]
        for n, peer in enumerate(vec_peers):
            send(near_out.at[peer], near_in.at[x], 9, 9, d, peer)
        near_in[x] = near_out[x]

    wait_for(nodes.at[0:15], recv_sem.at[1])

    @pl.when(row_start)
    def _():
        wait_for(arrived.at[0, 0:16], recv_sem.at[4])
        for peer in vec_peers:
            send(arrived.at[0, own], arrived.at[0, own], 10, 10, d, peer)

    @pl.when(row_end)
    def _():
        wait_for(arrived.at[2, 0:16], recv_sem.at[5])
        for peer in vec_peers:
            send(arrived.at[2, own], arrived.at[2, own], 11, 11, d, peer)

    roots = lanes(*[nodes[m] for m in range(ROW)])
    top_tile = hilo(nn(roots, from_row[0].reshape(2048, 128)) + nn(roots, from_row[1].reshape(2048, 128)))
    nodes[30 + y] = top_tile
    heads[8] = top_tile
    tails[8] = top_tile
    for peer in column_peers[:4] + column_peers[5:6]:
        send(nodes.at[30 + y], nodes.at[30 + y], 8, 8, peer, x)
    for u in range(3):
        base, count = BASES[u], ROW >> u
        for m in range(count // 2):
            left_m, right_m = dup[base + 2 * m], dup[base + 2 * m + 1]
            value = nn(lanes(nodes[base + 2 * m], nodes[base + 2 * m + 1]), rows(left_m, left_m, right_m, right_m))
            nodes[BASES[u + 1] + m] = hilo(value)
    for u in range(4):
        for e in range(2):
            heads[2 * u + e] = nodes[BASES[u] + e]
            tails[2 * u + e] = nodes[BASES[u + 1] - 2 + e]
    send(tails, nodes.at[PREV : PREV + 9], 6, 6, column_peers[4], x)
    send(heads, nodes.at[NEXT : NEXT + 9], 7, 7, column_peers[6], x)

    near_part()
    far_part()

    weights = []
    for o in range(2):
        pair = uc_v[:, 128 * o : 128 * o + 128]
        swapped = turned(pair)
        weights += [halves(pair, swapped), halves(swapped, pair)]
    weights = lanes(*weights)
    wait_for(nodes.at[0:9], recv_sem.at[6])
    wait_for(nodes.at[0:9], recv_sem.at[7])
    sources = []
    for u in range(4):
        g = d >> u
        odd = g & 1
        number = LEAF_COUNT >> u
        count = ROW >> u
        parts = []
        for o, wanted in ((-3, odd == 1), (-2, None), (2, None), (3, odd == 0)):
            shift = o if wanted is None else (-3 * odd if o < 0 else 3 * (1 - odd))
            place = (i >> u) + shift
            place = jnp.where(
                place < 0,
                PREV + 2 + 2 * u + place,
                jnp.where(place < count, BASES[u] + place, NEXT + 2 * u - count + place),
            )
            valid = (g + o >= 0) if o < 0 else (g + o < number)
            if wanted is not None:
                valid = jnp.logical_and(valid, wanted)
            keep = jnp.where(valid, 1.0, 0.0).astype(F32)
            parts.append((nodes[place].astype(F32) * keep).astype(BF))
        sources.append(lanes(*parts))
    coupled = nt(rows(*sources), rows(weights, weights))
    left_side, right_side = [], []
    for u in range(1, 4):
        tile = hilo(coupled[16 * u : 16 * u + 16])
        left_side.append(tile)
        right_side.append(path_hi[u - 1])
        if u > 1:
            left_side.append(tile)
            right_side.append(path_lo[u - 1])
    matrix = lanes(*right_side)
    down = coupled[0:16] + nt(lanes(*left_side), rows(matrix, matrix))

    nodes[30 + ((y + 7) & 7)] = nodes[PREV + 8]
    nodes[30 + ((y + 1) & 7)] = nodes[NEXT + 8]
    wait_for(nodes.at[0:5], recv_sem.at[8])
    tops = lanes(*[nodes[30 + n] for n in range(8)])
    down = down + nn(tops, from_top[0].reshape(1024, 128)) + nn(tops, from_top[1].reshape(1024, 128))
    down = hilo(down)
    value = nn(lanes(down, down), to_points[...])
    wait_for(near_in.at[0:3], recv_sem.at[9])
    for j in range(8):
        at = slice(128 * j, 128 * j + 128)
        out_ref[:, at] = (value[:, at] + far_out[j] + near_in[j // 2, j % 2].astype(F32)).astype(BF)

    wait_for(arrived.at[1, 0:48], send_sem.at[0])
    wait_for(nodes.at[0:15], send_sem.at[1])
    wait_for(coeffs.at[0:8, 0], send_sem.at[2])
    wait_for(coeffs.at[0:8, 0], send_sem.at[3])

    @pl.when(row_end)
    def _():
        wait_for(arrived.at[0, 0:16], send_sem.at[10])
        wait_for(arrived.at[2, 0:48], send_sem.at[11])

    @pl.when(row_start)
    def _():
        wait_for(arrived.at[0, 0:48], send_sem.at[10])
        wait_for(arrived.at[2, 0:16], send_sem.at[11])

    @pl.when(jnp.logical_not(row_end))
    def _():
        wait_for(arrived.at[0], send_sem.at[4])

    @pl.when(jnp.logical_not(row_start))
    def _():
        wait_for(arrived.at[2], send_sem.at[5])

    wait_for(nodes.at[0:9], send_sem.at[6])
    wait_for(nodes.at[0:9], send_sem.at[7])
    wait_for(nodes.at[0:5], send_sem.at[8])
    wait_for(near_out.at[0:3], send_sem.at[9])


def shards(vectors, leaf_basis, local_transfer, upper_transfer, upper_coupling, leaf_coupling, far_list, near_list, near_tiles):
    tile = (16, 128)
    scratch = [
        pltpu.VMEM(leaf_basis.shape, BF),
        pltpu.VMEM(local_transfer.shape, BF),
        pltpu.VMEM((64, 2432), BF),
        pltpu.VMEM(upper_coupling.shape, BF),
        pltpu.VMEM(leaf_coupling.shape, BF),
        pltpu.SMEM(far_list.shape, jnp.int32),
        pltpu.SMEM(near_list.shape, jnp.int32),
        pltpu.VMEM(near_tiles.shape, BF),
        pltpu.VMEM((3, 64, 1024), BF),
        pltpu.VMEM((24, 2, 64, 128), BF),
        pltpu.VMEM((24, 2) + tile, BF),
        pltpu.VMEM(tile, BF),
        pltpu.VMEM((60,) + tile, BF),
        pltpu.VMEM((9,) + tile, BF),
        pltpu.VMEM((9,) + tile, BF),
        pltpu.VMEM((38, 64, 128), BF),
        pltpu.VMEM((5, 64, 128), BF),
        pltpu.VMEM((5, 64, 128), BF),
        pltpu.VMEM((8, 128, 128), BF),
        pltpu.VMEM((8, 128, 128), BF),
        pltpu.VMEM((256, 1024), BF),
        pltpu.VMEM((2, 4, 64, 128), F32),
        pltpu.VMEM((2, 8, 128, 128), BF),
        pltpu.VMEM((2, ROW, 128, 128), BF),
        pltpu.VMEM((8,) + tile, F32),
        pltpu.VMEM((4, 2) + tile, BF),
        pltpu.VMEM((4, 2) + tile, BF),
        pltpu.SemaphoreType.DMA((13,)),
        pltpu.SemaphoreType.DMA((12,)),
        pltpu.SemaphoreType.DMA((12,)),
        pltpu.SemaphoreType.REGULAR,
        pltpu.SemaphoreType.REGULAR,
    ]
    return pl.pallas_call(
        kernel,
        out_shape=pltpu.VMEM(vectors.shape, BF),
        in_specs=[pl.BlockSpec(memory_space=pl.ANY)] * 9,
        out_specs=pl.BlockSpec(memory_space=pltpu.VMEM),
        scratch_shapes=scratch,
        compiler_params=pltpu.CompilerParams(
            collective_id=0, has_side_effects=True, vmem_limit_bytes=62 * 1024 * 1024
        ),
    )(vectors, leaf_basis, local_transfer, upper_transfer, upper_coupling, leaf_coupling, far_list, near_list, near_tiles)


def solution(mesh):
    placed = (
        P("vec", "leaf"),
        P(None, "leaf"),
        P(None, "leaf"),
        P(),
        P(),
        P(None, "leaf"),
        P(None, "leaf"),
        P(None, "leaf"),
        P(("leaf", "vec"), None, None),
    )
    return jax.shard_map(
        shards, mesh=mesh, in_specs=placed, out_specs=P("vec", "leaf"), check_vma=False
    )
```

```python
import jax
import jax.numpy as jnp
from jax import lax
from jax.experimental import pallas as pl
from jax.experimental.pallas import tpu as pltpu
from jax.sharding import PartitionSpec as P

MESH = pl.DeviceIdType.MESH
BF = jnp.bfloat16
F32 = jnp.float32
ROW = 16
ROWS = 8
LEAF_COUNT = ROW * ROWS
BASES = (0, 16, 24, 28, 30)
PREV = 42
NEXT = 51


def low(shape):
    return lax.broadcasted_iota(jnp.int32, shape, 1) < 64


def halves(a, b):
    return jnp.where(low(a.shape), a, b)


def turned(tile):
    return pltpu.roll(tile, 64, 1)


def rounded(x):
    return x.astype(BF).astype(F32)


def hilo(x):
    hi = rounded(x)
    return halves(hi, x - hi).astype(BF)


def two_terms(x):
    hi = rounded(x)
    return hi.astype(BF), (x - hi).astype(BF)


def nn(a, b):
    return jnp.dot(a, b, preferred_element_type=F32)


def nt(a, b):
    return lax.dot_general(a, b, (((1,), (1,)), ((), ())), preferred_element_type=F32)


def tn(a, b):
    return lax.dot_general(a, b, (((0,), (0,)), ((), ())), preferred_element_type=F32)


def diagonal(block):
    none = jnp.zeros_like(block)
    return rows(halves(block, none), halves(none, block))


def rows(*parts):
    return jnp.concatenate(parts, axis=0)


def lanes(*parts):
    return jnp.concatenate(parts, axis=1)


def kernel(
    vec_h, basis_h, lt_h, ut_h, uc_h, lc_h, far_h, near_h, tiles_h, out_ref,
    basis_v, lt_v, ut_v, uc_v, lc_v, far_s, near_s, tiles_v,
    arrived, points, coeffs, root_tile, nodes, heads, tails,
    dup, path_hi, path_lo, r0_hi, r0_lo, to_points, lifted_couplings, from_top, from_row, far_out, near_out, near_in,
    in_sem, send_sem, recv_sem, flag_0, flag_1,
):
    d = lax.axis_index("leaf")
    x = lax.axis_index("vec")
    y = d >> 4
    i = d & 15
    z = i >> 1
    c = i & 1

    def load(src, dst, n):
        copy = pltpu.make_async_copy(src, dst, in_sem.at[n])
        copy.start()
        return copy

    own = pl.ds(pl.multiple_of(16 * x, 16), 16)
    vec_in = load(vec_h, arrived.at[1, own], 0)
    basis_in = load(basis_h, basis_v, 1)
    lt_in = load(lt_h, lt_v, 2)

    right = (d + 1) & (LEAF_COUNT - 1)
    left = (d + LEAF_COUNT - 1) & (LEAF_COUNT - 1)
    sibling = d + 1 - 2 * c
    column_peers = [(d + ROW * k) & (LEAF_COUNT - 1) for k in (4, 3, 5, 2, 1, 6, 7)]
    vec_peers = [(x + k) & 3 for k in (2, 1, 3)]

    barrier = pltpu.get_barrier_semaphore()

    def announce(leaf, vec):
        pl.semaphore_signal(barrier, inc=1, device_id={"leaf": leaf, "vec": vec}, device_id_type=MESH)

    @pl.when(z < 4)
    def _():
        for k in range(1, 8):
            announce(ROW * y + 2 * ((z + k) & 7), x)

    @pl.when(z >= 4)
    def _():
        for k in range(1, 8):
            announce(ROW * y + 2 * ((z + k) & 7) + 1, x)

    announce(sibling, x)
    near_start = z < 4
    announce((d + jnp.where(c == 0, LEAF_COUNT - 2 + (z >> 2), jnp.where(z == 7, 2, 1))) & (LEAF_COUNT - 1), x)
    for peer in vec_peers:
        announce(d - c + (z >> 2), peer)
    for peer in column_peers:
        announce(peer - c + 1, x)

    ends = jnp.where(jnp.logical_or(z == 0, z == 3), 1, 0)
    last = jnp.where(z == 7, 1, 0)
    count_0 = jnp.where(near_start, 15 - ends, 10 + last)
    count_1 = jnp.where(near_start, 23 + ends, 28 - last)

    def tell(flag):
        pl.semaphore_signal(flag, inc=1, device_id={"leaf": sibling, "vec": x}, device_id_type=MESH)

    @pl.when(jnp.logical_and(c == 0, z == 7))
    def _():
        pl.semaphore_wait(barrier, count_0)
        tell(flag_0)

    ut_in = [
        load(ut_h.at[:, pl.ds(pl.multiple_of(1024 * y, 128), 1024)], ut_v.at[:, 0:1024], 3),
        load(ut_h.at[:, pl.ds(pl.multiple_of(8192 + 512 * y, 128), 512)], ut_v.at[:, 1024:1536], 4),
        load(ut_h.at[:, pl.ds(pl.multiple_of(12288 + 256 * y, 128), 256)], ut_v.at[:, 1536:1792], 5),
        load(ut_h.at[:, pl.ds(pl.multiple_of(14336 + 128 * y, 128), 128)], ut_v.at[:, 1792:1920], 6),
        load(ut_h.at[:, 15360:15872], ut_v.at[:, 1920:2432], 7),
    ]

    def send(src, dst, n_send, n_recv, leaf, vec):
        copy = pltpu.make_async_remote_copy(
            src_ref=src, dst_ref=dst, send_sem=send_sem.at[n_send], recv_sem=recv_sem.at[n_recv],
            device_id={"leaf": leaf, "vec": vec}, device_id_type=MESH,
        )
        copy.start()
        return copy

    def wait_for(ref, sem):
        pltpu.make_async_copy(ref, ref, sem).wait()

    def send_root(t):
        send(root_tile, nodes.at[i], 1, 1, ROW * y + t, x)

    def to_vec_peers():
        for peer in vec_peers:
            send(vec_h, arrived.at[1, own], 0, 0, d, peer)

    def far_right():
        send(coeffs.at[8:16, 0], coeffs.at[0:8, 0], 2, 2, right, x)

    def far_left():
        send(coeffs.at[8:16, 0], coeffs.at[16:24, 0], 3, 3, left, x)

    def near_right():
        send(arrived.at[1], arrived.at[0], 4, 4, right, x)

    def near_left():
        send(arrived.at[1], arrived.at[2], 5, 5, left, x)

    row_end = jnp.logical_and(c == 1, z == 7)
    row_start = jnp.logical_and(c == 0, z == 0)
    left_now = jnp.logical_and(near_start, jnp.logical_or(c == 1, z > 0))
    right_now = jnp.logical_and(near_start, jnp.logical_or(c == 0, z < 3))
    left_later = jnp.logical_not(jnp.logical_or(left_now, row_start))
    right_later = jnp.logical_not(jnp.logical_or(right_now, row_end))

    vec_in.wait()
    basis_in.wait()
    lt_in.wait()
    transfer = lt_v[:, 1792:1920]
    crossed = turned(transfer)
    top = (halves(transfer, crossed), halves(crossed, transfer))

    group = lax.broadcasted_iota(jnp.int32, (16, 256), 1) >> 6
    zero = jnp.zeros((16, 256), BF)

    def paired(product):
        return [
            halves(product[0:16, 0:128], product[16:32, 0:128]),
            halves(product[32:48, 128:256], product[48:64, 128:256]),
        ]

    leaves = []
    for q in range(4):
        tile = arrived[1, own, 256 * q : 256 * q + 256]
        block = basis_v[:, 256 * q : 256 * q + 256]
        spread = rows(*[jnp.where(group == e, tile, zero) for e in range(4)])
        leaves.append(nt(spread, rows(block, block)))
    for j in range(8):
        pair = leaves[j // 2][32 * (j % 2) : 32 * (j % 2) + 32]
        coeffs[8 + j, 0] = halves(pair[0:16], pair[16:32]).astype(BF)
        coeffs[8 + j, 1] = halves(pair[16:32], pair[0:16]).astype(BF)

    @pl.when(row_end)
    def _():
        pl.semaphore_wait(flag_0, 1)
        send(vec_h, arrived.at[0, own], 10, 4, right, x)
        far_right()

    current = []
    for q in range(4):
        transfer = lt_v[:, 256 * q : 256 * q + 256]
        current += paired(nn(hilo(leaves[q]), rows(transfer, transfer)))
    for start in (1024, 1536):
        following = []
        for q in range(len(current) // 4):
            hi, lo = two_terms(rows(*current[4 * q : 4 * q + 4]))
            transfer = lt_v[:, start + 256 * q : start + 256 * q + 256]
            following += paired(nn(lanes(hi, lo), rows(transfer, transfer, transfer, transfer)))
        current = following
    first_hi, first_lo = two_terms(current[0])
    second_hi, second_lo = two_terms(current[1])
    root = nn(lanes(first_hi, first_lo, second_hi, second_lo), rows(*([top[0]] * 4 + [top[1]] * 4)))
    root_tile[...] = hilo(root)
    nodes[i] = root_tile[...]

    @pl.when(jnp.logical_and(c == 0, z < 7))
    def _():
        pl.semaphore_wait(barrier, count_0)
        tell(flag_0)

    @pl.when(jnp.logical_and(c == 1, z < 7))
    def _():
        pl.semaphore_wait(flag_0, 1)

    for k in range(1, 8):
        send_root((i + k) & 7)

    @pl.when(z >= 4)
    def _():
        send_root(i & 7)

    @pl.when(near_start)
    def _():
        to_vec_peers()

    @pl.when(left_now)
    def _():
        far_left()

    @pl.when(right_now)
    def _():
        far_right()

    @pl.when(near_start)
    def _():
        wait_for(arrived.at[1, 0:48], recv_sem.at[0])

    @pl.when(left_now)
    def _():
        near_left()

    @pl.when(right_now)
    def _():
        near_right()

    uc_in = load(uc_h, uc_v, 8)
    lc_in = load(lc_h, lc_v, 9)
    far_in_s = load(far_h, far_s, 10)
    near_in_s = load(near_h, near_s, 11)
    tiles_in = load(tiles_h, tiles_v, 12)

    for copy in ut_in:
        copy.wait()
    for p in range(19):
        pair = ut_v[:, 128 * p : 128 * p + 128]
        swapped = turned(pair)
        dup[2 * p] = halves(pair, swapped)
        dup[2 * p + 1] = halves(swapped, pair)

    path = dup[i]
    path_hi[0] = path
    path = path.astype(F32)
    below = [(top[0], None), (top[1], None)]
    row_below = [(dup[28], None), (dup[29], None)]

    def path_step(path, u):
        matrix = dup[BASES[u] + (i >> u if u < 4 else y)]
        path = nn(hilo(path), rows(matrix, matrix))
        path_hi[u], path_lo[u] = two_terms(path)
        return path

    def product_step(below, transfers, start):
        following = []
        for m, (hi, lo) in enumerate(below):
            left_side = diagonal(transfers[:, start + 128 * m : start + 128 * m + 128])
            if lo is None:
                product = nn(left_side, rows(hi, hi))
            else:
                product = nn(lanes(left_side, left_side), rows(hi, hi, lo, lo))
            hi, lo = two_terms(product)
            following += [(hi[0:64], lo[0:64]), (hi[64:128], lo[64:128])]
        return following

    for u, start in ((1, 1536), (2, 1024), (3, 0)):
        path = path_step(path, u)
        below = product_step(below, lt_v, start)
        row_below = product_step(row_below, ut_v, start)
    path_step(path, 4)
    for m in range(8):
        r0_hi[m] = rows(below[2 * m][0], below[2 * m + 1][0])
        r0_lo[m] = rows(below[2 * m][1], below[2 * m + 1][1])
    for m, (hi, lo) in enumerate(row_below):
        from_row[0, m] = rows(hi, hi)
        from_row[1, m] = rows(lo, lo)

    def fold(j, carry):
        at = pl.ds(pl.multiple_of(128 * j, 128), 128)
        block = diagonal(basis_v[:, at])
        hi, lo = two_terms(tn(r0_hi[j], block) + tn(r0_lo[j], block))
        to_points[0:128, at] = hi
        to_points[128:256, at] = lo
        return carry

    lax.fori_loop(0, 8, fold, 0, unroll=2)

    uc_in.wait()
    couplings = rows(uc_v[...], uc_v[...])
    for e in range(2):
        value = nn(halves(path_hi[3 + e], path_lo[3 + e]), couplings)
        value = jnp.transpose(rows(value, value))
        for o in range(4):
            lifted_couplings[e, o] = value[64 * o : 64 * o + 64]

    def slot(offset, odd):
        index = jnp.where(offset == -3, 0, jnp.where(offset == -2, 1, jnp.where(offset == 2, 2, 3)))
        wide = jnp.logical_or(
            jnp.logical_and(offset == -3, odd == 1), jnp.logical_and(offset == 3, odd == 0)
        )
        valid = jnp.logical_or(jnp.logical_or(offset == -2, offset == 2), wide)
        return index, jnp.where(valid, 1.0, 0.0).astype(F32)

    def gather_top(n, carry):
        index, keep = slot(n - y, y & 1)
        value = lifted_couplings[0, index] * keep
        index, keep = slot((n >> 1) - (y >> 1), (y >> 1) & 1)
        hi, lo = two_terms(lifted_couplings[1, index] * keep)
        hi, lo = two_terms(value + nn(dup[30 + n], rows(hi, lo)))
        from_top[0, n] = rows(hi, hi)
        from_top[1, n] = rows(lo, lo)
        return carry

    lax.fori_loop(0, 8, gather_top, 0, unroll=4)

    def fill(w):
        def step(j, carry):
            block = arrived[w, :, pl.ds(pl.multiple_of(128 * j, 128), 128)]
            points[8 * w + j, 0] = block
            points[8 * w + j, 1] = turned(block)
            return carry

        lax.fori_loop(0, 8, step, 0, unroll=2)

    @pl.when(c == 1)
    def _():
        pl.semaphore_wait(barrier, count_1)
        tell(flag_1)

    @pl.when(c == 0)
    def _():
        pl.semaphore_wait(flag_1, 1)

    for k in range(1, 8):
        send_root(8 + ((i + k) & 7))

    @pl.when(z < 4)
    def _():
        send_root(8 + i)

    @pl.when(z >= 4)
    def _():
        to_vec_peers()

    @pl.when(jnp.logical_not(left_now))
    def _():
        far_left()

    @pl.when(right_later)
    def _():
        far_right()

    @pl.when(z >= 4)
    def _():
        wait_for(arrived.at[1, 0:48], recv_sem.at[0])

    @pl.when(row_start)
    def _():
        send(vec_h, arrived.at[2, own], 11, 5, left, x)

    @pl.when(left_later)
    def _():
        near_left()

    @pl.when(right_later)
    def _():
        near_right()

    fill(1)

    first_leaf = ROW * d - ROW

    def chosen(table, lists, slots, column):
        parts = []
        for s in range(0, slots, 2):
            a = jnp.clip(lists[s, column] - first_leaf, 0, 3 * ROW - 1)
            b = jnp.clip(lists[s + 1, column] - first_leaf, 0, 3 * ROW - 1)
            parts.append(halves(table[a >> 1, a & 1], table[b >> 1, 1 - (b & 1)]))
        return lanes(*parts)

    def far_part():
        far_in_s.wait()
        lc_in.wait()
        wait_for(coeffs.at[0:8, 0], recv_sem.at[2])
        wait_for(coeffs.at[16:24, 0], recv_sem.at[3])
        for p in list(range(8)) + list(range(16, 24)):
            coeffs[p, 1] = turned(coeffs[p, 0])
        for j in range(8):
            source = rows(*[chosen(coeffs, far_s, 6, 2 * j + e) for e in range(2)])
            value = nt(source, rows(lc_v[:, 768 * j : 768 * j + 384], lc_v[:, 768 * j + 384 : 768 * j + 768]))
            hi, lo = two_terms(halves(value[0:16], value[16:32]))
            block = diagonal(basis_v[:, 128 * j : 128 * j + 128])
            far_out[j] = nn(lanes(hi, lo), rows(block, block))

    def near_part():
        near_in_s.wait()
        tiles_in.wait()

        @pl.when(row_start)
        def _():
            wait_for(arrived.at[0, 0:48], recv_sem.at[10])

        @pl.when(jnp.logical_not(row_start))
        def _():
            wait_for(arrived.at[0], recv_sem.at[4])

        @pl.when(row_end)
        def _():
            wait_for(arrived.at[2, 0:48], recv_sem.at[11])

        @pl.when(jnp.logical_not(row_end))
        def _():
            wait_for(arrived.at[2], recv_sem.at[5])

        fill(0)
        fill(2)
        for q in range(2):
            source = rows(*[chosen(points, near_s, 6, 4 * x + 2 * q + e) for e in range(2)])
            value = nt(source, rows(tiles_v[2 * q], tiles_v[2 * q + 1]))
            value = halves(value[0:64], value[64:128]).astype(BF)
            for v in range(4):
                near_out[v, q] = value[16 * v : 16 * v + 16]
        for n, peer in enumerate(vec_peers):
            send(near_out.at[peer], near_in.at[x], 9, 9, d, peer)
        near_in[x] = near_out[x]

    @pl.when(row_start)
    def _():
        wait_for(arrived.at[0, 0:16], recv_sem.at[4])
        for peer in vec_peers:
            send(arrived.at[0, own], arrived.at[0, own], 10, 10, d, peer)

    def row_tree():
        wait_for(nodes.at[0:15], recv_sem.at[1])

        @pl.when(row_end)
        def _():
            wait_for(arrived.at[2, 0:16], recv_sem.at[5])
            for peer in vec_peers:
                send(arrived.at[2, own], arrived.at[2, own], 11, 11, d, peer)

        roots = lanes(*[nodes[m] for m in range(ROW)])
        top_tile = hilo(nn(roots, from_row[0].reshape(2048, 128)) + nn(roots, from_row[1].reshape(2048, 128)))
        nodes[30 + y] = top_tile
        heads[8] = top_tile
        tails[8] = top_tile
        for peer in column_peers[:4] + column_peers[5:6]:
            send(nodes.at[30 + y], nodes.at[30 + y], 8, 8, peer, x)
        for u in range(3):
            base, count = BASES[u], ROW >> u
            for m in range(count // 2):
                left_m, right_m = dup[base + 2 * m], dup[base + 2 * m + 1]
                value = nn(lanes(nodes[base + 2 * m], nodes[base + 2 * m + 1]), rows(left_m, left_m, right_m, right_m))
                nodes[BASES[u + 1] + m] = hilo(value)
        for u in range(4):
            for e in range(2):
                heads[2 * u + e] = nodes[BASES[u] + e]
                tails[2 * u + e] = nodes[BASES[u + 1] - 2 + e]
        send(tails, nodes.at[PREV : PREV + 9], 6, 6, column_peers[4], x)
        send(heads, nodes.at[NEXT : NEXT + 9], 7, 7, column_peers[6], x)

    near_turn = jnp.where(jnp.logical_and(z < 3, jnp.logical_not(row_start)), 0, 1)
    far_turn = jnp.where(z < 3, 0, 1)

    def turn(n, carry):
        @pl.when(n == 1)
        def _():
            row_tree()

        @pl.when(n == near_turn)
        def _():
            near_part()

        @pl.when(n == far_turn)
        def _():
            far_part()

        return carry

    lax.fori_loop(0, 2, turn, 0)

    weights = []
    for o in range(2):
        pair = uc_v[:, 128 * o : 128 * o + 128]
        swapped = turned(pair)
        weights += [halves(pair, swapped), halves(swapped, pair)]
    weights = lanes(*weights)
    wait_for(nodes.at[0:9], recv_sem.at[6])
    wait_for(nodes.at[0:9], recv_sem.at[7])
    sources = []
    for u in range(4):
        g = d >> u
        odd = g & 1
        number = LEAF_COUNT >> u
        count = ROW >> u
        parts = []
        for o, wanted in ((-3, odd == 1), (-2, None), (2, None), (3, odd == 0)):
            shift = o if wanted is None else (-3 * odd if o < 0 else 3 * (1 - odd))
            place = (i >> u) + shift
            place = jnp.where(
                place < 0,
                PREV + 2 + 2 * u + place,
                jnp.where(place < count, BASES[u] + place, NEXT + 2 * u - count + place),
            )
            valid = (g + o >= 0) if o < 0 else (g + o < number)
            if wanted is not None:
                valid = jnp.logical_and(valid, wanted)
            keep = jnp.where(valid, 1.0, 0.0).astype(F32)
            parts.append((nodes[place].astype(F32) * keep).astype(BF))
        sources.append(lanes(*parts))
    coupled = nt(rows(*sources), rows(weights, weights))
    left_side, right_side = [], []
    for u in range(1, 4):
        tile = hilo(coupled[16 * u : 16 * u + 16])
        left_side.append(tile)
        right_side.append(path_hi[u - 1])
        if u > 1:
            left_side.append(tile)
            right_side.append(path_lo[u - 1])
    matrix = lanes(*right_side)
    down = coupled[0:16] + nt(lanes(*left_side), rows(matrix, matrix))

    nodes[30 + ((y + 7) & 7)] = nodes[PREV + 8]
    nodes[30 + ((y + 1) & 7)] = nodes[NEXT + 8]
    wait_for(nodes.at[0:5], recv_sem.at[8])
    tops = lanes(*[nodes[30 + n] for n in range(8)])
    down = down + nn(tops, from_top[0].reshape(1024, 128)) + nn(tops, from_top[1].reshape(1024, 128))
    down = hilo(down)
    value = nn(lanes(down, down), to_points[...])
    wait_for(near_in.at[0:3], recv_sem.at[9])
    for j in range(8):
        at = slice(128 * j, 128 * j + 128)
        out_ref[:, at] = (value[:, at] + far_out[j] + near_in[j // 2, j % 2].astype(F32)).astype(BF)

    wait_for(arrived.at[1, 0:48], send_sem.at[0])
    wait_for(nodes.at[0:15], send_sem.at[1])
    wait_for(coeffs.at[0:8, 0], send_sem.at[2])
    wait_for(coeffs.at[0:8, 0], send_sem.at[3])

    @pl.when(row_end)
    def _():
        wait_for(arrived.at[0, 0:16], send_sem.at[10])
        wait_for(arrived.at[2, 0:48], send_sem.at[11])

    @pl.when(row_start)
    def _():
        wait_for(arrived.at[0, 0:48], send_sem.at[10])
        wait_for(arrived.at[2, 0:16], send_sem.at[11])

    @pl.when(jnp.logical_not(row_end))
    def _():
        wait_for(arrived.at[0], send_sem.at[4])

    @pl.when(jnp.logical_not(row_start))
    def _():
        wait_for(arrived.at[2], send_sem.at[5])

    wait_for(nodes.at[0:9], send_sem.at[6])
    wait_for(nodes.at[0:9], send_sem.at[7])
    wait_for(nodes.at[0:5], send_sem.at[8])
    wait_for(near_out.at[0:3], send_sem.at[9])


def shards(vectors, leaf_basis, local_transfer, upper_transfer, upper_coupling, leaf_coupling, far_list, near_list, near_tiles):
    tile = (16, 128)
    scratch = [
        pltpu.VMEM(leaf_basis.shape, BF),
        pltpu.VMEM(local_transfer.shape, BF),
        pltpu.VMEM((64, 2432), BF),
        pltpu.VMEM(upper_coupling.shape, BF),
        pltpu.VMEM(leaf_coupling.shape, BF),
        pltpu.SMEM(far_list.shape, jnp.int32),
        pltpu.SMEM(near_list.shape, jnp.int32),
        pltpu.VMEM(near_tiles.shape, BF),
        pltpu.VMEM((3, 64, 1024), BF),
        pltpu.VMEM((24, 2, 64, 128), BF),
        pltpu.VMEM((24, 2) + tile, BF),
        pltpu.VMEM(tile, BF),
        pltpu.VMEM((60,) + tile, BF),
        pltpu.VMEM((9,) + tile, BF),
        pltpu.VMEM((9,) + tile, BF),
        pltpu.VMEM((38, 64, 128), BF),
        pltpu.VMEM((5, 64, 128), BF),
        pltpu.VMEM((5, 64, 128), BF),
        pltpu.VMEM((8, 128, 128), BF),
        pltpu.VMEM((8, 128, 128), BF),
        pltpu.VMEM((256, 1024), BF),
        pltpu.VMEM((2, 4, 64, 128), F32),
        pltpu.VMEM((2, 8, 128, 128), BF),
        pltpu.VMEM((2, ROW, 128, 128), BF),
        pltpu.VMEM((8,) + tile, F32),
        pltpu.VMEM((4, 2) + tile, BF),
        pltpu.VMEM((4, 2) + tile, BF),
        pltpu.SemaphoreType.DMA((13,)),
        pltpu.SemaphoreType.DMA((12,)),
        pltpu.SemaphoreType.DMA((12,)),
        pltpu.SemaphoreType.REGULAR,
        pltpu.SemaphoreType.REGULAR,
    ]
    return pl.pallas_call(
        kernel,
        out_shape=pltpu.VMEM(vectors.shape, BF),
        in_specs=[pl.BlockSpec(memory_space=pl.ANY)] * 9,
        out_specs=pl.BlockSpec(memory_space=pltpu.VMEM),
        scratch_shapes=scratch,
        compiler_params=pltpu.CompilerParams(
            collective_id=0, has_side_effects=True, vmem_limit_bytes=62 * 1024 * 1024
        ),
    )(vectors, leaf_basis, local_transfer, upper_transfer, upper_coupling, leaf_coupling, far_list, near_list, near_tiles)


def solution(mesh):
    placed = (
        P("vec", "leaf"),
        P(None, "leaf"),
        P(None, "leaf"),
        P(),
        P(),
        P(None, "leaf"),
        P(None, "leaf"),
        P(None, "leaf"),
        P(("leaf", "vec"), None, None),
    )
    return jax.shard_map(
        shards, mesh=mesh, in_specs=placed, out_specs=P("vec", "leaf"), check_vma=False
    )
```

```python
import jax
import jax.numpy as jnp
from jax import lax
from jax.experimental import pallas as pl
from jax.experimental.pallas import tpu as pltpu
from jax.sharding import PartitionSpec as P

MESH = pl.DeviceIdType.MESH
BF = jnp.bfloat16
F32 = jnp.float32
ROW = 16
ROWS = 8
LEAF_COUNT = ROW * ROWS
BASES = (0, 16, 24, 28, 30)
PREV = 42
NEXT = 51


def low(shape):
    return lax.broadcasted_iota(jnp.int32, shape, 1) < 64


def halves(a, b):
    return jnp.where(low(a.shape), a, b)


def turned(tile):
    return pltpu.roll(tile, 64, 1)


def rounded(x):
    return x.astype(BF).astype(F32)


def hilo(x):
    hi = rounded(x)
    return halves(hi, x - hi).astype(BF)


def two_terms(x):
    hi = rounded(x)
    return hi.astype(BF), (x - hi).astype(BF)


def nn(a, b):
    return jnp.dot(a, b, preferred_element_type=F32)


def nt(a, b):
    return lax.dot_general(a, b, (((1,), (1,)), ((), ())), preferred_element_type=F32)


def tn(a, b):
    return lax.dot_general(a, b, (((0,), (0,)), ((), ())), preferred_element_type=F32)


def diagonal(block):
    none = jnp.zeros_like(block)
    return rows(halves(block, none), halves(none, block))


def rows(*parts):
    return jnp.concatenate(parts, axis=0)


def lanes(*parts):
    return jnp.concatenate(parts, axis=1)


def kernel(
    vec_h, basis_h, lt_h, ut_h, uc_h, lc_h, far_h, near_h, tiles_h, out_ref,
    basis_v, lt_v, ut_v, uc_v, lc_v, far_s, near_s, tiles_v,
    arrived, points, coeffs, root_tile, nodes, heads, tails,
    dup, path_hi, path_lo, r0_hi, r0_lo, to_points, lifted_couplings, from_top, from_row, far_out, near_out, near_in,
    in_sem, send_sem, recv_sem, flag_0, flag_1,
):
    d = lax.axis_index("leaf")
    x = lax.axis_index("vec")
    y = d >> 4
    i = d & 15
    z = i >> 1
    c = i & 1

    def load(src, dst, n):
        copy = pltpu.make_async_copy(src, dst, in_sem.at[n])
        copy.start()
        return copy

    own = pl.ds(pl.multiple_of(16 * x, 16), 16)
    vec_in = load(vec_h, arrived.at[1, own], 0)
    basis_in = load(basis_h, basis_v, 1)
    lt_in = load(lt_h, lt_v, 2)

    right = (d + 1) & (LEAF_COUNT - 1)
    left = (d + LEAF_COUNT - 1) & (LEAF_COUNT - 1)
    sibling = d + 1 - 2 * c
    column_peers = [(d + ROW * k) & (LEAF_COUNT - 1) for k in (4, 3, 5, 2, 1, 6, 7)]
    vec_peers = [(x + k) & 3 for k in (2, 1, 3)]

    barrier = pltpu.get_barrier_semaphore()

    def announce(leaf, vec):
        pl.semaphore_signal(barrier, inc=1, device_id={"leaf": leaf, "vec": vec}, device_id_type=MESH)

    @pl.when(z < 4)
    def _():
        for k in range(1, 8):
            announce(ROW * y + 2 * ((z + k) & 7), x)

    @pl.when(z >= 4)
    def _():
        for k in range(1, 8):
            announce(ROW * y + 2 * ((z + k) & 7) + 1, x)

    announce(sibling, x)
    near_start = z < 4
    announce((d + jnp.where(c == 0, LEAF_COUNT - 2 + (z >> 2), jnp.where(z == 7, 2, 1))) & (LEAF_COUNT - 1), x)
    for peer in vec_peers:
        announce(d - c + (z >> 2), peer)
    for peer in column_peers:
        announce(peer - c + 1, x)

    ends = jnp.where(jnp.logical_or(z == 0, z == 3), 1, 0)
    last = jnp.where(z == 7, 1, 0)
    count_0 = jnp.where(near_start, 15 - ends, 10 + last)
    count_1 = jnp.where(near_start, 23 + ends, 28 - last)

    def tell(flag):
        pl.semaphore_signal(flag, inc=1, device_id={"leaf": sibling, "vec": x}, device_id_type=MESH)

    @pl.when(jnp.logical_and(c == 0, z == 7))
    def _():
        pl.semaphore_wait(barrier, count_0)
        tell(flag_0)

    ut_in = [
        load(ut_h.at[:, pl.ds(pl.multiple_of(1024 * y, 128), 1024)], ut_v.at[:, 0:1024], 3),
        load(ut_h.at[:, pl.ds(pl.multiple_of(8192 + 512 * y, 128), 512)], ut_v.at[:, 1024:1536], 4),
        load(ut_h.at[:, pl.ds(pl.multiple_of(12288 + 256 * y, 128), 256)], ut_v.at[:, 1536:1792], 5),
        load(ut_h.at[:, pl.ds(pl.multiple_of(14336 + 128 * y, 128), 128)], ut_v.at[:, 1792:1920], 6),
        load(ut_h.at[:, 15360:15872], ut_v.at[:, 1920:2432], 7),
    ]

    def send(src, dst, n_send, n_recv, leaf, vec):
        copy = pltpu.make_async_remote_copy(
            src_ref=src, dst_ref=dst, send_sem=send_sem.at[n_send], recv_sem=recv_sem.at[n_recv],
            device_id={"leaf": leaf, "vec": vec}, device_id_type=MESH,
        )
        copy.start()
        return copy

    def wait_for(ref, sem):
        pltpu.make_async_copy(ref, ref, sem).wait()

    def send_root(t):
        send(root_tile, nodes.at[i], 1, 1, ROW * y + t, x)

    def to_vec_peers():
        for peer in vec_peers:
            send(vec_h, arrived.at[1, own], 0, 0, d, peer)

    def far_right():
        send(coeffs.at[8:16, 0], coeffs.at[0:8, 0], 2, 2, right, x)

    def far_left():
        send(coeffs.at[8:16, 0], coeffs.at[16:24, 0], 3, 3, left, x)

    def near_right():
        send(arrived.at[1], arrived.at[0], 4, 4, right, x)

    def near_left():
        send(arrived.at[1], arrived.at[2], 5, 5, left, x)

    row_end = jnp.logical_and(c == 1, z == 7)
    row_start = jnp.logical_and(c == 0, z == 0)
    left_now = jnp.logical_and(near_start, jnp.logical_or(c == 1, z > 0))
    right_now = jnp.logical_and(near_start, jnp.logical_or(c == 0, z < 3))
    left_later = jnp.logical_not(jnp.logical_or(left_now, row_start))
    right_later = jnp.logical_not(jnp.logical_or(right_now, row_end))

    vec_in.wait()
    basis_in.wait()
    lt_in.wait()

    def local_top():
        transfer = lt_v[:, 1792:1920]
        crossed = turned(transfer)
        return halves(transfer, crossed), halves(crossed, transfer)

    top = local_top()

    group = lax.broadcasted_iota(jnp.int32, (16, 256), 1) >> 6
    zero = jnp.zeros((16, 256), BF)

    def paired(product):
        return [
            halves(product[0:16, 0:128], product[16:32, 0:128]),
            halves(product[32:48, 128:256], product[48:64, 128:256]),
        ]

    leaves = []
    for q in range(4):
        tile = arrived[1, own, 256 * q : 256 * q + 256]
        block = basis_v[:, 256 * q : 256 * q + 256]
        spread = rows(*[jnp.where(group == e, tile, zero) for e in range(4)])
        leaves.append(nt(spread, rows(block, block)))
    for j in range(8):
        pair = leaves[j // 2][32 * (j % 2) : 32 * (j % 2) + 32]
        coeffs[8 + j, 0] = halves(pair[0:16], pair[16:32]).astype(BF)
        coeffs[8 + j, 1] = halves(pair[16:32], pair[0:16]).astype(BF)

    @pl.when(row_end)
    def _():
        pl.semaphore_wait(flag_0, 1)
        send(vec_h, arrived.at[0, own], 10, 4, right, x)
        far_right()

    current = []
    for q in range(4):
        transfer = lt_v[:, 256 * q : 256 * q + 256]
        current += paired(nn(hilo(leaves[q]), rows(transfer, transfer)))
    for start in (1024, 1536):
        following = []
        for q in range(len(current) // 4):
            hi, lo = two_terms(rows(*current[4 * q : 4 * q + 4]))
            transfer = lt_v[:, start + 256 * q : start + 256 * q + 256]
            following += paired(nn(lanes(hi, lo), rows(transfer, transfer, transfer, transfer)))
        current = following
    first_hi, first_lo = two_terms(current[0])
    second_hi, second_lo = two_terms(current[1])
    root = nn(lanes(first_hi, first_lo, second_hi, second_lo), rows(*([top[0]] * 4 + [top[1]] * 4)))
    root_tile[...] = hilo(root)
    nodes[i] = root_tile[...]

    late_loads = [
        pltpu.make_async_copy(src, dst, in_sem.at[8 + n])
        for n, (src, dst) in enumerate(
            ((uc_h, uc_v), (lc_h, lc_v), (far_h, far_s), (near_h, near_s), (tiles_h, tiles_v))
        )
    ]
    uc_in, lc_in, far_in_s, near_in_s, tiles_in = late_loads

    def roots_out():
        @pl.when(jnp.logical_and(c == 0, z < 7))
        def _():
            pl.semaphore_wait(barrier, count_0)
            tell(flag_0)

        @pl.when(jnp.logical_and(c == 1, z < 7))
        def _():
            pl.semaphore_wait(flag_0, 1)

        for k in range(1, 8):
            send_root((i + k) & 7)

        @pl.when(z >= 4)
        def _():
            send_root(i & 7)

        @pl.when(near_start)
        def _():
            to_vec_peers()

        @pl.when(left_now)
        def _():
            far_left()

        @pl.when(right_now)
        def _():
            far_right()

        for copy in late_loads:
            copy.start()

    def matrices():
        for copy in ut_in:
            copy.wait()
        for p in range(19):
            pair = ut_v[:, 128 * p : 128 * p + 128]
            swapped = turned(pair)
            dup[2 * p] = halves(pair, swapped)
            dup[2 * p + 1] = halves(swapped, pair)

        path = dup[i]
        path_hi[0] = path
        path = path.astype(F32)
        below = local_top()
        below = [(below[0], None), (below[1], None)]
        row_below = [(dup[28], None), (dup[29], None)]

        def path_step(path, u):
            matrix = dup[BASES[u] + (i >> u if u < 4 else y)]
            path = nn(hilo(path), rows(matrix, matrix))
            path_hi[u], path_lo[u] = two_terms(path)
            return path

        def product_step(below, transfers, start):
            following = []
            for m, (hi, lo) in enumerate(below):
                left_side = diagonal(transfers[:, start + 128 * m : start + 128 * m + 128])
                if lo is None:
                    product = nn(left_side, rows(hi, hi))
                else:
                    product = nn(lanes(left_side, left_side), rows(hi, hi, lo, lo))
                hi, lo = two_terms(product)
                following += [(hi[0:64], lo[0:64]), (hi[64:128], lo[64:128])]
            return following

        for u, start in ((1, 1536), (2, 1024), (3, 0)):
            path = path_step(path, u)
            below = product_step(below, lt_v, start)
            row_below = product_step(row_below, ut_v, start)
        path_step(path, 4)
        for m in range(8):
            r0_hi[m] = rows(below[2 * m][0], below[2 * m + 1][0])
            r0_lo[m] = rows(below[2 * m][1], below[2 * m + 1][1])
        for m, (hi, lo) in enumerate(row_below):
            from_row[0, m] = rows(hi, hi)
            from_row[1, m] = rows(lo, lo)

    def turn(n, carry):
        @pl.when(n == (z >> 2))
        def _():
            matrices()

        @pl.when(n == 0)
        def _():
            roots_out()

        return carry

    lax.fori_loop(0, 2, turn, 0)

    def fold(j, carry):
        at = pl.ds(pl.multiple_of(128 * j, 128), 128)
        block = diagonal(basis_v[:, at])
        hi, lo = two_terms(tn(r0_hi[j], block) + tn(r0_lo[j], block))
        to_points[0:128, at] = hi
        to_points[128:256, at] = lo
        return carry

    lax.fori_loop(0, 8, fold, 0, unroll=2)

    @pl.when(near_start)
    def _():
        wait_for(arrived.at[1, 0:48], recv_sem.at[0])

    @pl.when(left_now)
    def _():
        near_left()

    @pl.when(right_now)
    def _():
        near_right()

    uc_in.wait()
    couplings = rows(uc_v[...], uc_v[...])
    for e in range(2):
        value = nn(halves(path_hi[3 + e], path_lo[3 + e]), couplings)
        value = jnp.transpose(rows(value, value))
        for o in range(4):
            lifted_couplings[e, o] = value[64 * o : 64 * o + 64]

    def slot(offset, odd):
        index = jnp.where(offset == -3, 0, jnp.where(offset == -2, 1, jnp.where(offset == 2, 2, 3)))
        wide = jnp.logical_or(
            jnp.logical_and(offset == -3, odd == 1), jnp.logical_and(offset == 3, odd == 0)
        )
        valid = jnp.logical_or(jnp.logical_or(offset == -2, offset == 2), wide)
        return index, jnp.where(valid, 1.0, 0.0).astype(F32)

    def gather_top(n, carry):
        index, keep = slot(n - y, y & 1)
        value = lifted_couplings[0, index] * keep
        index, keep = slot((n >> 1) - (y >> 1), (y >> 1) & 1)
        hi, lo = two_terms(lifted_couplings[1, index] * keep)
        hi, lo = two_terms(value + nn(dup[30 + n], rows(hi, lo)))
        from_top[0, n] = rows(hi, hi)
        from_top[1, n] = rows(lo, lo)
        return carry

    lax.fori_loop(0, 8, gather_top, 0, unroll=4)

    def fill(w):
        def step(j, carry):
            block = arrived[w, :, pl.ds(pl.multiple_of(128 * j, 128), 128)]
            points[8 * w + j, 0] = block
            points[8 * w + j, 1] = turned(block)
            return carry

        lax.fori_loop(0, 8, step, 0, unroll=2)

    @pl.when(c == 1)
    def _():
        pl.semaphore_wait(barrier, count_1)
        tell(flag_1)

    @pl.when(c == 0)
    def _():
        pl.semaphore_wait(flag_1, 1)

    for k in range(1, 8):
        send_root(8 + ((i + k) & 7))

    @pl.when(z < 4)
    def _():
        send_root(8 + i)

    @pl.when(z >= 4)
    def _():
        to_vec_peers()

    @pl.when(jnp.logical_not(left_now))
    def _():
        far_left()

    @pl.when(right_later)
    def _():
        far_right()

    @pl.when(z >= 4)
    def _():
        wait_for(arrived.at[1, 0:48], recv_sem.at[0])

    @pl.when(row_start)
    def _():
        send(vec_h, arrived.at[2, own], 11, 5, left, x)

    @pl.when(left_later)
    def _():
        near_left()

    @pl.when(right_later)
    def _():
        near_right()

    fill(1)

    first_leaf = ROW * d - ROW

    def chosen(table, lists, slots, column):
        parts = []
        for s in range(0, slots, 2):
            a = jnp.clip(lists[s, column] - first_leaf, 0, 3 * ROW - 1)
            b = jnp.clip(lists[s + 1, column] - first_leaf, 0, 3 * ROW - 1)
            parts.append(halves(table[a >> 1, a & 1], table[b >> 1, 1 - (b & 1)]))
        return lanes(*parts)

    def far_part():
        far_in_s.wait()
        lc_in.wait()
        wait_for(coeffs.at[0:8, 0], recv_sem.at[2])
        wait_for(coeffs.at[16:24, 0], recv_sem.at[3])
        for p in list(range(8)) + list(range(16, 24)):
            coeffs[p, 1] = turned(coeffs[p, 0])
        for j in range(8):
            source = rows(*[chosen(coeffs, far_s, 6, 2 * j + e) for e in range(2)])
            value = nt(source, rows(lc_v[:, 768 * j : 768 * j + 384], lc_v[:, 768 * j + 384 : 768 * j + 768]))
            hi, lo = two_terms(halves(value[0:16], value[16:32]))
            block = diagonal(basis_v[:, 128 * j : 128 * j + 128])
            far_out[j] = nn(lanes(hi, lo), rows(block, block))

    def near_part():
        near_in_s.wait()
        tiles_in.wait()

        @pl.when(row_start)
        def _():
            wait_for(arrived.at[0, 0:48], recv_sem.at[10])

        @pl.when(jnp.logical_not(row_start))
        def _():
            wait_for(arrived.at[0], recv_sem.at[4])

        @pl.when(row_end)
        def _():
            wait_for(arrived.at[2, 0:48], recv_sem.at[11])

        @pl.when(jnp.logical_not(row_end))
        def _():
            wait_for(arrived.at[2], recv_sem.at[5])

        fill(0)
        fill(2)
        for q in range(2):
            source = rows(*[chosen(points, near_s, 6, 4 * x + 2 * q + e) for e in range(2)])
            value = nt(source, rows(tiles_v[2 * q], tiles_v[2 * q + 1]))
            value = halves(value[0:64], value[64:128]).astype(BF)
            for v in range(4):
                near_out[v, q] = value[16 * v : 16 * v + 16]
        for n, peer in enumerate(vec_peers):
            send(near_out.at[peer], near_in.at[x], 9, 9, d, peer)
        near_in[x] = near_out[x]

    @pl.when(row_start)
    def _():
        wait_for(arrived.at[0, 0:16], recv_sem.at[4])
        for peer in vec_peers:
            send(arrived.at[0, own], arrived.at[0, own], 10, 10, d, peer)

    def row_tree():
        wait_for(nodes.at[0:15], recv_sem.at[1])

        @pl.when(row_end)
        def _():
            wait_for(arrived.at[2, 0:16], recv_sem.at[5])
            for peer in vec_peers:
                send(arrived.at[2, own], arrived.at[2, own], 11, 11, d, peer)

        roots = lanes(*[nodes[m] for m in range(ROW)])
        top_tile = hilo(nn(roots, from_row[0].reshape(2048, 128)) + nn(roots, from_row[1].reshape(2048, 128)))
        nodes[30 + y] = top_tile
        heads[8] = top_tile
        tails[8] = top_tile
        for peer in column_peers[:4] + column_peers[5:6]:
            send(nodes.at[30 + y], nodes.at[30 + y], 8, 8, peer, x)
        for u in range(3):
            base, count = BASES[u], ROW >> u
            for m in range(count // 2):
                left_m, right_m = dup[base + 2 * m], dup[base + 2 * m + 1]
                value = nn(lanes(nodes[base + 2 * m], nodes[base + 2 * m + 1]), rows(left_m, left_m, right_m, right_m))
                nodes[BASES[u + 1] + m] = hilo(value)
        for u in range(4):
            for e in range(2):
                heads[2 * u + e] = nodes[BASES[u] + e]
                tails[2 * u + e] = nodes[BASES[u + 1] - 2 + e]
        send(tails, nodes.at[PREV : PREV + 9], 6, 6, column_peers[4], x)
        send(heads, nodes.at[NEXT : NEXT + 9], 7, 7, column_peers[6], x)

    row_tree()
    near_part()
    far_part()

    weights = []
    for o in range(2):
        pair = uc_v[:, 128 * o : 128 * o + 128]
        swapped = turned(pair)
        weights += [halves(pair, swapped), halves(swapped, pair)]
    weights = lanes(*weights)
    wait_for(nodes.at[0:9], recv_sem.at[6])
    wait_for(nodes.at[0:9], recv_sem.at[7])
    sources = []
    for u in range(4):
        g = d >> u
        odd = g & 1
        number = LEAF_COUNT >> u
        count = ROW >> u
        parts = []
        for o, wanted in ((-3, odd == 1), (-2, None), (2, None), (3, odd == 0)):
            shift = o if wanted is None else (-3 * odd if o < 0 else 3 * (1 - odd))
            place = (i >> u) + shift
            place = jnp.where(
                place < 0,
                PREV + 2 + 2 * u + place,
                jnp.where(place < count, BASES[u] + place, NEXT + 2 * u - count + place),
            )
            valid = (g + o >= 0) if o < 0 else (g + o < number)
            if wanted is not None:
                valid = jnp.logical_and(valid, wanted)
            keep = jnp.where(valid, 1.0, 0.0).astype(F32)
            parts.append((nodes[place].astype(F32) * keep).astype(BF))
        sources.append(lanes(*parts))
    coupled = nt(rows(*sources), rows(weights, weights))
    left_side, right_side = [], []
    for u in range(1, 4):
        tile = hilo(coupled[16 * u : 16 * u + 16])
        left_side.append(tile)
        right_side.append(path_hi[u - 1])
        if u > 1:
            left_side.append(tile)
            right_side.append(path_lo[u - 1])
    matrix = lanes(*right_side)
    down = coupled[0:16] + nt(lanes(*left_side), rows(matrix, matrix))

    nodes[30 + ((y + 7) & 7)] = nodes[PREV + 8]
    nodes[30 + ((y + 1) & 7)] = nodes[NEXT + 8]
    wait_for(nodes.at[0:5], recv_sem.at[8])
    tops = lanes(*[nodes[30 + n] for n in range(8)])
    down = down + nn(tops, from_top[0].reshape(1024, 128)) + nn(tops, from_top[1].reshape(1024, 128))
    down = hilo(down)
    value = nn(lanes(down, down), to_points[...])
    wait_for(near_in.at[0:3], recv_sem.at[9])
    for j in range(8):
        at = slice(128 * j, 128 * j + 128)
        out_ref[:, at] = (value[:, at] + far_out[j] + near_in[j // 2, j % 2].astype(F32)).astype(BF)

    wait_for(arrived.at[1, 0:48], send_sem.at[0])
    wait_for(nodes.at[0:15], send_sem.at[1])
    wait_for(coeffs.at[0:8, 0], send_sem.at[2])
    wait_for(coeffs.at[0:8, 0], send_sem.at[3])

    @pl.when(row_end)
    def _():
        wait_for(arrived.at[0, 0:16], send_sem.at[10])
        wait_for(arrived.at[2, 0:48], send_sem.at[11])

    @pl.when(row_start)
    def _():
        wait_for(arrived.at[0, 0:48], send_sem.at[10])
        wait_for(arrived.at[2, 0:16], send_sem.at[11])

    @pl.when(jnp.logical_not(row_end))
    def _():
        wait_for(arrived.at[0], send_sem.at[4])

    @pl.when(jnp.logical_not(row_start))
    def _():
        wait_for(arrived.at[2], send_sem.at[5])

    wait_for(nodes.at[0:9], send_sem.at[6])
    wait_for(nodes.at[0:9], send_sem.at[7])
    wait_for(nodes.at[0:5], send_sem.at[8])
    wait_for(near_out.at[0:3], send_sem.at[9])


def shards(vectors, leaf_basis, local_transfer, upper_transfer, upper_coupling, leaf_coupling, far_list, near_list, near_tiles):
    tile = (16, 128)
    scratch = [
        pltpu.VMEM(leaf_basis.shape, BF),
        pltpu.VMEM(local_transfer.shape, BF),
        pltpu.VMEM((64, 2432), BF),
        pltpu.VMEM(upper_coupling.shape, BF),
        pltpu.VMEM(leaf_coupling.shape, BF),
        pltpu.SMEM(far_list.shape, jnp.int32),
        pltpu.SMEM(near_list.shape, jnp.int32),
        pltpu.VMEM(near_tiles.shape, BF),
        pltpu.VMEM((3, 64, 1024), BF),
        pltpu.VMEM((24, 2, 64, 128), BF),
        pltpu.VMEM((24, 2) + tile, BF),
        pltpu.VMEM(tile, BF),
        pltpu.VMEM((60,) + tile, BF),
        pltpu.VMEM((9,) + tile, BF),
        pltpu.VMEM((9,) + tile, BF),
        pltpu.VMEM((38, 64, 128), BF),
        pltpu.VMEM((5, 64, 128), BF),
        pltpu.VMEM((5, 64, 128), BF),
        pltpu.VMEM((8, 128, 128), BF),
        pltpu.VMEM((8, 128, 128), BF),
        pltpu.VMEM((256, 1024), BF),
        pltpu.VMEM((2, 4, 64, 128), F32),
        pltpu.VMEM((2, 8, 128, 128), BF),
        pltpu.VMEM((2, ROW, 128, 128), BF),
        pltpu.VMEM((8,) + tile, F32),
        pltpu.VMEM((4, 2) + tile, BF),
        pltpu.VMEM((4, 2) + tile, BF),
        pltpu.SemaphoreType.DMA((13,)),
        pltpu.SemaphoreType.DMA((12,)),
        pltpu.SemaphoreType.DMA((12,)),
        pltpu.SemaphoreType.REGULAR,
        pltpu.SemaphoreType.REGULAR,
    ]
    return pl.pallas_call(
        kernel,
        out_shape=pltpu.VMEM(vectors.shape, BF),
        in_specs=[pl.BlockSpec(memory_space=pl.ANY)] * 9,
        out_specs=pl.BlockSpec(memory_space=pltpu.VMEM),
        scratch_shapes=scratch,
        compiler_params=pltpu.CompilerParams(
            collective_id=0, has_side_effects=True, vmem_limit_bytes=62 * 1024 * 1024
        ),
    )(vectors, leaf_basis, local_transfer, upper_transfer, upper_coupling, leaf_coupling, far_list, near_list, near_tiles)


def solution(mesh):
    placed = (
        P("vec", "leaf"),
        P(None, "leaf"),
        P(None, "leaf"),
        P(),
        P(),
        P(None, "leaf"),
        P(None, "leaf"),
        P(None, "leaf"),
        P(("leaf", "vec"), None, None),
    )
    return jax.shard_map(
        shards, mesh=mesh, in_specs=placed, out_specs=P("vec", "leaf"), check_vma=False
    )
```

```python
import jax
import jax.numpy as jnp
from jax import lax
from jax.experimental import pallas as pl
from jax.experimental.pallas import tpu as pltpu
from jax.sharding import PartitionSpec as P

MESH = pl.DeviceIdType.MESH
BF = jnp.bfloat16
F32 = jnp.float32
ROW = 16
ROWS = 8
LEAF_COUNT = ROW * ROWS
BASES = (0, 16, 24, 28, 30)
PREV = 42
NEXT = 51


def low(shape):
    return lax.broadcasted_iota(jnp.int32, shape, 1) < 64


def halves(a, b):
    return jnp.where(low(a.shape), a, b)


def turned(tile):
    return pltpu.roll(tile, 64, 1)


def rounded(x):
    return x.astype(BF).astype(F32)


def hilo(x):
    hi = rounded(x)
    return halves(hi, x - hi).astype(BF)


def two_terms(x):
    hi = rounded(x)
    return hi.astype(BF), (x - hi).astype(BF)


def nn(a, b):
    return jnp.dot(a, b, preferred_element_type=F32)


def nt(a, b):
    return lax.dot_general(a, b, (((1,), (1,)), ((), ())), preferred_element_type=F32)


def tn(a, b):
    return lax.dot_general(a, b, (((0,), (0,)), ((), ())), preferred_element_type=F32)


def diagonal(block):
    none = jnp.zeros_like(block)
    return rows(halves(block, none), halves(none, block))


def rows(*parts):
    return jnp.concatenate(parts, axis=0)


def lanes(*parts):
    return jnp.concatenate(parts, axis=1)


def kernel(
    vec_h, basis_h, lt_h, ut_h, uc_h, lc_h, far_h, near_h, tiles_h, out_ref,
    basis_v, lt_v, ut_v, uc_v, lc_v, far_s, near_s, tiles_v,
    arrived, points, coeffs, root_tile, nodes, heads, tails,
    dup, path_hi, path_lo, r0_hi, r0_lo, to_points, lifted_couplings, from_top, from_row, far_out, near_out, near_in,
    in_sem, send_sem, recv_sem, flag_0, flag_1,
):
    d = lax.axis_index("leaf")
    x = lax.axis_index("vec")
    y = d >> 4
    i = d & 15
    z = i >> 1
    c = i & 1
    row_end = jnp.logical_and(c == 1, z == 7)
    row_start = jnp.logical_and(c == 0, z == 0)

    def load(src, dst, n):
        copy = pltpu.make_async_copy(src, dst, in_sem.at[n])
        copy.start()
        return copy

    own = pl.ds(pl.multiple_of(16 * x, 16), 16)
    vec_in = load(vec_h, arrived.at[1, own], 0)
    basis_in = load(basis_h, basis_v, 1)
    lt_in = load(lt_h, lt_v, 2)

    right = (d + 1) & (LEAF_COUNT - 1)
    left = (d + LEAF_COUNT - 1) & (LEAF_COUNT - 1)
    sibling = d + 1 - 2 * c
    column_peers = [(d + ROW * k) & (LEAF_COUNT - 1) for k in (4, 3, 5, 2, 1, 6, 7)]
    vec_peers = [(x + k) & 3 for k in (2, 1, 3)]

    barrier = pltpu.get_barrier_semaphore()

    def announce(leaf, vec):
        pl.semaphore_signal(barrier, inc=1, device_id={"leaf": leaf, "vec": vec}, device_id_type=MESH)

    announce(sibling, x)
    near_start = z < 4
    ends = jnp.where(jnp.logical_or(z == 0, z == 3), 1, 0)
    last = jnp.where(z == 7, 1, 0)
    count_0 = jnp.where(near_start, 15 - ends, 10 + 4 * last)
    count_1 = jnp.where(near_start, 23 + ends, 28 - last)

    def tell(flag):
        pl.semaphore_signal(flag, inc=1, device_id={"leaf": sibling, "vec": x}, device_id_type=MESH)

    @pl.when(jnp.logical_and(c == 0, z == 7))
    def _():
        pl.semaphore_wait(barrier, count_0)
        tell(flag_0)

    @pl.when(row_start)
    def _():
        for peer in vec_peers:
            announce((d + LEAF_COUNT - 2) & (LEAF_COUNT - 1), peer)

    @pl.when(z < 4)
    def _():
        for k in range(1, 8):
            announce(ROW * y + 2 * ((z + k) & 7), x)

    @pl.when(z >= 4)
    def _():
        for k in range(1, 8):
            announce(ROW * y + 2 * ((z + k) & 7) + 1, x)

    announce((d + jnp.where(c == 0, LEAF_COUNT - 2 + (z >> 2), jnp.where(z == 7, 2, 1))) & (LEAF_COUNT - 1), x)
    for peer in vec_peers:
        announce(d - c + (z >> 2), peer)
    for peer in column_peers:
        announce(peer - c + 1, x)


    ut_in = [
        load(ut_h.at[:, pl.ds(pl.multiple_of(1024 * y, 128), 1024)], ut_v.at[:, 0:1024], 3),
        load(ut_h.at[:, pl.ds(pl.multiple_of(8192 + 512 * y, 128), 512)], ut_v.at[:, 1024:1536], 4),
        load(ut_h.at[:, pl.ds(pl.multiple_of(12288 + 256 * y, 128), 256)], ut_v.at[:, 1536:1792], 5),
        load(ut_h.at[:, pl.ds(pl.multiple_of(14336 + 128 * y, 128), 128)], ut_v.at[:, 1792:1920], 6),
        load(ut_h.at[:, 15360:15872], ut_v.at[:, 1920:2432], 7),
    ]

    def send(src, dst, n_send, n_recv, leaf, vec):
        copy = pltpu.make_async_remote_copy(
            src_ref=src, dst_ref=dst, send_sem=send_sem.at[n_send], recv_sem=recv_sem.at[n_recv],
            device_id={"leaf": leaf, "vec": vec}, device_id_type=MESH,
        )
        copy.start()
        return copy

    def wait_for(ref, sem):
        pltpu.make_async_copy(ref, ref, sem).wait()

    def send_root(t):
        send(root_tile, nodes.at[i], 1, 1, ROW * y + t, x)

    def to_vec_peers():
        for peer in vec_peers:
            send(vec_h, arrived.at[1, own], 0, 0, d, peer)

    def far_right():
        send(coeffs.at[8:16, 0], coeffs.at[0:8, 0], 2, 2, right, x)

    def far_left():
        send(coeffs.at[8:16, 0], coeffs.at[16:24, 0], 3, 3, left, x)

    def near_right():
        send(arrived.at[1], arrived.at[0], 4, 4, right, x)

    def near_left():
        send(arrived.at[1], arrived.at[2], 5, 5, left, x)

    left_now = jnp.logical_and(near_start, jnp.logical_or(c == 1, z > 0))
    right_now = jnp.logical_and(near_start, jnp.logical_or(c == 0, z < 3))
    left_later = jnp.logical_not(jnp.logical_or(left_now, row_start))
    right_later = jnp.logical_not(jnp.logical_or(right_now, row_end))

    @pl.when(row_end)
    def _():
        pl.semaphore_wait(flag_0, 1)
        for peer in [x] + vec_peers:
            send(vec_h, arrived.at[0, own], 10, 4, right, peer)

    vec_in.wait()
    basis_in.wait()
    lt_in.wait()

    def local_top():
        transfer = lt_v[:, 1792:1920]
        crossed = turned(transfer)
        return halves(transfer, crossed), halves(crossed, transfer)

    top = local_top()

    group = lax.broadcasted_iota(jnp.int32, (16, 256), 1) >> 6
    zero = jnp.zeros((16, 256), BF)

    def paired(product):
        return [
            halves(product[0:16, 0:128], product[16:32, 0:128]),
            halves(product[32:48, 128:256], product[48:64, 128:256]),
        ]

    leaves = []
    for q in range(4):
        tile = arrived[1, own, 256 * q : 256 * q + 256]
        block = basis_v[:, 256 * q : 256 * q + 256]
        spread = rows(*[jnp.where(group == e, tile, zero) for e in range(4)])
        leaves.append(nt(spread, rows(block, block)))
    for j in range(8):
        pair = leaves[j // 2][32 * (j % 2) : 32 * (j % 2) + 32]
        coeffs[8 + j, 0] = halves(pair[0:16], pair[16:32]).astype(BF)
        coeffs[8 + j, 1] = halves(pair[16:32], pair[0:16]).astype(BF)

    @pl.when(row_end)
    def _():
        far_right()

    current = []
    for q in range(4):
        transfer = lt_v[:, 256 * q : 256 * q + 256]
        current += paired(nn(hilo(leaves[q]), rows(transfer, transfer)))
    for start in (1024, 1536):
        following = []
        for q in range(len(current) // 4):
            hi, lo = two_terms(rows(*current[4 * q : 4 * q + 4]))
            transfer = lt_v[:, start + 256 * q : start + 256 * q + 256]
            following += paired(nn(lanes(hi, lo), rows(transfer, transfer, transfer, transfer)))
        current = following
    first_hi, first_lo = two_terms(current[0])
    second_hi, second_lo = two_terms(current[1])
    root = nn(lanes(first_hi, first_lo, second_hi, second_lo), rows(*([top[0]] * 4 + [top[1]] * 4)))
    root_tile[...] = hilo(root)
    nodes[i] = root_tile[...]

    late_loads = [
        pltpu.make_async_copy(src, dst, in_sem.at[8 + n])
        for n, (src, dst) in enumerate(
            ((uc_h, uc_v), (lc_h, lc_v), (far_h, far_s), (near_h, near_s), (tiles_h, tiles_v))
        )
    ]
    uc_in, lc_in, far_in_s, near_in_s, tiles_in = late_loads

    def roots_out():
        @pl.when(jnp.logical_and(c == 0, z < 7))
        def _():
            pl.semaphore_wait(barrier, count_0)
            tell(flag_0)

        @pl.when(jnp.logical_and(c == 1, z < 7))
        def _():
            pl.semaphore_wait(flag_0, 1)

        for k in range(1, 8):
            send_root((i + k) & 7)

        @pl.when(z >= 4)
        def _():
            send_root(i & 7)

        @pl.when(near_start)
        def _():
            to_vec_peers()

        @pl.when(left_now)
        def _():
            far_left()

        @pl.when(right_now)
        def _():
            far_right()

        for copy in late_loads:
            copy.start()

    def matrices():
        for copy in ut_in:
            copy.wait()
        for p in range(19):
            pair = ut_v[:, 128 * p : 128 * p + 128]
            swapped = turned(pair)
            dup[2 * p] = halves(pair, swapped)
            dup[2 * p + 1] = halves(swapped, pair)

        path = dup[i]
        path_hi[0] = path
        path = path.astype(F32)
        below = local_top()
        below = [(below[0], None), (below[1], None)]
        row_below = [(dup[28], None), (dup[29], None)]

        def path_step(path, u):
            matrix = dup[BASES[u] + (i >> u if u < 4 else y)]
            path = nn(hilo(path), rows(matrix, matrix))
            path_hi[u], path_lo[u] = two_terms(path)
            return path

        def product_step(below, transfers, start):
            following = []
            for m, (hi, lo) in enumerate(below):
                left_side = diagonal(transfers[:, start + 128 * m : start + 128 * m + 128])
                if lo is None:
                    product = nn(left_side, rows(hi, hi))
                else:
                    product = nn(lanes(left_side, left_side), rows(hi, hi, lo, lo))
                hi, lo = two_terms(product)
                following += [(hi[0:64], lo[0:64]), (hi[64:128], lo[64:128])]
            return following

        for u, start in ((1, 1536), (2, 1024), (3, 0)):
            path = path_step(path, u)
            below = product_step(below, lt_v, start)
            row_below = product_step(row_below, ut_v, start)
        path_step(path, 4)
        for m in range(8):
            r0_hi[m] = rows(below[2 * m][0], below[2 * m + 1][0])
            r0_lo[m] = rows(below[2 * m][1], below[2 * m + 1][1])
        for m, (hi, lo) in enumerate(row_below):
            from_row[0, m] = rows(hi, hi)
            from_row[1, m] = rows(lo, lo)

    def turn(n, carry):
        @pl.when(n == (z >> 2))
        def _():
            matrices()

        @pl.when(n == 0)
        def _():
            roots_out()

        return carry

    lax.fori_loop(0, 2, turn, 0)

    def fold(j, carry):
        at = pl.ds(pl.multiple_of(128 * j, 128), 128)
        block = diagonal(basis_v[:, at])
        hi, lo = two_terms(tn(r0_hi[j], block) + tn(r0_lo[j], block))
        to_points[0:128, at] = hi
        to_points[128:256, at] = lo
        return carry

    lax.fori_loop(0, 8, fold, 0, unroll=2)

    @pl.when(near_start)
    def _():
        wait_for(arrived.at[1, 0:48], recv_sem.at[0])

    @pl.when(left_now)
    def _():
        near_left()

    @pl.when(right_now)
    def _():
        near_right()

    uc_in.wait()
    couplings = rows(uc_v[...], uc_v[...])
    for e in range(2):
        value = nn(halves(path_hi[3 + e], path_lo[3 + e]), couplings)
        value = jnp.transpose(rows(value, value))
        for o in range(4):
            lifted_couplings[e, o] = value[64 * o : 64 * o + 64]

    def slot(offset, odd):
        index = jnp.where(offset == -3, 0, jnp.where(offset == -2, 1, jnp.where(offset == 2, 2, 3)))
        wide = jnp.logical_or(
            jnp.logical_and(offset == -3, odd == 1), jnp.logical_and(offset == 3, odd == 0)
        )
        valid = jnp.logical_or(jnp.logical_or(offset == -2, offset == 2), wide)
        return index, jnp.where(valid, 1.0, 0.0).astype(F32)

    def gather_top(n, carry):
        index, keep = slot(n - y, y & 1)
        value = lifted_couplings[0, index] * keep
        index, keep = slot((n >> 1) - (y >> 1), (y >> 1) & 1)
        hi, lo = two_terms(lifted_couplings[1, index] * keep)
        hi, lo = two_terms(value + nn(dup[30 + n], rows(hi, lo)))
        from_top[0, n] = rows(hi, hi)
        from_top[1, n] = rows(lo, lo)
        return carry

    lax.fori_loop(0, 8, gather_top, 0, unroll=4)

    def fill(w):
        def step(j, carry):
            block = arrived[w, :, pl.ds(pl.multiple_of(128 * j, 128), 128)]
            points[8 * w + j, 0] = block
            points[8 * w + j, 1] = turned(block)
            return carry

        lax.fori_loop(0, 8, step, 0, unroll=2)

    @pl.when(c == 1)
    def _():
        pl.semaphore_wait(barrier, count_1)
        tell(flag_1)

    @pl.when(c == 0)
    def _():
        pl.semaphore_wait(flag_1, 1)

    for k in range(1, 8):
        send_root(8 + ((i + k) & 7))

    @pl.when(z < 4)
    def _():
        send_root(8 + i)

    @pl.when(z >= 4)
    def _():
        to_vec_peers()

    @pl.when(jnp.logical_not(left_now))
    def _():
        far_left()

    @pl.when(right_later)
    def _():
        far_right()

    @pl.when(z >= 4)
    def _():
        wait_for(arrived.at[1, 0:48], recv_sem.at[0])

    @pl.when(row_start)
    def _():
        send(vec_h, arrived.at[2, own], 11, 5, left, x)

    @pl.when(left_later)
    def _():
        near_left()

    @pl.when(right_later)
    def _():
        near_right()

    fill(1)

    first_leaf = ROW * d - ROW

    def chosen(table, lists, slots, column):
        parts = []
        for s in range(0, slots, 2):
            a = jnp.clip(lists[s, column] - first_leaf, 0, 3 * ROW - 1)
            b = jnp.clip(lists[s + 1, column] - first_leaf, 0, 3 * ROW - 1)
            parts.append(halves(table[a >> 1, a & 1], table[b >> 1, 1 - (b & 1)]))
        return lanes(*parts)

    def far_part():
        far_in_s.wait()
        lc_in.wait()
        wait_for(coeffs.at[0:8, 0], recv_sem.at[2])
        wait_for(coeffs.at[16:24, 0], recv_sem.at[3])
        for p in list(range(8)) + list(range(16, 24)):
            coeffs[p, 1] = turned(coeffs[p, 0])
        for j in range(8):
            source = rows(*[chosen(coeffs, far_s, 6, 2 * j + e) for e in range(2)])
            value = nt(source, rows(lc_v[:, 768 * j : 768 * j + 384], lc_v[:, 768 * j + 384 : 768 * j + 768]))
            hi, lo = two_terms(halves(value[0:16], value[16:32]))
            block = diagonal(basis_v[:, 128 * j : 128 * j + 128])
            far_out[j] = nn(lanes(hi, lo), rows(block, block))

    def near_part():
        near_in_s.wait()
        tiles_in.wait()
        wait_for(arrived.at[0], recv_sem.at[4])

        @pl.when(row_end)
        def _():
            wait_for(arrived.at[2, 0:48], recv_sem.at[11])

        @pl.when(jnp.logical_not(row_end))
        def _():
            wait_for(arrived.at[2], recv_sem.at[5])

        fill(0)
        fill(2)
        for q in range(2):
            source = rows(*[chosen(points, near_s, 6, 4 * x + 2 * q + e) for e in range(2)])
            value = nt(source, rows(tiles_v[2 * q], tiles_v[2 * q + 1]))
            value = halves(value[0:64], value[64:128]).astype(BF)
            for v in range(4):
                near_out[v, q] = value[16 * v : 16 * v + 16]
        for n, peer in enumerate(vec_peers):
            send(near_out.at[peer], near_in.at[x], 9, 9, d, peer)
        near_in[x] = near_out[x]

    def row_tree():
        wait_for(nodes.at[0:15], recv_sem.at[1])

        @pl.when(row_end)
        def _():
            wait_for(arrived.at[2, 0:16], recv_sem.at[5])
            for peer in vec_peers:
                send(arrived.at[2, own], arrived.at[2, own], 11, 11, d, peer)

        roots = lanes(*[nodes[m] for m in range(ROW)])
        top_tile = hilo(nn(roots, from_row[0].reshape(2048, 128)) + nn(roots, from_row[1].reshape(2048, 128)))
        nodes[30 + y] = top_tile
        heads[8] = top_tile
        tails[8] = top_tile
        for peer in column_peers[:4] + column_peers[5:6]:
            send(nodes.at[30 + y], nodes.at[30 + y], 8, 8, peer, x)
        for u in range(3):
            base, count = BASES[u], ROW >> u
            for m in range(count // 2):
                left_m, right_m = dup[base + 2 * m], dup[base + 2 * m + 1]
                value = nn(lanes(nodes[base + 2 * m], nodes[base + 2 * m + 1]), rows(left_m, left_m, right_m, right_m))
                nodes[BASES[u + 1] + m] = hilo(value)
        for u in range(4):
            for e in range(2):
                heads[2 * u + e] = nodes[BASES[u] + e]
                tails[2 * u + e] = nodes[BASES[u + 1] - 2 + e]
        send(tails, nodes.at[PREV : PREV + 9], 6, 6, column_peers[4], x)
        send(heads, nodes.at[NEXT : NEXT + 9], 7, 7, column_peers[6], x)

    row_tree()
    near_part()
    far_part()

    weights = []
    for o in range(2):
        pair = uc_v[:, 128 * o : 128 * o + 128]
        swapped = turned(pair)
        weights += [halves(pair, swapped), halves(swapped, pair)]
    weights = lanes(*weights)
    wait_for(nodes.at[0:9], recv_sem.at[6])
    wait_for(nodes.at[0:9], recv_sem.at[7])
    sources = []
    for u in range(4):
        g = d >> u
        odd = g & 1
        number = LEAF_COUNT >> u
        count = ROW >> u
        parts = []
        for o, wanted in ((-3, odd == 1), (-2, None), (2, None), (3, odd == 0)):
            shift = o if wanted is None else (-3 * odd if o < 0 else 3 * (1 - odd))
            place = (i >> u) + shift
            place = jnp.where(
                place < 0,
                PREV + 2 + 2 * u + place,
                jnp.where(place < count, BASES[u] + place, NEXT + 2 * u - count + place),
            )
            valid = (g + o >= 0) if o < 0 else (g + o < number)
            if wanted is not None:
                valid = jnp.logical_and(valid, wanted)
            keep = jnp.where(valid, 1.0, 0.0).astype(F32)
            parts.append((nodes[place].astype(F32) * keep).astype(BF))
        sources.append(lanes(*parts))
    coupled = nt(rows(*sources), rows(weights, weights))
    left_side, right_side = [], []
    for u in range(1, 4):
        tile = hilo(coupled[16 * u : 16 * u + 16])
        left_side.append(tile)
        right_side.append(path_hi[u - 1])
        if u > 1:
            left_side.append(tile)
            right_side.append(path_lo[u - 1])
    matrix = lanes(*right_side)
    down = coupled[0:16] + nt(lanes(*left_side), rows(matrix, matrix))

    nodes[30 + ((y + 7) & 7)] = nodes[PREV + 8]
    nodes[30 + ((y + 1) & 7)] = nodes[NEXT + 8]
    wait_for(nodes.at[0:5], recv_sem.at[8])
    tops = lanes(*[nodes[30 + n] for n in range(8)])
    down = down + nn(tops, from_top[0].reshape(1024, 128)) + nn(tops, from_top[1].reshape(1024, 128))
    down = hilo(down)
    value = nn(lanes(down, down), to_points[...])
    wait_for(near_in.at[0:3], recv_sem.at[9])
    for j in range(8):
        at = slice(128 * j, 128 * j + 128)
        out_ref[:, at] = (value[:, at] + far_out[j] + near_in[j // 2, j % 2].astype(F32)).astype(BF)

    wait_for(arrived.at[1, 0:48], send_sem.at[0])
    wait_for(nodes.at[0:15], send_sem.at[1])
    wait_for(coeffs.at[0:8, 0], send_sem.at[2])
    wait_for(coeffs.at[0:8, 0], send_sem.at[3])

    @pl.when(row_end)
    def _():
        wait_for(arrived.at[0], send_sem.at[10])
        wait_for(arrived.at[2, 0:48], send_sem.at[11])

    @pl.when(row_start)
    def _():
        wait_for(arrived.at[2, 0:16], send_sem.at[11])

    @pl.when(jnp.logical_not(row_end))
    def _():
        wait_for(arrived.at[0], send_sem.at[4])

    @pl.when(jnp.logical_not(row_start))
    def _():
        wait_for(arrived.at[2], send_sem.at[5])

    wait_for(nodes.at[0:9], send_sem.at[6])
    wait_for(nodes.at[0:9], send_sem.at[7])
    wait_for(nodes.at[0:5], send_sem.at[8])
    wait_for(near_out.at[0:3], send_sem.at[9])


def shards(vectors, leaf_basis, local_transfer, upper_transfer, upper_coupling, leaf_coupling, far_list, near_list, near_tiles):
    tile = (16, 128)
    scratch = [
        pltpu.VMEM(leaf_basis.shape, BF),
        pltpu.VMEM(local_transfer.shape, BF),
        pltpu.VMEM((64, 2432), BF),
        pltpu.VMEM(upper_coupling.shape, BF),
        pltpu.VMEM(leaf_coupling.shape, BF),
        pltpu.SMEM(far_list.shape, jnp.int32),
        pltpu.SMEM(near_list.shape, jnp.int32),
        pltpu.VMEM(near_tiles.shape, BF),
        pltpu.VMEM((3, 64, 1024), BF),
        pltpu.VMEM((24, 2, 64, 128), BF),
        pltpu.VMEM((24, 2) + tile, BF),
        pltpu.VMEM(tile, BF),
        pltpu.VMEM((60,) + tile, BF),
        pltpu.VMEM((9,) + tile, BF),
        pltpu.VMEM((9,) + tile, BF),
        pltpu.VMEM((38, 64, 128), BF),
        pltpu.VMEM((5, 64, 128), BF),
        pltpu.VMEM((5, 64, 128), BF),
        pltpu.VMEM((8, 128, 128), BF),
        pltpu.VMEM((8, 128, 128), BF),
        pltpu.VMEM((256, 1024), BF),
        pltpu.VMEM((2, 4, 64, 128), F32),
        pltpu.VMEM((2, 8, 128, 128), BF),
        pltpu.VMEM((2, ROW, 128, 128), BF),
        pltpu.VMEM((8,) + tile, F32),
        pltpu.VMEM((4, 2) + tile, BF),
        pltpu.VMEM((4, 2) + tile, BF),
        pltpu.SemaphoreType.DMA((13,)),
        pltpu.SemaphoreType.DMA((12,)),
        pltpu.SemaphoreType.DMA((12,)),
        pltpu.SemaphoreType.REGULAR,
        pltpu.SemaphoreType.REGULAR,
    ]
    return pl.pallas_call(
        kernel,
        out_shape=pltpu.VMEM(vectors.shape, BF),
        in_specs=[pl.BlockSpec(memory_space=pl.ANY)] * 9,
        out_specs=pl.BlockSpec(memory_space=pltpu.VMEM),
        scratch_shapes=scratch,
        compiler_params=pltpu.CompilerParams(
            collective_id=0, has_side_effects=True, vmem_limit_bytes=62 * 1024 * 1024
        ),
    )(vectors, leaf_basis, local_transfer, upper_transfer, upper_coupling, leaf_coupling, far_list, near_list, near_tiles)


def solution(mesh):
    placed = (
        P("vec", "leaf"),
        P(None, "leaf"),
        P(None, "leaf"),
        P(),
        P(),
        P(None, "leaf"),
        P(None, "leaf"),
        P(None, "leaf"),
        P(("leaf", "vec"), None, None),
    )
    return jax.shard_map(
        shards, mesh=mesh, in_specs=placed, out_specs=P("vec", "leaf"), check_vma=False
    )
```

```python
import jax
import jax.numpy as jnp
from jax import lax
from jax.experimental import pallas as pl
from jax.experimental.pallas import tpu as pltpu
from jax.sharding import PartitionSpec as P

MESH = pl.DeviceIdType.MESH
BF = jnp.bfloat16
F32 = jnp.float32
ROW = 16
ROWS = 8
LEAF_COUNT = ROW * ROWS
BASES = (0, 16, 24, 28, 30)
PREV = 42
NEXT = 51


def low(shape):
    return lax.broadcasted_iota(jnp.int32, shape, 1) < 64


def halves(a, b):
    return jnp.where(low(a.shape), a, b)


def turned(tile):
    return pltpu.roll(tile, 64, 1)


def rounded(x):
    return x.astype(BF).astype(F32)


def hilo(x):
    hi = rounded(x)
    return halves(hi, x - hi).astype(BF)


def two_terms(x):
    hi = rounded(x)
    return hi.astype(BF), (x - hi).astype(BF)


def nn(a, b):
    return jnp.dot(a, b, preferred_element_type=F32)


def nt(a, b):
    return lax.dot_general(a, b, (((1,), (1,)), ((), ())), preferred_element_type=F32)


def tn(a, b):
    return lax.dot_general(a, b, (((0,), (0,)), ((), ())), preferred_element_type=F32)


def diagonal(block):
    none = jnp.zeros_like(block)
    return rows(halves(block, none), halves(none, block))


def rows(*parts):
    return jnp.concatenate(parts, axis=0)


def lanes(*parts):
    return jnp.concatenate(parts, axis=1)


def kernel(
    vec_h, basis_h, lt_h, ut_h, uc_h, lc_h, far_h, near_h, tiles_h, out_ref,
    basis_v, lt_v, ut_v, uc_v, lc_v, far_s, near_s, tiles_v,
    arrived, points, coeffs, root_tile, nodes, heads, tails,
    dup, path_hi, path_lo, r0_hi, r0_lo, to_points, lifted_couplings, from_top, from_row, far_out, near_out, near_in,
    in_sem, send_sem, recv_sem, flag_0, flag_1,
):
    d = lax.axis_index("leaf")
    x = lax.axis_index("vec")
    y = d >> 4
    i = d & 15
    z = i >> 1
    c = i & 1
    row_end = jnp.logical_and(c == 1, z == 7)
    row_start = jnp.logical_and(c == 0, z == 0)

    def load(src, dst, n):
        copy = pltpu.make_async_copy(src, dst, in_sem.at[n])
        copy.start()
        return copy

    own = pl.ds(pl.multiple_of(16 * x, 16), 16)
    vec_in = load(vec_h, arrived.at[1, own], 0)
    basis_in = load(basis_h, basis_v, 1)
    lt_in = load(lt_h, lt_v, 2)

    right = (d + 1) & (LEAF_COUNT - 1)
    left = (d + LEAF_COUNT - 1) & (LEAF_COUNT - 1)
    sibling = d + 1 - 2 * c
    column_peers = [(d + ROW * k) & (LEAF_COUNT - 1) for k in (4, 3, 5, 2, 1, 6, 7)]
    vec_peers = [(x + k) & 3 for k in (2, 1, 3)]

    barrier = pltpu.get_barrier_semaphore()

    def announce(leaf, vec):
        pl.semaphore_signal(barrier, inc=1, device_id={"leaf": leaf, "vec": vec}, device_id_type=MESH)

    announce(sibling, x)
    near_start = z < 4
    ends = jnp.where(jnp.logical_or(z == 0, z == 3), 1, 0)
    last = jnp.where(z == 7, 1, 0)
    count_0 = jnp.where(near_start, 15 - ends, 10 + 4 * last)
    count_1 = jnp.where(near_start, 23 + ends, 28 - last)

    def tell(flag):
        pl.semaphore_signal(flag, inc=1, device_id={"leaf": sibling, "vec": x}, device_id_type=MESH)

    @pl.when(jnp.logical_and(c == 0, z == 7))
    def _():
        pl.semaphore_wait(barrier, count_0)
        tell(flag_0)

    @pl.when(row_start)
    def _():
        for peer in vec_peers:
            announce((d + LEAF_COUNT - 2) & (LEAF_COUNT - 1), peer)

    @pl.when(z < 4)
    def _():
        for k in range(1, 8):
            announce(ROW * y + 2 * ((z + k) & 7), x)

    @pl.when(z >= 4)
    def _():
        for k in range(1, 8):
            announce(ROW * y + 2 * ((z + k) & 7) + 1, x)

    announce((d + jnp.where(c == 0, LEAF_COUNT - 2 + (z >> 2), jnp.where(z == 7, 2, 1))) & (LEAF_COUNT - 1), x)
    for peer in vec_peers:
        announce(d - c + (z >> 2), peer)
    for peer in column_peers:
        announce(peer - c + 1, x)

    ut_in = [
        load(ut_h.at[:, pl.ds(pl.multiple_of(1024 * y, 128), 1024)], ut_v.at[:, 0:1024], 3),
        load(ut_h.at[:, pl.ds(pl.multiple_of(8192 + 512 * y, 128), 512)], ut_v.at[:, 1024:1536], 4),
        load(ut_h.at[:, pl.ds(pl.multiple_of(12288 + 256 * y, 128), 256)], ut_v.at[:, 1536:1792], 5),
        load(ut_h.at[:, pl.ds(pl.multiple_of(14336 + 128 * y, 128), 128)], ut_v.at[:, 1792:1920], 6),
        load(ut_h.at[:, 15360:15872], ut_v.at[:, 1920:2432], 7),
    ]

    def send(src, dst, n_send, n_recv, leaf, vec):
        copy = pltpu.make_async_remote_copy(
            src_ref=src, dst_ref=dst, send_sem=send_sem.at[n_send], recv_sem=recv_sem.at[n_recv],
            device_id={"leaf": leaf, "vec": vec}, device_id_type=MESH,
        )
        copy.start()
        return copy

    def wait_for(ref, sem):
        pltpu.make_async_copy(ref, ref, sem).wait()

    def send_root(t):
        send(root_tile, nodes.at[i], 1, 1, ROW * y + t, x)

    def to_vec_peers():
        for peer in vec_peers:
            send(vec_h, arrived.at[1, own], 0, 0, d, peer)

    def far_right():
        send(coeffs.at[8:16, 0], coeffs.at[0:8, 0], 2, 2, right, x)

    def far_left():
        send(coeffs.at[8:16, 0], coeffs.at[16:24, 0], 3, 3, left, x)

    def near_right():
        send(arrived.at[1], arrived.at[0], 4, 4, right, x)

    def near_left():
        send(arrived.at[1], arrived.at[2], 5, 5, left, x)

    left_now = jnp.logical_and(near_start, jnp.logical_or(c == 1, z > 0))
    right_now = jnp.logical_and(near_start, jnp.logical_or(c == 0, z < 3))
    left_later = jnp.logical_not(jnp.logical_or(left_now, row_start))
    right_later = jnp.logical_not(jnp.logical_or(right_now, row_end))

    vec_in.wait()
    basis_in.wait()

    group = lax.broadcasted_iota(jnp.int32, (16, 256), 1) >> 6
    zero = jnp.zeros((16, 256), BF)

    def paired(product):
        return [
            halves(product[0:16, 0:128], product[16:32, 0:128]),
            halves(product[32:48, 128:256], product[48:64, 128:256]),
        ]

    leaves = []
    for q in range(4):
        tile = arrived[1, own, 256 * q : 256 * q + 256]
        block = basis_v[:, 256 * q : 256 * q + 256]
        spread = rows(*[jnp.where(group == e, tile, zero) for e in range(4)])
        leaves.append(nt(spread, rows(block, block)))
    for j in range(8):
        pair = leaves[j // 2][32 * (j % 2) : 32 * (j % 2) + 32]
        coeffs[8 + j, 0] = halves(pair[0:16], pair[16:32]).astype(BF)
        coeffs[8 + j, 1] = halves(pair[16:32], pair[0:16]).astype(BF)

    @pl.when(row_end)
    def _():
        pl.semaphore_wait(flag_0, 1)
        for peer in [x] + vec_peers:
            send(vec_h, arrived.at[0, own], 10, 4, right, peer)
        far_right()

    lt_in.wait()

    def local_top():
        transfer = lt_v[:, 1792:1920]
        crossed = turned(transfer)
        return halves(transfer, crossed), halves(crossed, transfer)

    top = local_top()

    current = []
    for q in range(4):
        transfer = lt_v[:, 256 * q : 256 * q + 256]
        current += paired(nn(hilo(leaves[q]), rows(transfer, transfer)))
    for start in (1024, 1536):
        following = []
        for q in range(len(current) // 4):
            hi, lo = two_terms(rows(*current[4 * q : 4 * q + 4]))
            transfer = lt_v[:, start + 256 * q : start + 256 * q + 256]
            following += paired(nn(lanes(hi, lo), rows(transfer, transfer, transfer, transfer)))
        current = following
    first_hi, first_lo = two_terms(current[0])
    second_hi, second_lo = two_terms(current[1])
    root = nn(lanes(first_hi, first_lo, second_hi, second_lo), rows(*([top[0]] * 4 + [top[1]] * 4)))
    root_tile[...] = hilo(root)
    nodes[i] = root_tile[...]

    late_loads = [
        pltpu.make_async_copy(src, dst, in_sem.at[8 + n])
        for n, (src, dst) in enumerate(
            ((uc_h, uc_v), (lc_h, lc_v), (far_h, far_s), (near_h, near_s), (tiles_h, tiles_v))
        )
    ]
    uc_in, lc_in, far_in_s, near_in_s, tiles_in = late_loads

    def roots_out():
        @pl.when(jnp.logical_and(c == 0, z < 7))
        def _():
            pl.semaphore_wait(barrier, count_0)
            tell(flag_0)

        @pl.when(jnp.logical_and(c == 1, z < 7))
        def _():
            pl.semaphore_wait(flag_0, 1)

        for k in range(1, 8):
            send_root((i + k) & 7)

        @pl.when(z >= 4)
        def _():
            send_root(i & 7)

        @pl.when(near_start)
        def _():
            to_vec_peers()

        @pl.when(left_now)
        def _():
            far_left()

        @pl.when(right_now)
        def _():
            far_right()

        for copy in late_loads:
            copy.start()

    def matrices():
        for copy in ut_in:
            copy.wait()
        for p in range(19):
            pair = ut_v[:, 128 * p : 128 * p + 128]
            swapped = turned(pair)
            dup[2 * p] = halves(pair, swapped)
            dup[2 * p + 1] = halves(swapped, pair)

        path = dup[i]
        path_hi[0] = path
        path = path.astype(F32)
        below = local_top()
        below = [(below[0], None), (below[1], None)]
        row_below = [(dup[28], None), (dup[29], None)]

        def path_step(path, u):
            matrix = dup[BASES[u] + (i >> u if u < 4 else y)]
            path = nn(hilo(path), rows(matrix, matrix))
            path_hi[u], path_lo[u] = two_terms(path)
            return path

        def product_step(below, transfers, start):
            following = []
            for m, (hi, lo) in enumerate(below):
                left_side = diagonal(transfers[:, start + 128 * m : start + 128 * m + 128])
                if lo is None:
                    product = nn(left_side, rows(hi, hi))
                else:
                    product = nn(lanes(left_side, left_side), rows(hi, hi, lo, lo))
                hi, lo = two_terms(product)
                following += [(hi[0:64], lo[0:64]), (hi[64:128], lo[64:128])]
            return following

        for u, start in ((1, 1536), (2, 1024), (3, 0)):
            path = path_step(path, u)
            below = product_step(below, lt_v, start)
            row_below = product_step(row_below, ut_v, start)
        path_step(path, 4)
        for m in range(8):
            r0_hi[m] = rows(below[2 * m][0], below[2 * m + 1][0])
            r0_lo[m] = rows(below[2 * m][1], below[2 * m + 1][1])
        for m, (hi, lo) in enumerate(row_below):
            from_row[0, m] = rows(hi, hi)
            from_row[1, m] = rows(lo, lo)

    def turn(n, carry):
        @pl.when(n == (z >> 2))
        def _():
            matrices()

        @pl.when(n == 0)
        def _():
            roots_out()

        return carry

    lax.fori_loop(0, 2, turn, 0)

    def fold(j, carry):
        at = pl.ds(pl.multiple_of(128 * j, 128), 128)
        block = diagonal(basis_v[:, at])
        hi, lo = two_terms(tn(r0_hi[j], block) + tn(r0_lo[j], block))
        to_points[0:128, at] = hi
        to_points[128:256, at] = lo
        return carry

    lax.fori_loop(0, 8, fold, 0, unroll=2)

    @pl.when(near_start)
    def _():
        wait_for(arrived.at[1, 0:48], recv_sem.at[0])

    @pl.when(left_now)
    def _():
        near_left()

    @pl.when(right_now)
    def _():
        near_right()

    uc_in.wait()
    couplings = rows(uc_v[...], uc_v[...])
    for e in range(2):
        value = nn(halves(path_hi[3 + e], path_lo[3 + e]), couplings)
        value = jnp.transpose(rows(value, value))
        for o in range(4):
            lifted_couplings[e, o] = value[64 * o : 64 * o + 64]

    def slot(offset, odd):
        index = jnp.where(offset == -3, 0, jnp.where(offset == -2, 1, jnp.where(offset == 2, 2, 3)))
        wide = jnp.logical_or(
            jnp.logical_and(offset == -3, odd == 1), jnp.logical_and(offset == 3, odd == 0)
        )
        valid = jnp.logical_or(jnp.logical_or(offset == -2, offset == 2), wide)
        return index, jnp.where(valid, 1.0, 0.0).astype(F32)

    def gather_top(n, carry):
        index, keep = slot(n - y, y & 1)
        value = lifted_couplings[0, index] * keep
        index, keep = slot((n >> 1) - (y >> 1), (y >> 1) & 1)
        hi, lo = two_terms(lifted_couplings[1, index] * keep)
        hi, lo = two_terms(value + nn(dup[30 + n], rows(hi, lo)))
        from_top[0, n] = rows(hi, hi)
        from_top[1, n] = rows(lo, lo)
        return carry

    lax.fori_loop(0, 8, gather_top, 0, unroll=4)

    def fill(w):
        def step(j, carry):
            block = arrived[w, :, pl.ds(pl.multiple_of(128 * j, 128), 128)]
            points[8 * w + j, 0] = block
            points[8 * w + j, 1] = turned(block)
            return carry

        lax.fori_loop(0, 8, step, 0, unroll=4)

    @pl.when(c == 1)
    def _():
        pl.semaphore_wait(barrier, count_1)
        tell(flag_1)

    @pl.when(c == 0)
    def _():
        pl.semaphore_wait(flag_1, 1)

    for k in range(1, 8):
        send_root(8 + ((i + k) & 7))

    @pl.when(z < 4)
    def _():
        send_root(8 + i)

    @pl.when(z >= 4)
    def _():
        to_vec_peers()

    @pl.when(jnp.logical_not(left_now))
    def _():
        far_left()

    @pl.when(right_later)
    def _():
        far_right()

    @pl.when(z >= 4)
    def _():
        wait_for(arrived.at[1, 0:48], recv_sem.at[0])

    @pl.when(row_start)
    def _():
        send(vec_h, arrived.at[2, own], 11, 5, left, x)

    @pl.when(left_later)
    def _():
        near_left()

    @pl.when(right_later)
    def _():
        near_right()

    fill(1)

    first_leaf = ROW * d - ROW

    def chosen(table, lists, slots, column):
        parts = []
        for s in range(0, slots, 2):
            a = jnp.clip(lists[s, column] - first_leaf, 0, 3 * ROW - 1)
            b = jnp.clip(lists[s + 1, column] - first_leaf, 0, 3 * ROW - 1)
            parts.append(halves(table[a >> 1, a & 1], table[b >> 1, 1 - (b & 1)]))
        return lanes(*parts)

    def far_part():
        far_in_s.wait()
        lc_in.wait()
        wait_for(coeffs.at[0:8, 0], recv_sem.at[2])
        wait_for(coeffs.at[16:24, 0], recv_sem.at[3])
        for p in list(range(8)) + list(range(16, 24)):
            coeffs[p, 1] = turned(coeffs[p, 0])
        for j in range(8):
            source = rows(*[chosen(coeffs, far_s, 6, 2 * j + e) for e in range(2)])
            value = nt(source, rows(lc_v[:, 768 * j : 768 * j + 384], lc_v[:, 768 * j + 384 : 768 * j + 768]))
            hi, lo = two_terms(halves(value[0:16], value[16:32]))
            block = diagonal(basis_v[:, 128 * j : 128 * j + 128])
            far_out[j] = nn(lanes(hi, lo), rows(block, block))

    def near_part():
        near_in_s.wait()
        tiles_in.wait()
        wait_for(arrived.at[0], recv_sem.at[4])

        @pl.when(row_end)
        def _():
            wait_for(arrived.at[2, 0:48], recv_sem.at[11])

        @pl.when(jnp.logical_not(row_end))
        def _():
            wait_for(arrived.at[2], recv_sem.at[5])

        fill(0)
        fill(2)
        for q in range(2):
            source = rows(*[chosen(points, near_s, 6, 4 * x + 2 * q + e) for e in range(2)])
            value = nt(source, rows(tiles_v[2 * q], tiles_v[2 * q + 1]))
            value = halves(value[0:64], value[64:128]).astype(BF)
            for v in range(4):
                near_out[v, q] = value[16 * v : 16 * v + 16]
        for n, peer in enumerate(vec_peers):
            send(near_out.at[peer], near_in.at[x], 9, 9, d, peer)
        near_in[x] = near_out[x]

    def row_tree():
        wait_for(nodes.at[0:15], recv_sem.at[1])

        @pl.when(row_end)
        def _():
            wait_for(arrived.at[2, 0:16], recv_sem.at[5])
            for peer in vec_peers:
                send(arrived.at[2, own], arrived.at[2, own], 11, 11, d, peer)

        roots = lanes(*[nodes[m] for m in range(ROW)])
        top_tile = hilo(nn(roots, from_row[0].reshape(2048, 128)) + nn(roots, from_row[1].reshape(2048, 128)))
        nodes[30 + y] = top_tile
        heads[8] = top_tile
        tails[8] = top_tile
        for peer in column_peers[:4] + column_peers[5:6]:
            send(nodes.at[30 + y], nodes.at[30 + y], 8, 8, peer, x)
        for u in range(3):
            base, count = BASES[u], ROW >> u
            for m in range(count // 2):
                left_m, right_m = dup[base + 2 * m], dup[base + 2 * m + 1]
                value = nn(lanes(nodes[base + 2 * m], nodes[base + 2 * m + 1]), rows(left_m, left_m, right_m, right_m))
                nodes[BASES[u + 1] + m] = hilo(value)
        for u in range(4):
            for e in range(2):
                heads[2 * u + e] = nodes[BASES[u] + e]
                tails[2 * u + e] = nodes[BASES[u + 1] - 2 + e]
        send(tails, nodes.at[PREV : PREV + 9], 6, 6, column_peers[4], x)
        send(heads, nodes.at[NEXT : NEXT + 9], 7, 7, column_peers[6], x)

    row_tree()
    near_part()
    far_part()

    weights = []
    for o in range(2):
        pair = uc_v[:, 128 * o : 128 * o + 128]
        swapped = turned(pair)
        weights += [halves(pair, swapped), halves(swapped, pair)]
    weights = lanes(*weights)
    wait_for(nodes.at[0:9], recv_sem.at[6])
    wait_for(nodes.at[0:9], recv_sem.at[7])
    sources = []
    for u in range(4):
        g = d >> u
        odd = g & 1
        number = LEAF_COUNT >> u
        count = ROW >> u
        parts = []
        for o, wanted in ((-3, odd == 1), (-2, None), (2, None), (3, odd == 0)):
            shift = o if wanted is None else (-3 * odd if o < 0 else 3 * (1 - odd))
            place = (i >> u) + shift
            place = jnp.where(
                place < 0,
                PREV + 2 + 2 * u + place,
                jnp.where(place < count, BASES[u] + place, NEXT + 2 * u - count + place),
            )
            valid = (g + o >= 0) if o < 0 else (g + o < number)
            if wanted is not None:
                valid = jnp.logical_and(valid, wanted)
            keep = jnp.where(valid, 1.0, 0.0).astype(F32)
            parts.append((nodes[place].astype(F32) * keep).astype(BF))
        sources.append(lanes(*parts))
    coupled = nt(rows(*sources), rows(weights, weights))
    left_side, right_side = [], []
    for u in range(1, 4):
        tile = hilo(coupled[16 * u : 16 * u + 16])
        left_side.append(tile)
        right_side.append(path_hi[u - 1])
        if u > 1:
            left_side.append(tile)
            right_side.append(path_lo[u - 1])
    matrix = lanes(*right_side)
    down = coupled[0:16] + nt(lanes(*left_side), rows(matrix, matrix))

    nodes[30 + ((y + 7) & 7)] = nodes[PREV + 8]
    nodes[30 + ((y + 1) & 7)] = nodes[NEXT + 8]
    wait_for(nodes.at[0:5], recv_sem.at[8])
    tops = lanes(*[nodes[30 + n] for n in range(8)])
    down = down + nn(tops, from_top[0].reshape(1024, 128)) + nn(tops, from_top[1].reshape(1024, 128))
    down = hilo(down)
    value = nn(lanes(down, down), to_points[...])
    wait_for(near_in.at[0:3], recv_sem.at[9])
    for j in range(8):
        at = slice(128 * j, 128 * j + 128)
        out_ref[:, at] = (value[:, at] + far_out[j] + near_in[j // 2, j % 2].astype(F32)).astype(BF)

    wait_for(arrived.at[1, 0:48], send_sem.at[0])
    wait_for(nodes.at[0:15], send_sem.at[1])
    wait_for(coeffs.at[0:8, 0], send_sem.at[2])
    wait_for(coeffs.at[0:8, 0], send_sem.at[3])

    @pl.when(row_end)
    def _():
        wait_for(arrived.at[0], send_sem.at[10])
        wait_for(arrived.at[2, 0:48], send_sem.at[11])

    @pl.when(row_start)
    def _():
        wait_for(arrived.at[2, 0:16], send_sem.at[11])

    @pl.when(jnp.logical_not(row_end))
    def _():
        wait_for(arrived.at[0], send_sem.at[4])

    @pl.when(jnp.logical_not(row_start))
    def _():
        wait_for(arrived.at[2], send_sem.at[5])

    wait_for(nodes.at[0:9], send_sem.at[6])
    wait_for(nodes.at[0:9], send_sem.at[7])
    wait_for(nodes.at[0:5], send_sem.at[8])
    wait_for(near_out.at[0:3], send_sem.at[9])


def shards(vectors, leaf_basis, local_transfer, upper_transfer, upper_coupling, leaf_coupling, far_list, near_list, near_tiles):
    tile = (16, 128)
    scratch = [
        pltpu.VMEM(leaf_basis.shape, BF),
        pltpu.VMEM(local_transfer.shape, BF),
        pltpu.VMEM((64, 2432), BF),
        pltpu.VMEM(upper_coupling.shape, BF),
        pltpu.VMEM(leaf_coupling.shape, BF),
        pltpu.SMEM(far_list.shape, jnp.int32),
        pltpu.SMEM(near_list.shape, jnp.int32),
        pltpu.VMEM(near_tiles.shape, BF),
        pltpu.VMEM((3, 64, 1024), BF),
        pltpu.VMEM((24, 2, 64, 128), BF),
        pltpu.VMEM((24, 2) + tile, BF),
        pltpu.VMEM(tile, BF),
        pltpu.VMEM((60,) + tile, BF),
        pltpu.VMEM((9,) + tile, BF),
        pltpu.VMEM((9,) + tile, BF),
        pltpu.VMEM((38, 64, 128), BF),
        pltpu.VMEM((5, 64, 128), BF),
        pltpu.VMEM((5, 64, 128), BF),
        pltpu.VMEM((8, 128, 128), BF),
        pltpu.VMEM((8, 128, 128), BF),
        pltpu.VMEM((256, 1024), BF),
        pltpu.VMEM((2, 4, 64, 128), F32),
        pltpu.VMEM((2, 8, 128, 128), BF),
        pltpu.VMEM((2, ROW, 128, 128), BF),
        pltpu.VMEM((8,) + tile, F32),
        pltpu.VMEM((4, 2) + tile, BF),
        pltpu.VMEM((4, 2) + tile, BF),
        pltpu.SemaphoreType.DMA((13,)),
        pltpu.SemaphoreType.DMA((12,)),
        pltpu.SemaphoreType.DMA((12,)),
        pltpu.SemaphoreType.REGULAR,
        pltpu.SemaphoreType.REGULAR,
    ]
    return pl.pallas_call(
        kernel,
        out_shape=pltpu.VMEM(vectors.shape, BF),
        in_specs=[pl.BlockSpec(memory_space=pl.ANY)] * 9,
        out_specs=pl.BlockSpec(memory_space=pltpu.VMEM),
        scratch_shapes=scratch,
        compiler_params=pltpu.CompilerParams(
            collective_id=0, has_side_effects=True, vmem_limit_bytes=62 * 1024 * 1024
        ),
    )(vectors, leaf_basis, local_transfer, upper_transfer, upper_coupling, leaf_coupling, far_list, near_list, near_tiles)


def solution(mesh):
    placed = (
        P("vec", "leaf"),
        P(None, "leaf"),
        P(None, "leaf"),
        P(),
        P(),
        P(None, "leaf"),
        P(None, "leaf"),
        P(None, "leaf"),
        P(("leaf", "vec"), None, None),
    )
    return jax.shard_map(
        shards, mesh=mesh, in_specs=placed, out_specs=P("vec", "leaf"), check_vma=False
    )
```
